32 devices in a mesh: fsdp: 2 (over y), seq: 16 (over z, x, core).
Axes of the slice: x: 2, y: 2, z: 4, core: 2. Of those that a mesh axis runs over, the one named last changes fastest.
Arguments:
- tokens: bfloat16 [4, 1024, 1024], P('fsdp', 'seq'), may hold values from -6 to 6
- cotangent: bfloat16 [4, 1024, 1024], P('fsdp', 'seq'), may hold values from -6 to 6
- lengths: int32 [4], P('fsdp'), may hold values from 256 to 1024, as said below
- adapter_ids: int32 [4], P('fsdp'), may hold values from 0 to 7
- attn_weight: bfloat16 [1024, 4, 1024], P(('fsdp', 'seq')), may hold values from -2.25 to 2.25
- fc1_weight: bfloat16 [1024, 4096], P(('fsdp', 'seq')), may hold values from -0.1875 to 0.1875
- fc2_weight: bfloat16 [4096, 1024], P(('fsdp', 'seq')), may hold values from -0.09375 to 0.09375
- vectors: bfloat16 [1024, 8], P(('fsdp', 'seq')), may hold values from -0.6 to 1.4
- fc1_bias: bfloat16 [4096], P(('fsdp', 'seq')), may hold values from -1.1953125 to 1.1953125
- adapter_down: bfloat16 [1024, 8, 5, 16], P(('fsdp', 'seq')), may hold values from -0.1875 to 0.1875
- adapter_up: bfloat16 [1024, 8, 5, 16], P(('fsdp', 'seq')), may hold values from -0.75 to 0.75
- ff_adapters: bfloat16 [4096, 8, 2, 16], P(('fsdp', 'seq')), may hold values from -0.375 to 0.375
Outputs:
- layer_out: bfloat16 [4, 1024, 1024], P('fsdp', 'seq')
- input_grad: bfloat16 [4, 1024, 1024], P('fsdp', 'seq')
- down_grad: float32 [1024, 8, 5, 16], P(('fsdp', 'seq'))
- up_grad: float32 [1024, 8, 5, 16], P(('fsdp', 'seq'))
- ff_grad: float32 [4096, 8, 2, 16], P(('fsdp', 'seq'))
The draws below stay inside these ranges and needn't reach their ends.
Inputs may be any that keep to these rules, and one draw needn't show every extreme that they name: `lengths`: in each aligned block of 2 slots one length is 1024.
All inputs are finite; a program needn't handle non-finite values.
Results may differ from the reference program's by a relative error of at most 0.019.
Values may be sent and summed in bfloat16 or wider, within the bound.
A program may use at most 320 MiB of HBM per device.

```python
import math
import jax
import jax.numpy as jnp
from jax import lax

D = 1024
HEADS = 16
HEAD = 64
FF = 4096
RANK = 16
ADAPTERS = 8
SEQS_DEV = 2
SLOTS = 4
SLOT = 1024


def draw_lengths(key, part):
    key = jax.random.fold_in(key, 11)
    key_base, key_pick = jax.random.split(key)
    groups = SLOTS // SEQS_DEV
    drawn = jax.random.randint(key_base, (groups, SEQS_DEV), SLOT // 4, SLOT + 1)
    chosen = jax.random.randint(key_pick, (groups, 1), 0, SEQS_DEV)
    is_full = jnp.arange(SEQS_DEV)[None, :] == chosen
    return jnp.where(is_full, SLOT, drawn).reshape(SLOTS).astype(jnp.int32)


def draw_attn_weight(key, part):
    key = jax.random.fold_in(key, 12)
    drawn = jax.random.truncated_normal(key, -3.0, 3.0, (D, 4, D), jnp.float32)
    factor = jnp.where(jnp.arange(4) == 3, 24.0, 1.0)[None, :, None]
    return (drawn * factor * D ** (-0.5)).astype(jnp.bfloat16)


def draw_vectors(key, part):
    key = jax.random.fold_in(key, 13)
    key_gain, key_shift = jax.random.split(key)
    gains = jax.random.uniform(key_gain, (D, 8), jnp.float32, 0.6, 1.4)
    shifts = 0.2 * jax.random.truncated_normal(key_shift, -3.0, 3.0, (D, 8), jnp.float32)
    is_gain = (jnp.arange(8) == 4) | (jnp.arange(8) == 6)
    return jnp.where(is_gain[None, :], gains, shifts).astype(jnp.bfloat16)


def draw_ff_adapters(key, part):
    key = jax.random.fold_in(key, 14)
    drawn = jax.random.truncated_normal(key, -3.0, 3.0, (FF, ADAPTERS, 2, RANK), jnp.float32)
    factor = jnp.where(jnp.arange(2) == 0, (4 * RANK) ** (-0.5), FF ** (-0.5))[None, None, :, None]
    return (drawn * factor).astype(jnp.bfloat16)


def place_ends(values, key, smallest, top_value):
    place = [jax.random.randint(jax.random.fold_in(key, axis), (), 0, length) for axis, length in enumerate(values.shape)]
    longest = values.shape.index(max(values.shape))
    beside = place[:longest] + [(place[longest] + 1) % values.shape[longest]] + place[longest + 1:]
    return values.at[tuple(place)].set(smallest).at[tuple(beside)].set(top_value)


def levels(key, extent, shards, smallest, top_value):
    level = 1.0
    for position, parts in shards:
        steps = jax.random.uniform(jax.random.fold_in(jax.random.fold_in(key, 6), position), (parts,), jnp.float32, smallest / len(shards), top_value / len(shards))
        level = level * jnp.repeat(jnp.exp(steps), extent[position] // parts).reshape((-1,) + (1,) * (len(extent) - 1 - position))
    return level


def gaussian(stream_key, extent, width, reach, shards=(), held_as=jnp.bfloat16):
    level = levels(stream_key, extent, shards, -0.22, 0.18) if shards else 1.0
    result = jax.random.normal(stream_key, extent, jnp.float32) * width * level
    return jnp.minimum(jnp.maximum(result, -reach), reach).astype(held_as)


def setup_inputs(seed: int = 0) -> dict:
    arg_keys = jax.random.split(jax.random.key(seed), 13)
    return {
        "tokens": gaussian(arg_keys[0], (SLOTS, SLOT, D), 1.0, 6.0, ((0, 2), (1, 16))),
        "cotangent": gaussian(arg_keys[1], (SLOTS, SLOT, D), 1.0, 6.0, ((0, 2), (1, 16))),
        "lengths": draw_lengths(jax.random.fold_in(arg_keys[12], 71), 0),
        "adapter_ids": place_ends(jax.random.randint(arg_keys[3], (SLOTS,), 0, ADAPTERS), jax.random.fold_in(arg_keys[3], 1), 0, ADAPTERS - 1).astype(jnp.int32),
        "attn_weight": draw_attn_weight(jax.random.fold_in(arg_keys[12], 71), 0),
        "fc1_weight": gaussian(arg_keys[5], (D, FF), D ** -0.5, 0.1875, ((0, 32),)),
        "fc2_weight": gaussian(arg_keys[6], (FF, D), FF ** -0.5, 0.09375, ((0, 32),)),
        "vectors": draw_vectors(jax.random.fold_in(arg_keys[12], 71), 0),
        "fc1_bias": gaussian(arg_keys[8], (FF,), 0.3, 1.1953125, ((0, 32),)),
        "adapter_down": gaussian(arg_keys[9], (D, ADAPTERS, 5, RANK), D ** -0.5, 0.1875, ((0, 32),)),
        "adapter_up": gaussian(arg_keys[10], (D, ADAPTERS, 5, RANK), (4 * RANK) ** -0.5, 0.75, ((0, 32),)),
        "ff_adapters": draw_ff_adapters(jax.random.fold_in(arg_keys[12], 71), 0),
    }


@jax.custom_vjp
def low(v):
    return lax.optimization_barrier(v.astype(jnp.bfloat16)).astype(jnp.float32)

@jax.custom_vjp
def low_back(v):
    return v

def low_keep(v):
    return (low(v), None)

def low_pass(kept, grad):
    return (grad,)

def back_keep(v):
    return (v, None)

def back_low(kept, grad):
    return (low(grad),)
low.defvjp(low_keep, low_pass)
low_back.defvjp(back_keep, back_low)

def matmul_hi(left, right):
    return jnp.dot(left, right, precision=lax.Precision.HIGHEST)

def layer_norm(value, gain, shift):
    centered = value - lax.optimization_barrier(jnp.mean(value, axis=-1, keepdims=True))
    scaled = centered * lax.rsqrt(lax.optimization_barrier(jnp.mean(centered * centered, axis=-1, keepdims=True)) + 1e-05)
    return scaled * gain + shift

def adapted(inputs, weight, down_table, up_table):
    inner_low = low(low_back(matmul_hi(inputs, down_table)))
    return matmul_hi(inputs, weight) + matmul_hi(inner_low, up_table.T)

def slot_layer(inputs, length, adapter, frozen, trainable):
    attn_all, fc1_all, fc2_all, vector_all, bias_ff = frozen
    down_all, up_all, ff_all = trainable
    down_pick = lax.dynamic_index_in_dim(down_all, adapter, 1, keepdims=False)
    up_pick = lax.dynamic_index_in_dim(up_all, adapter, 1, keepdims=False)
    ff_pick = lax.dynamic_index_in_dim(ff_all, adapter, 1, keepdims=False)
    seq_span = inputs.shape[0]
    positions = jnp.arange(seq_span)
    live_rows = (positions < length).astype(jnp.float32)[:, None]
    valid_keys = positions < length
    inputs_low = low(inputs)
    query = low_back(low(0.125 * (adapted(inputs_low, attn_all[:, 0, :], down_pick[:, 0, :], up_pick[:, 0, :]) + vector_all[:, 0])))
    keys = low_back(low(adapted(inputs_low, attn_all[:, 1, :], down_pick[:, 1, :], up_pick[:, 1, :])))
    values = low_back(low(adapted(inputs_low, attn_all[:, 2, :], down_pick[:, 2, :], up_pick[:, 2, :]) + vector_all[:, 1]))
    key_heads = keys.reshape(seq_span, HEADS, HEAD)
    value_heads = values.reshape(seq_span, HEADS, HEAD)
    block_rows = math.gcd(seq_span, 512)

    def attend_block(query_block):
        query_heads = query_block.reshape(block_rows, HEADS, HEAD)
        scores = jnp.einsum('qhd,khd->hqk', query_heads, key_heads, precision=lax.Precision.HIGHEST)
        scores = low_back(jnp.where(valid_keys[None, None, :], scores, -1e+30))
        shifted = jnp.exp(scores - lax.optimization_barrier(jnp.max(scores, axis=-1, keepdims=True)))
        probs = shifted / lax.optimization_barrier(jnp.sum(shifted, axis=-1, keepdims=True))
        mixed_heads = jnp.einsum('hqk,khd->qhd', low(probs), value_heads, precision=lax.Precision.HIGHEST)
        return mixed_heads.reshape(block_rows, HEADS * HEAD)
    mixed = lax.map(jax.checkpoint(attend_block), query.reshape(seq_span // block_rows, block_rows, HEADS * HEAD))
    mixed = low_back(low(mixed.reshape(seq_span, HEADS * HEAD)))
    branch = low_back(adapted(mixed, attn_all[:, 3, :], down_pick[:, 3, :], up_pick[:, 3, :]) + vector_all[:, 2])
    first_sum = inputs + branch
    normed = layer_norm(first_sum, vector_all[:, 4], vector_all[:, 5])
    normed_low = low(normed)
    hidden = low_back(adapted(normed_low, fc1_all, down_pick[:, 4, :], ff_pick[:, 0, :]) + bias_ff)
    activated = low(jax.nn.gelu(hidden, approximate=False))
    branch_two = low_back(adapted(activated, fc2_all, ff_pick[:, 1, :], up_pick[:, 4, :]) + vector_all[:, 3])
    second = normed + branch_two
    return layer_norm(second, vector_all[:, 6], vector_all[:, 7]) * live_rows

def reference(tokens, cotangent, lengths, adapter_ids, attn_weight, fc1_weight, fc2_weight, vectors, fc1_bias, adapter_down, adapter_up, ff_adapters):
    frozen = (attn_weight.astype(jnp.float32), fc1_weight.astype(jnp.float32), fc2_weight.astype(jnp.float32), vectors.astype(jnp.float32), fc1_bias.astype(jnp.float32))
    trainable = (adapter_down.astype(jnp.float32), adapter_up.astype(jnp.float32), ff_adapters.astype(jnp.float32))
    inputs_all = tokens.astype(jnp.float32)

    def forward(inputs_all, trainable):

        def slot_step(running, slot_item):
            inputs, length, adapter = slot_item
            return (running, slot_layer(inputs, length, adapter, frozen, trainable))
        _, results = lax.scan(jax.checkpoint(slot_step), jnp.zeros((), jnp.float32), (inputs_all, lengths, adapter_ids))
        return results
    results, pullback = jax.vjp(forward, inputs_all, trainable)
    grad_inputs, grads = pullback(cotangent.astype(jnp.float32))
    layer_out = results.astype(jnp.bfloat16)
    input_grad = grad_inputs.astype(jnp.bfloat16)
    return (layer_out, input_grad, grads[0], grads[1], grads[2])
```

```python
from functools import partial
import math

import jax
import jax.numpy as jnp
from jax import lax
from jax.experimental import pallas as pl
from jax.experimental.pallas import tpu as pltpu
from jax.sharding import PartitionSpec as P

HEADS = 16
HEAD = 64
ADAPTERS = 8


NEG_FILL = -1e30
NORM_EPS = 1e-05


def split_heads(values_in):
    return values_in.reshape(values_in.shape[:-1] + (HEADS, HEAD))


def norm_rows(value, gain, shift):
    centered = value - jnp.mean(value, axis=-1, keepdims=True)
    scaled = centered * lax.rsqrt(jnp.mean(centered * centered, axis=-1, keepdims=True) + NORM_EPS)
    return scaled * gain + shift


def gelu_exact(value):
    return jax.nn.gelu(value, approximate=False)


def choose(onehot, table):
    return jnp.einsum("si,dikr->sdkr", onehot, table, preferred_element_type=jnp.float32).astype(
        jnp.bfloat16
    )


def unpack(gathered, onehot):
    attn_all, fc1_all, fc2_all, vector_all, bias_ff, down_all, up_all, ff_all = gathered
    return (
        attn_all,
        fc1_all,
        fc2_all,
        vector_all.astype(jnp.float32),
        bias_ff.astype(jnp.float32),
        choose(onehot, down_all),
        choose(onehot, up_all),
        choose(onehot, ff_all),
    )


def project(inputs, weight, down_table, up_table):
    frozen_part = jnp.einsum("spd,de->spe", inputs, weight, preferred_element_type=jnp.float32)
    inner_low = jnp.einsum(
        "spd,sdr->spr", inputs, down_table, preferred_element_type=jnp.float32
    ).astype(jnp.bfloat16)
    return (
        frozen_part
        + jnp.einsum("spr,ser->spe", inner_low, up_table, preferred_element_type=jnp.float32),
        inner_low,
    )


def project_back(inputs, inner_low, grad_out, weight, down_table, up_table):
    grad_inner = jnp.einsum(
        "spe,ser->spr", grad_out, up_table, preferred_element_type=jnp.float32
    ).astype(jnp.bfloat16)
    grad_in = jnp.einsum("spe,de->spd", grad_out, weight, preferred_element_type=jnp.float32)
    grad_in = grad_in + jnp.einsum(
        "spr,sdr->spd", grad_inner, down_table, preferred_element_type=jnp.float32
    )
    grad_up = jnp.einsum("spe,spr->ser", grad_out, inner_low, preferred_element_type=jnp.float32)
    grad_down = jnp.einsum("spd,spr->sdr", inputs, grad_inner, preferred_element_type=jnp.float32)
    return (grad_in, grad_down, grad_up)


def block_scores(query_heads, key_block, key_start, lengths):
    block_rows = key_block.shape[1]
    scores = jnp.einsum(
        "sqhd,skhd->shqk", query_heads, split_heads(key_block), preferred_element_type=jnp.float32
    )
    valid_keys = (key_start + jnp.arange(block_rows))[None, :] < lengths[:, None]
    return jnp.where(valid_keys[:, None, None, :], scores, NEG_FILL)


def score_grads(scores, logsum, row_delta, grad_heads, value_heads):
    probs = jnp.exp(scores - logsum[..., None])
    grad_probs = jnp.einsum(
        "sqhd,skhd->shqk", grad_heads, value_heads, preferred_element_type=jnp.float32
    )
    grad_scores = (probs * (grad_probs - row_delta[..., None])).astype(jnp.bfloat16)
    return (grad_scores, probs.astype(jnp.bfloat16))


def attend(query, all_keys, all_values, lengths):
    seq_span = all_keys.shape[1]
    block_rows = math.gcd(seq_span, 512)
    blocks = seq_span // block_rows
    query_heads = split_heads(query)
    slot_count, query_rows = (query.shape[0], query.shape[1])
    stats_shape = (slot_count, HEADS, query_rows)

    def stats_step(running, step_index):
        row_top, row_total = running
        offset = step_index * block_rows
        scores = block_scores(
            query_heads, lax.dynamic_slice_in_dim(all_keys, offset, block_rows, 1), offset, lengths
        )
        new_top = jnp.maximum(row_top, jnp.max(scores, axis=-1))
        row_total = row_total * jnp.exp(row_top - new_top) + jnp.sum(
            jnp.exp(scores - new_top[..., None]), axis=-1
        )
        return ((new_top, row_total), None)

    start_top = jnp.full(stats_shape, NEG_FILL, jnp.float32)
    (row_top, row_total), _ = lax.scan(
        stats_step, (start_top, jnp.zeros(stats_shape, jnp.float32)), jnp.arange(blocks)
    )
    logsum = row_top + jnp.log(row_total)

    def mix_step(running, step_index):
        offset = step_index * block_rows
        scores = block_scores(
            query_heads, lax.dynamic_slice_in_dim(all_keys, offset, block_rows, 1), offset, lengths
        )
        weights_low = jnp.exp(scores - logsum[..., None]).astype(jnp.bfloat16)
        value_heads = split_heads(lax.dynamic_slice_in_dim(all_values, offset, block_rows, 1))
        return (
            running
            + jnp.einsum(
                "shqk,skhd->sqhd", weights_low, value_heads, preferred_element_type=jnp.float32
            ),
            None,
        )

    mixed_heads, _ = lax.scan(
        mix_step, jnp.zeros(query_heads.shape, jnp.float32), jnp.arange(blocks)
    )
    return (mixed_heads.reshape(query.shape), logsum)


def query_side(query, all_keys, all_values, grad_low, logsum, row_delta, lengths):
    seq_span = all_keys.shape[1]
    block_rows = math.gcd(seq_span, 512)
    blocks = seq_span // block_rows
    query_heads = split_heads(query)
    grad_heads = split_heads(grad_low)
    slot_count = query.shape[0]
    width = query.shape[2]

    def step(running, step_index):
        offset = step_index * block_rows
        key_block = lax.dynamic_slice_in_dim(all_keys, offset, block_rows, 1)
        value_block = lax.dynamic_slice_in_dim(all_values, offset, block_rows, 1)
        scores = block_scores(query_heads, key_block, offset, lengths)
        grad_scores, weights_low = score_grads(
            scores, logsum, row_delta, grad_heads, split_heads(value_block)
        )
        grad_acc = running[0] + jnp.einsum(
            "shqk,skhd->sqhd",
            grad_scores,
            split_heads(key_block),
            preferred_element_type=jnp.float32,
        )
        key_part = jnp.einsum(
            "shqk,sqhd->skhd", grad_scores, query_heads, preferred_element_type=jnp.float32
        ).reshape(slot_count, block_rows, width)
        value_part = jnp.einsum(
            "shqk,sqhd->skhd", weights_low, grad_heads, preferred_element_type=jnp.float32
        ).reshape(slot_count, block_rows, width)
        key_buffer = lax.dynamic_update_slice_in_dim(running[1], key_part, offset, 1)
        value_buffer = lax.dynamic_update_slice_in_dim(running[2], value_part, offset, 1)
        return ((grad_acc, key_buffer, value_buffer), None)

    start = (jnp.zeros(query_heads.shape, jnp.float32),)
    empty = jnp.zeros((slot_count, seq_span, width), jnp.float32)
    start = start + (empty, empty)
    result, _ = lax.scan(step, start, jnp.arange(blocks))
    return (result[0].reshape(query.shape), result[1:])


def sum_by_adapter(picks, terms):
    return jnp.einsum("si,sdkr->dikr", picks, terms, precision=lax.Precision.HIGHEST)


def on_device(
    tokens,
    cotangent,
    lengths,
    adapter_ids,
    attn_weight,
    fc1_weight,
    fc2_weight,
    vectors,
    fc1_bias,
    adapter_down,
    adapter_up,
    ff_adapters,
):
    slot_count, slot_rows, width = tokens.shape
    row_start = lax.axis_index("seq") * slot_rows
    positions = row_start + jnp.arange(slot_rows)
    live_rows = (positions[None, :] < lengths[:, None]).astype(jnp.float32)[..., None]
    matches = adapter_ids[:, None] == jnp.arange(ADAPTERS)[None, :]
    onehot_low = matches.astype(jnp.bfloat16)
    onehot_full = matches.astype(jnp.float32)
    gathered = (
        lax.all_gather(attn_weight, ("fsdp", "seq"), axis=0, tiled=True),
        lax.all_gather(fc1_weight, ("fsdp", "seq"), axis=0, tiled=True),
        lax.all_gather(fc2_weight, ("fsdp", "seq"), axis=0, tiled=True),
        lax.all_gather(vectors, ("fsdp", "seq"), axis=0, tiled=True),
        lax.all_gather(fc1_bias, ("fsdp", "seq"), axis=0, tiled=True),
        lax.all_gather(adapter_down, ("fsdp", "seq"), axis=0, tiled=True),
        lax.all_gather(adapter_up, ("fsdp", "seq"), axis=0, tiled=True),
        lax.all_gather(ff_adapters, ("fsdp", "seq"), axis=0, tiled=True),
    )
    attn_all, fc1_all, fc2_all, vector_cols, bias_ff, down_pick, up_pick, ff_pick = unpack(
        gathered, onehot_low
    )
    query_pre, inner_query = project(
        tokens, attn_all[:, 0, :], down_pick[:, :, 0], up_pick[:, :, 0]
    )
    query = ((query_pre + vector_cols[:, 0]) * 0.125).astype(jnp.bfloat16)
    key_pre, inner_key = project(tokens, attn_all[:, 1, :], down_pick[:, :, 1], up_pick[:, :, 1])
    keys = key_pre.astype(jnp.bfloat16)
    value_pre, inner_value = project(
        tokens, attn_all[:, 2, :], down_pick[:, :, 2], up_pick[:, :, 2]
    )
    values = (value_pre + vector_cols[:, 1]).astype(jnp.bfloat16)
    all_keys, all_values = (
        lax.all_gather(keys, "seq", axis=1, tiled=True),
        lax.all_gather(values, "seq", axis=1, tiled=True),
    )
    attended, logsum = attend(query, all_keys, all_values, lengths)
    mixed = attended.astype(jnp.bfloat16)
    branch_pre, inner_branch = project(
        mixed, attn_all[:, 3, :], down_pick[:, :, 3], up_pick[:, :, 3]
    )
    first_sum = tokens.astype(jnp.float32) + branch_pre + vector_cols[:, 2]
    normed, first_back = jax.vjp(
        partial(norm_rows, gain=vector_cols[:, 4], shift=vector_cols[:, 5]), first_sum
    )
    normed_low = normed.astype(jnp.bfloat16)
    hidden_pre, inner_hidden = project(normed_low, fc1_all, down_pick[:, :, 4], ff_pick[:, :, 0])
    activated, gelu_back = jax.vjp(gelu_exact, hidden_pre + bias_ff)
    activated_low = activated.astype(jnp.bfloat16)
    out_pre, inner_out = project(activated_low, fc2_all, ff_pick[:, :, 1], up_pick[:, :, 4])
    second = normed + out_pre + vector_cols[:, 3]
    final, second_back = jax.vjp(
        partial(norm_rows, gain=vector_cols[:, 6], shift=vector_cols[:, 7]), second
    )
    layer_out = (final * live_rows).astype(jnp.bfloat16)
    regathered = (
        lax.all_gather(attn_weight, ("fsdp", "seq"), axis=0, tiled=True),
        lax.all_gather(fc1_weight, ("fsdp", "seq"), axis=0, tiled=True),
        lax.all_gather(fc2_weight, ("fsdp", "seq"), axis=0, tiled=True),
        lax.all_gather(vectors, ("fsdp", "seq"), axis=0, tiled=True),
        lax.all_gather(fc1_bias, ("fsdp", "seq"), axis=0, tiled=True),
        lax.all_gather(adapter_down, ("fsdp", "seq"), axis=0, tiled=True),
        lax.all_gather(adapter_up, ("fsdp", "seq"), axis=0, tiled=True),
        lax.all_gather(ff_adapters, ("fsdp", "seq"), axis=0, tiled=True),
    )
    attn_all, fc1_all, fc2_all, vector_cols, bias_ff, down_pick, up_pick, ff_pick = unpack(
        regathered, onehot_low
    )
    grad_final = cotangent.astype(jnp.float32) * live_rows
    (grad_second,) = second_back(grad_final)
    grad_out_low = grad_second.astype(jnp.bfloat16)
    grad_activated, down_of_fc2, up_of_fc2 = project_back(
        activated_low, inner_out, grad_out_low, fc2_all, ff_pick[:, :, 1], up_pick[:, :, 4]
    )
    (grad_hidden,) = gelu_back(grad_activated)
    grad_hidden_low = grad_hidden.astype(jnp.bfloat16)
    grad_normed, down_of_fc1, up_of_fc1 = project_back(
        normed_low, inner_hidden, grad_hidden_low, fc1_all, down_pick[:, :, 4], ff_pick[:, :, 0]
    )
    (grad_first,) = first_back(grad_normed + grad_second)
    grad_branch_low = grad_first.astype(jnp.bfloat16)
    grad_mixed, down_of_out, up_of_out = project_back(
        mixed,
        inner_branch,
        grad_branch_low,
        attn_all[:, 3, :],
        down_pick[:, :, 3],
        up_pick[:, :, 3],
    )
    grad_mixed_low = grad_mixed.astype(jnp.bfloat16)
    row_delta = jnp.einsum(
        "sqhd,sqhd->shq", split_heads(grad_mixed_low.astype(jnp.float32)), split_heads(attended)
    )
    grad_query, parts = query_side(
        query, all_keys, all_values, grad_mixed_low, logsum, row_delta, lengths
    )
    grad_keys, grad_values = (
        lax.psum_scatter(
            parts[0].astype(jnp.bfloat16), "seq", scatter_dimension=1, tiled=True
        ).astype(jnp.float32),
        lax.psum_scatter(
            parts[1].astype(jnp.bfloat16), "seq", scatter_dimension=1, tiled=True
        ).astype(jnp.float32),
    )
    grad_query_low = grad_query.astype(jnp.bfloat16) * 0.125
    grad_keys_low = grad_keys.astype(jnp.bfloat16)
    grad_values_low = grad_values.astype(jnp.bfloat16)
    grad_from_query, down_of_query, up_of_query = project_back(
        tokens, inner_query, grad_query_low, attn_all[:, 0, :], down_pick[:, :, 0], up_pick[:, :, 0]
    )
    grad_from_key, down_of_key, up_of_key = project_back(
        tokens, inner_key, grad_keys_low, attn_all[:, 1, :], down_pick[:, :, 1], up_pick[:, :, 1]
    )
    grad_from_value, down_of_value, up_of_value = project_back(
        tokens,
        inner_value,
        grad_values_low,
        attn_all[:, 2, :],
        down_pick[:, :, 2],
        up_pick[:, :, 2],
    )
    input_grad = (grad_from_query + grad_from_key + grad_from_value + grad_first).astype(
        jnp.bfloat16
    )
    down_terms = jnp.stack(
        (down_of_query, down_of_key, down_of_value, down_of_out, down_of_fc1), axis=2
    )
    up_terms = jnp.stack((up_of_query, up_of_key, up_of_value, up_of_out, up_of_fc2), axis=2)
    ff_terms = jnp.stack((up_of_fc1, down_of_fc2), axis=2)
    down_table = sum_by_adapter(onehot_full, down_terms)
    up_table = sum_by_adapter(onehot_full, up_terms)
    ff_table = sum_by_adapter(onehot_full, ff_terms)
    down_grad, up_grad, ff_grad = (
        lax.psum_scatter(down_table, ("fsdp", "seq"), scatter_dimension=0, tiled=True),
        lax.psum_scatter(up_table, ("fsdp", "seq"), scatter_dimension=0, tiled=True),
        lax.psum_scatter(ff_table, ("fsdp", "seq"), scatter_dimension=0, tiled=True),
    )
    return (layer_out, input_grad, down_grad, up_grad, ff_grad)


MESH = pl.DeviceIdType.MESH
CHUNKS = 14
ROUTES = 11


class Spot:
    def __init__(self):
        self.y = lax.axis_index("fsdp")
        self.s = lax.axis_index("seq")
        self.z = self.s // 4
        self.x = (self.s // 2) % 2
        self.c = self.s % 2

    def at(self, dy=0, dz=0, dx=0, dc=0):
        y = (self.y + dy) % 2
        z = (self.z + dz) % 4
        x = (self.x + dx) % 2
        c = (self.c + dc) % 2
        return (y, (z * 2 + x) * 2 + c)


def enter(spot):
    barrier = pltpu.get_barrier_semaphore()
    for step in range(1, 16):
        peer = (spot.y, (spot.s + step) % 16)
        pl.semaphore_signal(barrier, inc=1, device_id=peer, device_id_type=MESH)
    pl.semaphore_signal(barrier, inc=1, device_id=spot.at(dy=1), device_id_type=MESH)
    pl.semaphore_wait(barrier, 16)


class Gather:
    def __init__(self, spot, parts, send, recv):
        self.spot, self.parts, self.send, self.recv = spot, parts, send, recv
        self.started = []

    def block(self, k, dy, dx, dc, zs=slice(None)):
        p = self.spot
        if zs == slice(None):
            zs = pl.ds(0, 4)
        return self.parts[k].at[(p.y + dy) % 2, zs, (p.x + dx) % 2, (p.c + dc) % 2]

    def piece(self, k, dz):
        p = self.spot
        return self.parts[k].at[p.y, (p.z + dz) % 4, p.x, p.c]

    def copy(self, ref, k, route, peer):
        return pltpu.make_async_remote_copy(
            src_ref=ref,
            dst_ref=ref,
            send_sem=self.send.at[k, route],
            recv_sem=self.recv.at[k, route],
            device_id=peer,
            device_id_type=MESH,
        )

    def push(self, ref, k, route, peer):
        copy = self.copy(ref, k, route, peer)
        copy.start()
        self.started.append(copy)

    def arrive(self, ref, k, route):
        self.copy(ref, k, route, self.spot.at(dc=1)).wait_recv()

    def along_z(self, k):
        for d in range(1, 4):
            self.push(self.piece(k, 0), k, d - 1, self.spot.at(dz=d))

    def across(self, k):
        for d in range(1, 4):
            self.arrive(self.piece(k, 4 - d), k, d - 1)
        line = self.block(k, 0, 0, 0)
        self.push(line, k, 3, self.spot.at(dx=1))
        self.push(line, k, 4, self.spot.at(dy=1))
        self.push(line, k, 5, self.spot.at(dc=1))

    def corner(self, k):
        self.arrive(self.block(k, 0, 1, 0), k, 3)
        self.push(self.block(k, 0, 1, 0, pl.ds(0, 2)), k, 6, self.spot.at(dy=1))
        self.arrive(self.block(k, 1, 0, 0), k, 4)
        self.push(self.block(k, 1, 0, 0, pl.ds(2, 2)), k, 7, self.spot.at(dx=1))
        self.push(self.block(k, 0, 1, 0), k, 8, self.spot.at(dc=1))
        self.push(self.block(k, 1, 0, 0), k, 9, self.spot.at(dc=1))

    def twin(self, k):
        self.arrive(self.block(k, 1, 1, 0, pl.ds(0, 2)), k, 6)
        self.arrive(self.block(k, 1, 1, 0, pl.ds(2, 2)), k, 7)
        self.push(self.block(k, 1, 1, 0), k, 10, self.spot.at(dc=1))

    def ready(self, k):
        self.arrive(self.block(k, 0, 0, 1), k, 5)
        self.arrive(self.block(k, 0, 1, 1), k, 8)
        self.arrive(self.block(k, 1, 0, 1), k, 9)
        self.arrive(self.block(k, 1, 1, 1), k, 10)

    def step(self, t):
        for k, move in ((t, self.along_z), (t - 1, self.across), (t - 2, self.corner), (t - 3, self.twin)):
            if 0 <= k < len(self.parts):
                move(k)
        if 0 <= t - 4 < len(self.parts):
            self.ready(t - 4)

    def finish(self):
        for copy in self.started:
            copy.wait_send()


def gather_kernel(attn, fc1, fc2, low_rank, ff_rank, wide, tall, rank_all, ff_all, own, send, recv):
    spot = Spot()
    here = (spot.y, spot.z, spot.x, spot.c)
    wides = [wide.at[k] for k in range(8)]
    talls = [tall.at[k] for k in range(4)]
    sources = [attn.at[j] for j in range(4)]
    sources += [fc1.at[:, pl.ds(q * 1024, 1024)] for q in range(4)]
    sources += [fc2.at[:, pl.ds(q * 256, 256)] for q in range(4)] + [low_rank, ff_rank]
    parts = wides + talls + [rank_all, ff_all]
    locals_ = []
    for k, (source, part) in enumerate(zip(sources, parts)):
        copy = pltpu.make_async_copy(source, part.at[here], own.at[k])
        copy.start()
        locals_.append(copy)
    order = [0, 12, 1, 2, 3, 13, 4, 5, 6, 7, 8, 9, 10, 11]
    gather = Gather(spot, [parts[k] for k in order], send, recv)
    enter(spot)
    for copy in locals_:
        copy.wait()
    for t in range(CHUNKS + 4):
        gather.step(t)
    gather.finish()


def gather_all(attn, fc1, fc2, low_rank, ff_rank):
    lead = (2, 4, 2, 2)
    shapes = [
        (8,) + lead + (32, 1024),
        (4,) + lead + (128, 256),
        lead + low_rank.shape,
        lead + ff_rank.shape,
    ]
    anywhere = pl.BlockSpec(memory_space=pl.ANY)
    return pl.pallas_call(
        gather_kernel,
        out_shape=[jax.ShapeDtypeStruct(shape, jnp.bfloat16) for shape in shapes],
        in_specs=[anywhere] * 5,
        out_specs=[anywhere] * 4,
        scratch_shapes=[
            pltpu.SemaphoreType.DMA((CHUNKS,)),
            pltpu.SemaphoreType.DMA((CHUNKS, ROUTES)),
            pltpu.SemaphoreType.DMA((CHUNKS, ROUTES)),
        ],
        compiler_params=pltpu.CompilerParams(collective_id=0, has_side_effects=True),
        name="gather_all",
    )(attn, fc1, fc2, low_rank, ff_rank)


def to_heads(stack):
    parts, slots, rows, _ = stack.shape
    split = stack.reshape(parts, slots, rows, HEADS, HEAD)
    return lax.all_to_all(split, "seq", split_axis=3, concat_axis=2, tiled=True)[:, :, :, 0]


def to_rows(stack):
    back = lax.all_to_all(stack[:, :, :, None], "seq", split_axis=2, concat_axis=3, tiled=True)
    return back.reshape(back.shape[:3] + (HEADS * HEAD,))


def fast_device(
    tokens,
    cotangent,
    lengths,
    adapter_ids,
    attn_weight,
    fc1_weight,
    fc2_weight,
    vectors,
    fc1_bias,
    adapter_down,
    adapter_up,
    ff_adapters,
):
    f32, bf16 = jnp.float32, jnp.bfloat16
    slot_count, slot_rows, width = tokens.shape
    group = lax.axis_index("fsdp")
    positions = lax.axis_index("seq") * slot_rows + jnp.arange(slot_rows)
    live_rows = (positions[None, :] < lengths[:, None]).astype(f32)[..., None]
    ids = lax.all_gather(adapter_ids, "fsdp", axis=0, tiled=True)
    onehot = (ids[:, None] == jnp.arange(ADAPTERS)[None, :]).astype(bf16)

    def pick(table):
        return jnp.einsum("si,dikr->dskr", onehot, table, preferred_element_type=f32).astype(bf16)

    own_rows = adapter_down.shape[0]
    ff_rows = ff_adapters.shape[0]
    down = pick(adapter_down).reshape(own_rows, -1)
    up = pick(adapter_up).reshape(own_rows, -1)
    low_rank = jnp.concatenate([down, up, vectors, jnp.zeros((own_rows, 120), bf16)], axis=1)
    ff_part = pick(ff_adapters).reshape(ff_rows, -1)
    bias_part = jnp.zeros((16, 128), bf16).at[0].set(fc1_bias)
    ff_rank = jnp.concatenate([ff_part, bias_part], axis=0)
    attn_split = attn_weight.transpose(1, 0, 2)
    wide, tall, rank_all, ff_all = gather_all(attn_split, fc1_weight, fc2_weight, low_rank, ff_rank)
    attn_all = [wide[j].reshape(width, width) for j in range(4)]
    fc1_all = jnp.concatenate([wide[4 + q].reshape(width, width) for q in range(4)], axis=1)
    fc2_all = jnp.concatenate([tall[q].reshape(4 * width, width // 4) for q in range(4)], axis=1)
    rank_all = rank_all.reshape(width, -1)
    ranks = rank_all.shape[1]

    def own_slots(table, rows, kinds):
        table = table.reshape(rows, 2, slot_count, kinds, 16)
        return lax.dynamic_index_in_dim(table, group, 1, keepdims=False).transpose(1, 0, 2, 3)

    down_pick = own_slots(rank_all[:, :320], width, 5)
    up_pick = own_slots(rank_all[:, 320:640], width, 5)
    vector_cols = rank_all[:, 640:648].astype(f32)
    ff_all = ff_all.reshape(32, 144, 128)
    ff_pick = own_slots(ff_all[:, :128].reshape(4 * width, 128), 4 * width, 2)
    bias_ff = ff_all[:, 128].reshape(4 * width).astype(f32)

    query_pre, inner_query = project(tokens, attn_all[0], down_pick[:, :, 0], up_pick[:, :, 0])
    query = ((query_pre + vector_cols[:, 0]) * 0.125).astype(bf16)
    key_pre, inner_key = project(tokens, attn_all[1], down_pick[:, :, 1], up_pick[:, :, 1])
    keys = key_pre.astype(bf16)
    value_pre, inner_value = project(tokens, attn_all[2], down_pick[:, :, 2], up_pick[:, :, 2])
    values = (value_pre + vector_cols[:, 1]).astype(bf16)
    head_q, head_k, head_v = to_heads(jnp.stack([query, keys, values]))
    scores = jnp.einsum("sqd,skd->sqk", head_q, head_k, preferred_element_type=f32)
    valid = jnp.arange(scores.shape[2])[None, :] < lengths[:, None]
    scores = jnp.where(valid[:, None, :], scores, NEG_FILL)
    top = jnp.max(scores, axis=-1, keepdims=True)
    shifted = jnp.exp(scores - top)
    probs = shifted / jnp.sum(shifted, axis=-1, keepdims=True)
    probs_low = probs.astype(bf16)
    head_out = jnp.einsum("sqk,skd->sqd", probs_low, head_v, preferred_element_type=f32)
    mixed = to_rows(head_out.astype(bf16)[None])[0]
    branch_pre, inner_branch = project(mixed, attn_all[3], down_pick[:, :, 3], up_pick[:, :, 3])
    first_sum = tokens.astype(f32) + branch_pre + vector_cols[:, 2]
    normed, first_back = jax.vjp(
        partial(norm_rows, gain=vector_cols[:, 4], shift=vector_cols[:, 5]), first_sum
    )
    normed_low = normed.astype(bf16)
    hidden_pre, inner_hidden = project(normed_low, fc1_all, down_pick[:, :, 4], ff_pick[:, :, 0])
    activated, gelu_back = jax.vjp(gelu_exact, hidden_pre + bias_ff)
    activated_low = activated.astype(bf16)
    out_pre, inner_out = project(activated_low, fc2_all, ff_pick[:, :, 1], up_pick[:, :, 4])
    second = normed + out_pre + vector_cols[:, 3]
    final, second_back = jax.vjp(
        partial(norm_rows, gain=vector_cols[:, 6], shift=vector_cols[:, 7]), second
    )
    layer_out = (final * live_rows).astype(bf16)

    (grad_second,) = second_back(cotangent.astype(f32) * live_rows)
    grad_out_low = grad_second.astype(bf16)
    grad_activated, down_of_fc2, up_of_fc2 = project_back(
        activated_low, inner_out, grad_out_low, fc2_all, ff_pick[:, :, 1], up_pick[:, :, 4]
    )
    (grad_hidden,) = gelu_back(grad_activated)
    grad_hidden_low = grad_hidden.astype(bf16)
    grad_normed, down_of_fc1, up_of_fc1 = project_back(
        normed_low, inner_hidden, grad_hidden_low, fc1_all, down_pick[:, :, 4], ff_pick[:, :, 0]
    )
    (grad_first,) = first_back(grad_normed + grad_second)
    grad_branch_low = grad_first.astype(bf16)
    grad_mixed, down_of_out, up_of_out = project_back(
        mixed, inner_branch, grad_branch_low, attn_all[3], down_pick[:, :, 3], up_pick[:, :, 3]
    )
    head_g = to_heads(grad_mixed.astype(bf16)[None])[0]
    delta = jnp.sum(head_g.astype(f32) * head_out, axis=-1, keepdims=True)
    grad_probs = jnp.einsum("sqd,skd->sqk", head_g, head_v, preferred_element_type=f32)
    grad_scores = (probs * (grad_probs - delta)).astype(bf16)
    grad_query = jnp.einsum("sqk,skd->sqd", grad_scores, head_k, preferred_element_type=f32)
    grad_keys = jnp.einsum("sqk,sqd->skd", grad_scores, head_q, preferred_element_type=f32)
    grad_values = jnp.einsum("sqk,sqd->skd", probs_low, head_g, preferred_element_type=f32)
    stack = jnp.stack([grad_query.astype(bf16), grad_keys.astype(bf16), grad_values.astype(bf16)])
    grad_query_low, grad_keys_low, grad_values_low = to_rows(stack)
    grad_query_low = grad_query_low * 0.125
    from_query, down_of_query, up_of_query = project_back(
        tokens, inner_query, grad_query_low, attn_all[0], down_pick[:, :, 0], up_pick[:, :, 0]
    )
    from_key, down_of_key, up_of_key = project_back(
        tokens, inner_key, grad_keys_low, attn_all[1], down_pick[:, :, 1], up_pick[:, :, 1]
    )
    from_value, down_of_value, up_of_value = project_back(
        tokens, inner_value, grad_values_low, attn_all[2], down_pick[:, :, 2], up_pick[:, :, 2]
    )
    input_grad = (from_query + from_key + from_value + grad_first).astype(bf16)

    def owners(terms, kinds):
        stacked = jnp.stack(terms, axis=2).astype(bf16)
        rows = stacked.shape[1] // 32
        return stacked.reshape(slot_count, 2, 16, rows * kinds * 16).transpose(2, 0, 1, 3)

    sent = jnp.concatenate(
        [
            owners((down_of_query, down_of_key, down_of_value, down_of_out, down_of_fc1), 5),
            owners((up_of_query, up_of_key, up_of_value, up_of_out, up_of_fc2), 5),
            owners((up_of_fc1, down_of_fc2), 2),
        ],
        axis=3,
    )
    got = lax.all_to_all(sent, "seq", split_axis=0, concat_axis=0, tiled=True)
    summed = jnp.sum(got.astype(f32), axis=0).astype(bf16)
    crossed = lax.all_to_all(summed[None], "fsdp", split_axis=2, concat_axis=0, tiled=True)
    slots = crossed.reshape(2 * slot_count, -1).astype(f32)
    cut = own_rows * 80
    picks = onehot.astype(f32)

    def spread(part, kinds):
        part = part.reshape(2 * slot_count, -1, kinds, 16)
        return jnp.einsum("si,sdkr->dikr", picks, part, precision=lax.Precision.HIGHEST)

    return (
        layer_out,
        input_grad,
        spread(slots[:, :cut], 5),
        spread(slots[:, cut : 2 * cut], 5),
        spread(slots[:, 2 * cut :], 2),
    )


def solution(mesh):
    in_specs = (
        P("fsdp", "seq", None),
        P("fsdp", "seq", None),
        P("fsdp"),
        P("fsdp"),
        P(("fsdp", "seq"), None, None),
        P(("fsdp", "seq"), None),
        P(("fsdp", "seq"), None),
        P(("fsdp", "seq"), None),
        P(("fsdp", "seq")),
        P(("fsdp", "seq"), None, None, None),
        P(("fsdp", "seq"), None, None, None),
        P(("fsdp", "seq"), None, None, None),
    )
    out_specs = (
        P("fsdp", "seq", None),
        P("fsdp", "seq", None),
        P(("fsdp", "seq"), None, None, None),
        P(("fsdp", "seq"), None, None, None),
        P(("fsdp", "seq"), None, None, None),
    )
    fast = mesh.shape["fsdp"] == 2 and mesh.shape["seq"] == HEADS
    return jax.shard_map(
        fast_device if fast else on_device, mesh=mesh, in_specs=in_specs, out_specs=out_specs, check_vma=False
    )
```

```python
from functools import partial
import math

import jax
import jax.numpy as jnp
from jax import lax
from jax.experimental import pallas as pl
from jax.experimental.pallas import tpu as pltpu
from jax.sharding import PartitionSpec as P

HEADS = 16
HEAD = 64
ADAPTERS = 8


NEG_FILL = -1e30
NORM_EPS = 1e-05


def split_heads(values_in):
    return values_in.reshape(values_in.shape[:-1] + (HEADS, HEAD))


def norm_rows(value, gain, shift):
    centered = value - jnp.mean(value, axis=-1, keepdims=True)
    scaled = centered * lax.rsqrt(jnp.mean(centered * centered, axis=-1, keepdims=True) + NORM_EPS)
    return scaled * gain + shift


def gelu_exact(value):
    return jax.nn.gelu(value, approximate=False)


def choose(onehot, table):
    return jnp.einsum("si,dikr->sdkr", onehot, table, preferred_element_type=jnp.float32).astype(
        jnp.bfloat16
    )


def unpack(gathered, onehot):
    attn_all, fc1_all, fc2_all, vector_all, bias_ff, down_all, up_all, ff_all = gathered
    return (
        attn_all,
        fc1_all,
        fc2_all,
        vector_all.astype(jnp.float32),
        bias_ff.astype(jnp.float32),
        choose(onehot, down_all),
        choose(onehot, up_all),
        choose(onehot, ff_all),
    )


def project(inputs, weight, down_table, up_table):
    frozen_part = jnp.einsum("spd,de->spe", inputs, weight, preferred_element_type=jnp.float32)
    inner_low = jnp.einsum(
        "spd,sdr->spr", inputs, down_table, preferred_element_type=jnp.float32
    ).astype(jnp.bfloat16)
    return (
        frozen_part
        + jnp.einsum("spr,ser->spe", inner_low, up_table, preferred_element_type=jnp.float32),
        inner_low,
    )


def project_back(inputs, inner_low, grad_out, weight, down_table, up_table):
    grad_inner = jnp.einsum(
        "spe,ser->spr", grad_out, up_table, preferred_element_type=jnp.float32
    ).astype(jnp.bfloat16)
    grad_in = jnp.einsum("spe,de->spd", grad_out, weight, preferred_element_type=jnp.float32)
    grad_in = grad_in + jnp.einsum(
        "spr,sdr->spd", grad_inner, down_table, preferred_element_type=jnp.float32
    )
    grad_up = jnp.einsum("spe,spr->ser", grad_out, inner_low, preferred_element_type=jnp.float32)
    grad_down = jnp.einsum("spd,spr->sdr", inputs, grad_inner, preferred_element_type=jnp.float32)
    return (grad_in, grad_down, grad_up)


def block_scores(query_heads, key_block, key_start, lengths):
    block_rows = key_block.shape[1]
    scores = jnp.einsum(
        "sqhd,skhd->shqk", query_heads, split_heads(key_block), preferred_element_type=jnp.float32
    )
    valid_keys = (key_start + jnp.arange(block_rows))[None, :] < lengths[:, None]
    return jnp.where(valid_keys[:, None, None, :], scores, NEG_FILL)


def score_grads(scores, logsum, row_delta, grad_heads, value_heads):
    probs = jnp.exp(scores - logsum[..., None])
    grad_probs = jnp.einsum(
        "sqhd,skhd->shqk", grad_heads, value_heads, preferred_element_type=jnp.float32
    )
    grad_scores = (probs * (grad_probs - row_delta[..., None])).astype(jnp.bfloat16)
    return (grad_scores, probs.astype(jnp.bfloat16))


def attend(query, all_keys, all_values, lengths):
    seq_span = all_keys.shape[1]
    block_rows = math.gcd(seq_span, 512)
    blocks = seq_span // block_rows
    query_heads = split_heads(query)
    slot_count, query_rows = (query.shape[0], query.shape[1])
    stats_shape = (slot_count, HEADS, query_rows)

    def stats_step(running, step_index):
        row_top, row_total = running
        offset = step_index * block_rows
        scores = block_scores(
            query_heads, lax.dynamic_slice_in_dim(all_keys, offset, block_rows, 1), offset, lengths
        )
        new_top = jnp.maximum(row_top, jnp.max(scores, axis=-1))
        row_total = row_total * jnp.exp(row_top - new_top) + jnp.sum(
            jnp.exp(scores - new_top[..., None]), axis=-1
        )
        return ((new_top, row_total), None)

    start_top = jnp.full(stats_shape, NEG_FILL, jnp.float32)
    (row_top, row_total), _ = lax.scan(
        stats_step, (start_top, jnp.zeros(stats_shape, jnp.float32)), jnp.arange(blocks)
    )
    logsum = row_top + jnp.log(row_total)

    def mix_step(running, step_index):
        offset = step_index * block_rows
        scores = block_scores(
            query_heads, lax.dynamic_slice_in_dim(all_keys, offset, block_rows, 1), offset, lengths
        )
        weights_low = jnp.exp(scores - logsum[..., None]).astype(jnp.bfloat16)
        value_heads = split_heads(lax.dynamic_slice_in_dim(all_values, offset, block_rows, 1))
        return (
            running
            + jnp.einsum(
                "shqk,skhd->sqhd", weights_low, value_heads, preferred_element_type=jnp.float32
            ),
            None,
        )

    mixed_heads, _ = lax.scan(
        mix_step, jnp.zeros(query_heads.shape, jnp.float32), jnp.arange(blocks)
    )
    return (mixed_heads.reshape(query.shape), logsum)


def query_side(query, all_keys, all_values, grad_low, logsum, row_delta, lengths):
    seq_span = all_keys.shape[1]
    block_rows = math.gcd(seq_span, 512)
    blocks = seq_span // block_rows
    query_heads = split_heads(query)
    grad_heads = split_heads(grad_low)
    slot_count = query.shape[0]
    width = query.shape[2]

    def step(running, step_index):
        offset = step_index * block_rows
        key_block = lax.dynamic_slice_in_dim(all_keys, offset, block_rows, 1)
        value_block = lax.dynamic_slice_in_dim(all_values, offset, block_rows, 1)
        scores = block_scores(query_heads, key_block, offset, lengths)
        grad_scores, weights_low = score_grads(
            scores, logsum, row_delta, grad_heads, split_heads(value_block)
        )
        grad_acc = running[0] + jnp.einsum(
            "shqk,skhd->sqhd",
            grad_scores,
            split_heads(key_block),
            preferred_element_type=jnp.float32,
        )
        key_part = jnp.einsum(
            "shqk,sqhd->skhd", grad_scores, query_heads, preferred_element_type=jnp.float32
        ).reshape(slot_count, block_rows, width)
        value_part = jnp.einsum(
            "shqk,sqhd->skhd", weights_low, grad_heads, preferred_element_type=jnp.float32
        ).reshape(slot_count, block_rows, width)
        key_buffer = lax.dynamic_update_slice_in_dim(running[1], key_part, offset, 1)
        value_buffer = lax.dynamic_update_slice_in_dim(running[2], value_part, offset, 1)
        return ((grad_acc, key_buffer, value_buffer), None)

    start = (jnp.zeros(query_heads.shape, jnp.float32),)
    empty = jnp.zeros((slot_count, seq_span, width), jnp.float32)
    start = start + (empty, empty)
    result, _ = lax.scan(step, start, jnp.arange(blocks))
    return (result[0].reshape(query.shape), result[1:])


def sum_by_adapter(picks, terms):
    return jnp.einsum("si,sdkr->dikr", picks, terms, precision=lax.Precision.HIGHEST)


def on_device(
    tokens,
    cotangent,
    lengths,
    adapter_ids,
    attn_weight,
    fc1_weight,
    fc2_weight,
    vectors,
    fc1_bias,
    adapter_down,
    adapter_up,
    ff_adapters,
):
    slot_count, slot_rows, width = tokens.shape
    row_start = lax.axis_index("seq") * slot_rows
    positions = row_start + jnp.arange(slot_rows)
    live_rows = (positions[None, :] < lengths[:, None]).astype(jnp.float32)[..., None]
    matches = adapter_ids[:, None] == jnp.arange(ADAPTERS)[None, :]
    onehot_low = matches.astype(jnp.bfloat16)
    onehot_full = matches.astype(jnp.float32)
    gathered = (
        lax.all_gather(attn_weight, ("fsdp", "seq"), axis=0, tiled=True),
        lax.all_gather(fc1_weight, ("fsdp", "seq"), axis=0, tiled=True),
        lax.all_gather(fc2_weight, ("fsdp", "seq"), axis=0, tiled=True),
        lax.all_gather(vectors, ("fsdp", "seq"), axis=0, tiled=True),
        lax.all_gather(fc1_bias, ("fsdp", "seq"), axis=0, tiled=True),
        lax.all_gather(adapter_down, ("fsdp", "seq"), axis=0, tiled=True),
        lax.all_gather(adapter_up, ("fsdp", "seq"), axis=0, tiled=True),
        lax.all_gather(ff_adapters, ("fsdp", "seq"), axis=0, tiled=True),
    )
    attn_all, fc1_all, fc2_all, vector_cols, bias_ff, down_pick, up_pick, ff_pick = unpack(
        gathered, onehot_low
    )
    query_pre, inner_query = project(
        tokens, attn_all[:, 0, :], down_pick[:, :, 0], up_pick[:, :, 0]
    )
    query = ((query_pre + vector_cols[:, 0]) * 0.125).astype(jnp.bfloat16)
    key_pre, inner_key = project(tokens, attn_all[:, 1, :], down_pick[:, :, 1], up_pick[:, :, 1])
    keys = key_pre.astype(jnp.bfloat16)
    value_pre, inner_value = project(
        tokens, attn_all[:, 2, :], down_pick[:, :, 2], up_pick[:, :, 2]
    )
    values = (value_pre + vector_cols[:, 1]).astype(jnp.bfloat16)
    all_keys, all_values = (
        lax.all_gather(keys, "seq", axis=1, tiled=True),
        lax.all_gather(values, "seq", axis=1, tiled=True),
    )
    attended, logsum = attend(query, all_keys, all_values, lengths)
    mixed = attended.astype(jnp.bfloat16)
    branch_pre, inner_branch = project(
        mixed, attn_all[:, 3, :], down_pick[:, :, 3], up_pick[:, :, 3]
    )
    first_sum = tokens.astype(jnp.float32) + branch_pre + vector_cols[:, 2]
    normed, first_back = jax.vjp(
        partial(norm_rows, gain=vector_cols[:, 4], shift=vector_cols[:, 5]), first_sum
    )
    normed_low = normed.astype(jnp.bfloat16)
    hidden_pre, inner_hidden = project(normed_low, fc1_all, down_pick[:, :, 4], ff_pick[:, :, 0])
    activated, gelu_back = jax.vjp(gelu_exact, hidden_pre + bias_ff)
    activated_low = activated.astype(jnp.bfloat16)
    out_pre, inner_out = project(activated_low, fc2_all, ff_pick[:, :, 1], up_pick[:, :, 4])
    second = normed + out_pre + vector_cols[:, 3]
    final, second_back = jax.vjp(
        partial(norm_rows, gain=vector_cols[:, 6], shift=vector_cols[:, 7]), second
    )
    layer_out = (final * live_rows).astype(jnp.bfloat16)
    regathered = (
        lax.all_gather(attn_weight, ("fsdp", "seq"), axis=0, tiled=True),
        lax.all_gather(fc1_weight, ("fsdp", "seq"), axis=0, tiled=True),
        lax.all_gather(fc2_weight, ("fsdp", "seq"), axis=0, tiled=True),
        lax.all_gather(vectors, ("fsdp", "seq"), axis=0, tiled=True),
        lax.all_gather(fc1_bias, ("fsdp", "seq"), axis=0, tiled=True),
        lax.all_gather(adapter_down, ("fsdp", "seq"), axis=0, tiled=True),
        lax.all_gather(adapter_up, ("fsdp", "seq"), axis=0, tiled=True),
        lax.all_gather(ff_adapters, ("fsdp", "seq"), axis=0, tiled=True),
    )
    attn_all, fc1_all, fc2_all, vector_cols, bias_ff, down_pick, up_pick, ff_pick = unpack(
        regathered, onehot_low
    )
    grad_final = cotangent.astype(jnp.float32) * live_rows
    (grad_second,) = second_back(grad_final)
    grad_out_low = grad_second.astype(jnp.bfloat16)
    grad_activated, down_of_fc2, up_of_fc2 = project_back(
        activated_low, inner_out, grad_out_low, fc2_all, ff_pick[:, :, 1], up_pick[:, :, 4]
    )
    (grad_hidden,) = gelu_back(grad_activated)
    grad_hidden_low = grad_hidden.astype(jnp.bfloat16)
    grad_normed, down_of_fc1, up_of_fc1 = project_back(
        normed_low, inner_hidden, grad_hidden_low, fc1_all, down_pick[:, :, 4], ff_pick[:, :, 0]
    )
    (grad_first,) = first_back(grad_normed + grad_second)
    grad_branch_low = grad_first.astype(jnp.bfloat16)
    grad_mixed, down_of_out, up_of_out = project_back(
        mixed,
        inner_branch,
        grad_branch_low,
        attn_all[:, 3, :],
        down_pick[:, :, 3],
        up_pick[:, :, 3],
    )
    grad_mixed_low = grad_mixed.astype(jnp.bfloat16)
    row_delta = jnp.einsum(
        "sqhd,sqhd->shq", split_heads(grad_mixed_low.astype(jnp.float32)), split_heads(attended)
    )
    grad_query, parts = query_side(
        query, all_keys, all_values, grad_mixed_low, logsum, row_delta, lengths
    )
    grad_keys, grad_values = (
        lax.psum_scatter(
            parts[0].astype(jnp.bfloat16), "seq", scatter_dimension=1, tiled=True
        ).astype(jnp.float32),
        lax.psum_scatter(
            parts[1].astype(jnp.bfloat16), "seq", scatter_dimension=1, tiled=True
        ).astype(jnp.float32),
    )
    grad_query_low = grad_query.astype(jnp.bfloat16) * 0.125
    grad_keys_low = grad_keys.astype(jnp.bfloat16)
    grad_values_low = grad_values.astype(jnp.bfloat16)
    grad_from_query, down_of_query, up_of_query = project_back(
        tokens, inner_query, grad_query_low, attn_all[:, 0, :], down_pick[:, :, 0], up_pick[:, :, 0]
    )
    grad_from_key, down_of_key, up_of_key = project_back(
        tokens, inner_key, grad_keys_low, attn_all[:, 1, :], down_pick[:, :, 1], up_pick[:, :, 1]
    )
    grad_from_value, down_of_value, up_of_value = project_back(
        tokens,
        inner_value,
        grad_values_low,
        attn_all[:, 2, :],
        down_pick[:, :, 2],
        up_pick[:, :, 2],
    )
    input_grad = (grad_from_query + grad_from_key + grad_from_value + grad_first).astype(
        jnp.bfloat16
    )
    down_terms = jnp.stack(
        (down_of_query, down_of_key, down_of_value, down_of_out, down_of_fc1), axis=2
    )
    up_terms = jnp.stack((up_of_query, up_of_key, up_of_value, up_of_out, up_of_fc2), axis=2)
    ff_terms = jnp.stack((up_of_fc1, down_of_fc2), axis=2)
    down_table = sum_by_adapter(onehot_full, down_terms)
    up_table = sum_by_adapter(onehot_full, up_terms)
    ff_table = sum_by_adapter(onehot_full, ff_terms)
    down_grad, up_grad, ff_grad = (
        lax.psum_scatter(down_table, ("fsdp", "seq"), scatter_dimension=0, tiled=True),
        lax.psum_scatter(up_table, ("fsdp", "seq"), scatter_dimension=0, tiled=True),
        lax.psum_scatter(ff_table, ("fsdp", "seq"), scatter_dimension=0, tiled=True),
    )
    return (layer_out, input_grad, down_grad, up_grad, ff_grad)


MESH = pl.DeviceIdType.MESH
CHUNKS = 14
ROUTES = 11


class Spot:
    def __init__(self):
        self.y = lax.axis_index("fsdp")
        self.s = lax.axis_index("seq")
        self.z = self.s // 4
        self.x = (self.s // 2) % 2
        self.c = self.s % 2

    def at(self, dy=0, dz=0, dx=0, dc=0):
        y = (self.y + dy) % 2
        z = (self.z + dz) % 4
        x = (self.x + dx) % 2
        c = (self.c + dc) % 2
        return (y, (z * 2 + x) * 2 + c)


def enter(spot):
    barrier = pltpu.get_barrier_semaphore()
    for step in range(1, 16):
        peer = (spot.y, (spot.s + step) % 16)
        pl.semaphore_signal(barrier, inc=1, device_id=peer, device_id_type=MESH)
    pl.semaphore_signal(barrier, inc=1, device_id=spot.at(dy=1), device_id_type=MESH)
    pl.semaphore_wait(barrier, 16)


class Gather:
    def __init__(self, spot, parts, send, recv):
        self.spot, self.parts, self.send, self.recv = spot, parts, send, recv
        self.started = []

    def block(self, k, dy, dx, dc, zs=slice(None)):
        p = self.spot
        if zs == slice(None):
            zs = pl.ds(0, 4)
        return self.parts[k].at[(p.y + dy) % 2, zs, (p.x + dx) % 2, (p.c + dc) % 2]

    def piece(self, k, dz):
        p = self.spot
        return self.parts[k].at[p.y, (p.z + dz) % 4, p.x, p.c]

    def copy(self, ref, k, route, peer):
        return pltpu.make_async_remote_copy(
            src_ref=ref,
            dst_ref=ref,
            send_sem=self.send.at[k, route],
            recv_sem=self.recv.at[k, route],
            device_id=peer,
            device_id_type=MESH,
        )

    def push(self, ref, k, route, peer):
        copy = self.copy(ref, k, route, peer)
        copy.start()
        self.started.append(copy)

    def arrive(self, ref, k, route):
        self.copy(ref, k, route, self.spot.at(dc=1)).wait_recv()

    def along_z(self, k):
        for d in range(1, 4):
            self.push(self.piece(k, 0), k, d - 1, self.spot.at(dz=d))

    def across(self, k):
        for d in range(1, 4):
            self.arrive(self.piece(k, 4 - d), k, d - 1)
        line = self.block(k, 0, 0, 0)
        self.push(line, k, 3, self.spot.at(dx=1))
        self.push(line, k, 4, self.spot.at(dy=1))
        self.push(line, k, 5, self.spot.at(dc=1))

    def corner(self, k):
        self.arrive(self.block(k, 0, 1, 0), k, 3)
        self.push(self.block(k, 0, 1, 0, pl.ds(0, 2)), k, 6, self.spot.at(dy=1))
        self.arrive(self.block(k, 1, 0, 0), k, 4)
        self.push(self.block(k, 1, 0, 0, pl.ds(2, 2)), k, 7, self.spot.at(dx=1))
        self.push(self.block(k, 0, 1, 0), k, 8, self.spot.at(dc=1))
        self.push(self.block(k, 1, 0, 0), k, 9, self.spot.at(dc=1))

    def twin(self, k):
        self.arrive(self.block(k, 1, 1, 0, pl.ds(0, 2)), k, 6)
        self.arrive(self.block(k, 1, 1, 0, pl.ds(2, 2)), k, 7)
        self.push(self.block(k, 1, 1, 0), k, 10, self.spot.at(dc=1))

    def ready(self, k):
        self.arrive(self.block(k, 0, 0, 1), k, 5)
        self.arrive(self.block(k, 0, 1, 1), k, 8)
        self.arrive(self.block(k, 1, 0, 1), k, 9)
        self.arrive(self.block(k, 1, 1, 1), k, 10)

    def step(self, t):
        for k, move in ((t, self.along_z), (t - 1, self.across), (t - 2, self.corner), (t - 3, self.twin)):
            if 0 <= k < len(self.parts):
                move(k)
        if 0 <= t - 4 < len(self.parts):
            self.ready(t - 4)

    def finish(self):
        for copy in self.started:
            copy.wait_send()


F32, BF16 = jnp.float32, jnp.bfloat16
ORDER = (0, 12, 1, 2, 3, 13, 4, 5, 6, 7, 8, 9, 10, 11)
EARLY, LATE = 96, 64


def dot(left, right):
    return jnp.dot(left, right, preferred_element_type=F32)


def dot_nt(left, right):
    return lax.dot_general(left, right, (((1,), (1,)), ((), ())), preferred_element_type=F32)


def dot_tn(left, right):
    return lax.dot_general(left, right, (((0,), (0,)), ((), ())), preferred_element_type=F32)


def lanes(shape):
    return lax.broadcasted_iota(jnp.int32, shape, len(shape) - 1)


def half(value, slot):
    low_half = lanes(value.shape) < HEAD
    zero = jnp.zeros_like(value)
    return jnp.where(low_half, value, zero) if slot == 0 else jnp.where(low_half, zero, value)


def pair(first, second):
    return jnp.where(lanes(first.shape) < HEAD, first, second)


def swap(value):
    return pltpu.roll(value, HEAD, 1)


def rows_to_heads(rows, heads):
    for p in range(HEADS // 2):
        first = rows[0:64, p * 128 : p * 128 + 128]
        second = rows[64:128, p * 128 : p * 128 + 128]
        heads[2 * p] = pair(first, swap(second)).astype(BF16)
        heads[2 * p + 1] = pair(swap(first), second).astype(BF16)


def heads_to_rows(heads, rows, factor):
    for p in range(HEADS // 2):
        even = heads[2 * p].astype(F32) * factor
        odd = heads[2 * p + 1].astype(F32) * factor
        rows[0:64, p * 128 : p * 128 + 128] = pair(even, swap(odd)).astype(BF16)
        rows[64:128, p * 128 : p * 128 + 128] = pair(swap(even), odd).astype(BF16)


class Exchange:
    def __init__(self, spot, out, into, send, recv):
        self.spot, self.out, self.into, self.send, self.recv = spot, out, into, send, recv

    def copy(self, unit, step, source, target, peer):
        return pltpu.make_async_remote_copy(
            src_ref=self.out.at[unit, source],
            dst_ref=self.into.at[unit, target],
            send_sem=self.send.at[unit, step],
            recv_sem=self.recv.at[unit, step],
            device_id=(self.spot.y, peer),
            device_id_type=MESH,
        )

    def start(self, unit):
        me = self.spot.s

        def body(step, carry):
            peer = (me + step) % 16
            self.copy(unit, step, peer, me, peer).start()
            return carry

        lax.fori_loop(1, 16, body, 0)
        self.into[unit, me] = self.out[unit, me]

    def wait(self, unit):
        me = self.spot.s

        def body(step, carry):
            peer = (me + 16 - step) % 16
            self.copy(unit, step, peer, peer, peer).wait_recv()
            return carry

        lax.fori_loop(1, 16, body, 0)

    def finish(self, units):
        me = self.spot.s

        def body(step, carry):
            for unit in range(units):
                self.copy(unit, step, (me + step) % 16, me, (me + step) % 16).wait_send()
            return carry

        lax.fori_loop(1, 16, body, 0)


class Scatter:
    def __init__(self, spot, own, core_in, core_sum, x_in, x_sum, z_in, z_sum, y_in, send, recv):
        self.spot = spot
        self.own, self.core_in, self.core_sum, self.x_in = own, core_in, core_sum, x_in
        self.x_sum, self.z_in, self.z_sum, self.y_in = x_sum, z_in, z_sum, y_in
        self.send, self.recv = send, recv
        self.started = []

    def push(self, source, target, route, peer):
        copy = pltpu.make_async_remote_copy(
            src_ref=source,
            dst_ref=target,
            send_sem=self.send.at[route],
            recv_sem=self.recv.at[route],
            device_id=peer,
            device_id_type=MESH,
        )
        copy.start()
        self.started.append(copy)

    def first(self):
        p = self.spot
        self.push(self.own.at[:, :, :, 1 - p.c], self.core_in, 0, p.at(dc=1))

    def second(self):
        p = self.spot
        self.started[0].wait_recv()
        self.core_sum[...] = (self.own[:, :, :, p.c].astype(F32) + self.core_in[...].astype(F32)).astype(BF16)
        self.push(self.core_sum.at[:, :, 1 - p.x], self.x_in, 1, p.at(dx=1))

    def third(self):
        p = self.spot
        self.started[1].wait_recv()
        self.x_sum[...] = (self.core_sum[:, :, p.x].astype(F32) + self.x_in[...].astype(F32)).astype(BF16)
        for d in range(1, 4):
            self.push(self.x_sum.at[:, (p.z + d) % 4], self.z_in.at[d - 1], 1 + d, p.at(dz=d))

    def fourth(self, result):
        p = self.spot
        for d in range(1, 4):
            self.started[1 + d].wait_recv()
        total = self.x_sum[:, p.z].astype(F32)
        for d in range(3):
            total = total + self.z_in[d].astype(F32)
        self.z_sum[...] = total.astype(BF16)
        self.push(self.z_sum.at[1 - p.y], self.y_in, 5, p.at(dy=1))
        result[p.y] = self.z_sum[p.y].astype(F32)

    def fifth(self, result):
        self.started[5].wait_recv()
        result[1 - self.spot.y] = self.y_in[...].astype(F32)

    def finish(self):
        for copy in self.started:
            copy.wait_send()


def scatter_shapes(rows):
    return [
        pltpu.VMEM((2, 4, 2, 2, rows, 128), BF16),
        pltpu.VMEM((2, 4, 2, rows, 128), BF16),
        pltpu.VMEM((2, 4, 2, rows, 128), BF16),
        pltpu.VMEM((2, 4, rows, 128), BF16),
        pltpu.VMEM((2, 4, rows, 128), BF16),
        pltpu.VMEM((3, 2, rows, 128), BF16),
        pltpu.VMEM((2, rows, 128), BF16),
        pltpu.VMEM((rows, 128), BF16),
        pltpu.SemaphoreType.DMA((6,)),
        pltpu.SemaphoreType.DMA((6,)),
    ]


def layer_kernel(*refs):
    it = iter(refs)

    def take(count):
        return [next(it) for _ in range(count)]

    attn, fc1, fc2, low_rank, ff_rank, tok, cot, lengths = take(8)
    layer_out, input_grad, early_out, late_out = take(4)
    wide, tall, rank_all, ff_all = take(4)
    rank_in, rank_up, rank_x, vec, ff_low, bias = take(6)
    heads_out, heads_in = take(2)
    weights_low, weights_back = take(2)
    tmp, attended, stat, sum_one, scaled_one, normed, scaled_two, grad_second, grad_first = take(9)
    mixed, normed_low, out_low, branch_low, query_low, key_low, value_low = take(7)
    slope, act, grad_hidden, inner4 = take(4)
    early_refs, late_refs = take(10), take(10)
    own, send, recv, hsend, hrecv = take(5)

    spot = Spot()
    here = (spot.y, spot.z, spot.x, spot.c)
    parts = [wide.at[k] for k in range(8)] + [tall.at[k] for k in range(4)] + [rank_all, ff_all]
    sources = [attn.at[j] for j in range(4)]
    sources += [fc1.at[:, pl.ds(q * 1024, 1024)] for q in range(4)]
    sources += [fc2.at[:, pl.ds(q * 256, 256)] for q in range(4)] + [low_rank, ff_rank]
    placed = [pltpu.make_async_copy(sources[k], parts[k].at[here], own.at[k]) for k in ORDER]
    for copy in placed:
        copy.start()
    gather = Gather(spot, [parts[k] for k in ORDER], send, recv)
    swaps = Exchange(spot, heads_out, heads_in, hsend, hrecv)
    early = Scatter(spot, *early_refs)
    late = Scatter(spot, *late_refs)
    enter(spot)
    for copy in placed:
        copy.wait()

    lane = lanes((128, 128))
    row_slot = lax.broadcasted_iota(jnp.int32, (128, 128), 0) >= 64
    slot_lane = ((lane & 16) != 0) == row_slot
    kind4 = [slot_lane & ((lane >> 5) == j) for j in range(4)]
    kind_ff = [slot_lane & ((lane >> 5) == spot.y * 2 + k) for k in range(2)]

    def only(mask, value):
        return jnp.where(mask, value, jnp.zeros_like(value))

    def square(k, t):
        return wide[k, t // 2, pl.ds((t % 2) * 2, 2)].reshape(256, 1024)

    def columns(k, cols):
        return wide[k, :, :, :, :, :, cols].reshape(1024, 256)

    def tile(n, size=256):
        return pl.ds(pl.multiple_of(n * size, size), size)

    def unpack_rank():
        y_lanes = pl.ds(pl.multiple_of(spot.y * 128, 128), 128)
        up_lanes = pl.ds(pl.multiple_of(spot.y * 128 + 256, 128), 128)
        rank_in[...] = rank_all[:, :, :, :, :, y_lanes].reshape(1024, 128)
        rank_up[...] = rank_all[:, :, :, :, :, up_lanes].reshape(1024, 128)
        rank_x[...] = rank_all[:, :, :, :, :, 512:640].reshape(1024, 128)
        vec[...] = rank_all[:, :, :, :, :, 640:768].reshape(1024, 128).astype(F32).T[0:8]

    def unpack_ff():
        ff_low[...] = ff_all[:, :, :, :, 0:128, :].reshape(4096, 128)
        for o in range(32):
            y, z, x, c = o // 16, (o // 4) % 4, (o // 2) % 2, o % 2
            bias[:, o * 128 : o * 128 + 128] = ff_all[y, z, x, c, 128:136, :].astype(F32)

    def project_in(j):
        inner = only(kind4[j], inner4[...])

        def body(n, carry):
            cols = tile(n)
            value = dot(tok[...], columns(j, cols)) + dot_nt(inner, rank_up[cols, :])
            if j == 0:
                value = (value + vec[0:1, cols]) * 0.125
            if j == 2:
                value = value + vec[1:2, cols]
            tmp[:, cols] = value
            return carry

        lax.fori_loop(0, 4, body, 0)
        rows_to_heads(tmp, heads_out.at[j])
        swaps.start(j)

    def attention():
        for j in range(3):
            swaps.wait(j)
        keys = heads_in[1].reshape(1024, 128)
        values = heads_in[2].reshape(1024, 128)

        def body(t, carry):
            rows = tile(t)
            query = heads_in[0, pl.ds(t * 4, 4)].reshape(256, 128)
            results, stats = [], []
            for slot in range(2):
                scores = dot_nt(half(query, slot), keys)
                scores = jnp.where(lanes(scores.shape) < lengths[slot], scores, NEG_FILL)
                top = jnp.max(scores, axis=-1, keepdims=True)
                shifted = jnp.exp(scores - top)
                total = jnp.sum(shifted, axis=-1, keepdims=True)
                low = (shifted * (1.0 / total)).astype(BF16)
                weights_low[slot, rows, :] = low
                results.append(dot(low, values))
                stats.append(jnp.broadcast_to(top + jnp.log(total), (256, 128)))
            result = pair(results[0], results[1])
            attended[rows, :] = result
            heads_out[3, pl.ds(t * 4, 4)] = result.astype(BF16).reshape(4, 64, 128)
            stat[rows, :] = pair(stats[0], stats[1])
            return carry

        lax.fori_loop(0, 4, body, 0)
        swaps.start(3)

    def attention_turned():
        logsum = stat[...].T
        queries = heads_in[0].reshape(1024, 128)
        turned = [logsum[0:1], logsum[64:65]]

        def body(t, carry):
            rows = tile(t)
            keys = heads_in[1, pl.ds(t * 4, 4)].reshape(256, 128)
            for slot in range(2):
                scores = dot_nt(half(keys, slot), queries)
                weights = jnp.exp(scores - turned[slot])
                place = lax.broadcasted_iota(jnp.int32, weights.shape, 0) + t * 256
                weights = jnp.where(place < lengths[slot], weights, 0.0)
                weights_back[slot, rows, :] = weights.astype(BF16)
            return carry

        lax.fori_loop(0, 4, body, 0)

    def normalize(value):
        centered = value - jnp.mean(value, axis=-1, keepdims=True)
        spread = lax.rsqrt(jnp.mean(centered * centered, axis=-1, keepdims=True) + NORM_EPS)
        return centered * spread, spread

    def normalize_back(grad, scaled, spread):
        shift = jnp.mean(grad, axis=-1, keepdims=True)
        along = jnp.mean(grad * scaled, axis=-1, keepdims=True)
        return spread * (grad - shift - scaled * along)

    saved = {}

    def branch():
        swaps.wait(3)
        heads_to_rows(heads_in.at[3], mixed, 1.0)
        saved["o"] = only(kind4[3], dot(mixed[...], rank_in[...])).astype(BF16)

        def body(n, carry):
            cols = tile(n)
            value = dot(mixed[...], columns(3, cols)) + dot_nt(saved["o"], rank_up[cols, :])
            sum_one[:, cols] = tok[:, cols].astype(F32) + value + vec[2:3, cols]
            return carry

        lax.fori_loop(0, 4, body, 0)
        scaled, saved["spread_one"] = normalize(sum_one[...])
        scaled_one[...] = scaled
        value = scaled * vec[4:5] + vec[5:6]
        normed[...] = value
        normed_low[...] = value.astype(BF16)
        saved["hidden"] = only(kind_ff[0], dot(normed_low[...], rank_x[...])).astype(BF16)

    def expand(q):
        def body(n, carry):
            cols = tile(n)
            wide_cols = tile(q * 4 + n)
            value = dot(normed_low[...], columns(4 + q, cols))
            value = value + dot_nt(saved["hidden"], ff_low[wide_cols, :]) + bias[0:1, wide_cols]
            share = 0.5 * (1.0 + lax.erf(value * math.sqrt(0.5)))
            act[:, wide_cols] = (value * share).astype(BF16)
            bell = jnp.exp(-0.5 * value * value) * (1.0 / math.sqrt(2.0 * math.pi))
            slope[:, wide_cols] = share + value * bell
            return carry

        lax.fori_loop(0, 4, body, 0)

    def contract(q):
        if q == 0:
            saved["out"] = only(kind_ff[1], dot(act[...], ff_low[...])).astype(BF16)
        cols = pl.ds(q * 256, 256)
        value = dot(act[...], tall[q].reshape(4096, 256)) + dot_nt(saved["out"], rank_x[cols, :])
        tmp[:, cols] = normed[:, cols] + value + vec[3:4, cols]

    def outer():
        rows = lax.broadcasted_iota(jnp.int32, (128, 1), 0)
        place = spot.s * 64 + (rows & 63)
        limit = jnp.where(rows < 64, lengths[0], lengths[1])
        live = (place < limit).astype(F32)
        scaled, spread = normalize(tmp[...])
        layer_out[...] = (live * (scaled * vec[6:7] + vec[7:8])).astype(BF16)
        grad = normalize_back(live * cot[...].astype(F32) * vec[6:7], scaled, spread)
        grad_second[...] = grad
        out_low[...] = grad.astype(BF16)
        saved["g_out"] = only(kind_ff[1], dot(out_low[...], rank_x[...])).astype(BF16)

    def hidden_back():
        def body(t, carry):
            rows = tile(t, 512)
            value = dot_nt(saved["g_out"], ff_low[rows, :])
            for q in range(4):
                piece = tall[q, t // 4, t % 4].reshape(512, 256)
                value = value + dot_nt(out_low[:, q * 256 : q * 256 + 256], piece)
            grad_hidden[:, rows] = (value * slope[:, rows]).astype(BF16)
            return carry

        lax.fori_loop(0, 8, body, 0)
        saved["g_hidden"] = only(kind_ff[0], dot(grad_hidden[...], ff_low[...])).astype(BF16)

    def normed_back():
        def body(t, carry):
            rows = tile(t)
            value = dot_nt(saved["g_hidden"], rank_x[rows, :]) + grad_second[:, rows]
            for q in range(4):
                value = value + dot_nt(grad_hidden[:, q * 1024 : q * 1024 + 1024], square(4 + q, t))
            tmp[:, rows] = value
            return carry

        lax.fori_loop(0, 4, body, 0)
        grad = normalize_back(tmp[...] * vec[4:5], scaled_one[...], saved["spread_one"])
        grad_first[...] = grad
        branch_low[...] = grad.astype(BF16)
        saved["g_o"] = only(kind4[3], dot(branch_low[...], rank_up[...])).astype(BF16)

    def mixed_back():
        def body(t, carry):
            rows = tile(t)
            tmp[:, rows] = dot_nt(branch_low[...], square(3, t)) + dot_nt(saved["g_o"], rank_in[rows, :])
            return carry

        lax.fori_loop(0, 4, body, 0)
        rows_to_heads(tmp, heads_out.at[4])
        swaps.start(4)

    def early_grads():
        own_grads = early.own
        value = dot_tn(normed_low[...], saved["g_hidden"]) + dot_tn(out_low[...], saved["out"])
        own_grads[:, :, :, :, 0:32, :] = value.astype(BF16).reshape(2, 4, 2, 2, 32, 128)
        for y in range(2):
            for z in range(4):
                cols = slice((y * 4 + z) * 512, (y * 4 + z) * 512 + 512)
                value = dot_tn(grad_hidden[:, cols], saved["hidden"]) + dot_tn(act[:, cols], saved["g_out"])
                value = value.reshape(4, 128, 128)
                for o in range(4):
                    packed = value[o, 0:64] + swap(value[o, 64:128])
                    own_grads[y, z, o // 2, o % 2, 32:96, :] = packed.astype(BF16)

    def attention_back():
        swaps.wait(4)
        keys = heads_in[1].reshape(1024, 128)
        values = heads_in[2].reshape(1024, 128)
        queries = heads_in[0].reshape(1024, 128)
        grads = heads_in[4].reshape(1024, 128)
        product = grads.astype(F32) * attended[...]
        deltas = [jnp.sum(half(product, slot), axis=-1, keepdims=True) for slot in range(2)]
        stat[...] = pair(*[jnp.broadcast_to(delta, (1024, 128)) for delta in deltas])
        turned = stat[...].T
        turned = [turned[0:1], turned[64:65]]

        def key_side(t, carry):
            rows = tile(t)
            value_block = heads_in[2, pl.ds(t * 4, 4)].reshape(256, 128)
            key_parts, value_parts = [], []
            for slot in range(2):
                weights = weights_back[slot, rows, :]
                grad_probs = dot_nt(half(value_block, slot), grads)
                grad_scores = (weights.astype(F32) * (grad_probs - turned[slot])).astype(BF16)
                key_parts.append(dot(grad_scores, queries))
                value_parts.append(dot(weights, grads))
            heads_out[6, pl.ds(t * 4, 4)] = pair(*key_parts).astype(BF16).reshape(4, 64, 128)
            heads_out[7, pl.ds(t * 4, 4)] = pair(*value_parts).astype(BF16).reshape(4, 64, 128)
            return carry

        lax.fori_loop(0, 4, key_side, 0)
        swaps.start(6)
        swaps.start(7)

        def query_side_block(t, carry):
            rows = tile(t)
            grad_block = heads_in[4, pl.ds(t * 4, 4)].reshape(256, 128)
            delta_block = stat[rows, :]
            query_parts = []
            for slot in range(2):
                grad_probs = dot_nt(half(grad_block, slot), values)
                delta = delta_block[:, 64 * slot : 64 * slot + 1]
                weights = weights_low[slot, rows, :].astype(F32)
                grad_scores = (weights * (grad_probs - delta)).astype(BF16)
                query_parts.append(dot(grad_scores, keys))
            heads_out[5, pl.ds(t * 4, 4)] = pair(*query_parts).astype(BF16).reshape(4, 64, 128)
            return carry

        lax.fori_loop(0, 4, query_side_block, 0)
        swaps.start(5)

    def inputs_back():
        swaps.wait(6)
        heads_to_rows(heads_in.at[6], key_low, 1.0)
        swaps.wait(7)
        heads_to_rows(heads_in.at[7], value_low, 1.0)
        swaps.wait(5)
        heads_to_rows(heads_in.at[5], query_low, 0.125)
        grads = (query_low, key_low, value_low)
        inner = jnp.zeros((128, 128), F32)
        for j in range(3):
            inner = jnp.where(kind4[j], dot(grads[j][...], rank_up[...]), inner)
        saved["g_in"] = inner.astype(BF16)
        value = dot_tn(tok[...], saved["g_in"]) + dot_tn(mixed[...], saved["g_o"])
        late.own[:, :, :, :, 0:32, :] = value.astype(BF16).reshape(2, 4, 2, 2, 32, 128)
        value = dot_tn(branch_low[...], saved["o"])
        for j in range(3):
            value = value + dot_tn(grads[j][...], only(kind4[j], inner4[...]))
        late.own[:, :, :, :, 32:64, :] = value.astype(BF16).reshape(2, 4, 2, 2, 32, 128)

    def tokens_back(t):
        rows = pl.ds(t * 256, 256)
        value = dot_nt(saved["g_in"], rank_in[rows, :]) + grad_first[:, rows]
        for j, grad in enumerate((query_low, key_low, value_low)):
            value = value + dot_nt(grad[...], square(j, t))
        input_grad[:, rows] = value.astype(BF16)

    for t in range(CHUNKS + 4):
        gather.step(t)
        if t == 5:
            unpack_rank()
            inner4[...] = dot(tok[...], rank_in[...]).astype(BF16)
        if 5 <= t <= 7:
            project_in(t - 5)
        if t == 9:
            unpack_ff()
            attention()
        if t == 10:
            attention_turned()
        if t == 11:
            branch()
            expand(0)
            expand(1)
        if 12 <= t <= 13:
            expand(t - 10)
        if t >= 14:
            contract(t - 14)
    outer()
    hidden_back()
    normed_back()
    mixed_back()
    early_grads()
    early.first()
    early.second()
    attention_back()
    early.third()
    early.fourth(early_out)
    inputs_back()
    late.first()
    tokens_back(0)
    late.second()
    tokens_back(1)
    tokens_back(2)
    late.third()
    tokens_back(3)
    late.fourth(late_out)
    early.fifth(early_out)
    late.fifth(late_out)
    gather.finish()
    swaps.finish(8)
    early.finish()
    late.finish()


def layer(attn, fc1, fc2, low_rank, ff_rank, tok, cot, lengths):
    lead = (2, 4, 2, 2)
    anywhere = pl.BlockSpec(memory_space=pl.ANY)
    near = pl.BlockSpec(memory_space=pltpu.VMEM)
    scalar = pl.BlockSpec(memory_space=pltpu.SMEM)

    def buffer(*shape, dtype=BF16):
        return pltpu.VMEM(shape, dtype)

    scratch = [
        buffer(8, *lead, 32, 1024),
        buffer(4, *lead, 128, 256),
        buffer(*lead, *low_rank.shape),
        buffer(*lead, *ff_rank.shape),
    ]
    scratch += [buffer(1024, 128)] * 3 + [buffer(8, 1024, dtype=F32), buffer(4096, 128)]
    scratch += [buffer(8, 4096, dtype=F32)]
    scratch += [buffer(8, 16, 64, 128)] * 2
    scratch += [buffer(2, 1024, 1024)] * 2
    scratch += [buffer(128, 1024, dtype=F32)] + [buffer(1024, 128, dtype=F32)] * 2
    scratch += [buffer(128, 1024, dtype=F32)] * 6
    scratch += [buffer(128, 1024)] * 7
    scratch += [buffer(128, 4096, dtype=F32), buffer(128, 4096), buffer(128, 4096), buffer(128, 128)]
    scratch += scatter_shapes(EARLY) + scatter_shapes(LATE)
    scratch += [pltpu.SemaphoreType.DMA((CHUNKS,))]
    scratch += [pltpu.SemaphoreType.DMA((CHUNKS, ROUTES))] * 2
    scratch += [pltpu.SemaphoreType.DMA((8, 16))] * 2
    return pl.pallas_call(
        layer_kernel,
        out_shape=[
            jax.ShapeDtypeStruct(tok.shape, BF16),
            jax.ShapeDtypeStruct(tok.shape, BF16),
            jax.ShapeDtypeStruct((2, EARLY, 128), F32),
            jax.ShapeDtypeStruct((2, LATE, 128), F32),
        ],
        in_specs=[anywhere] * 5 + [near] * 2 + [scalar],
        out_specs=[near] * 4,
        scratch_shapes=scratch,
        compiler_params=pltpu.CompilerParams(
            collective_id=0, has_side_effects=True, vmem_limit_bytes=63 * 2**20
        ),
        name="layer",
    )(attn, fc1, fc2, low_rank, ff_rank, tok, cot, lengths)


def fast_device(
    tokens,
    cotangent,
    lengths,
    adapter_ids,
    attn_weight,
    fc1_weight,
    fc2_weight,
    vectors,
    fc1_bias,
    adapter_down,
    adapter_up,
    ff_adapters,
):
    rows, width = adapter_down.shape[0], tokens.shape[2]
    ff_rows = ff_adapters.shape[0]
    ids = lax.all_gather(adapter_ids, "fsdp", axis=0, tiled=True)
    onehot = ids[:, None] == jnp.arange(ADAPTERS)[None, :]

    def pick(table):
        picked = jnp.einsum("si,dikr->dskr", onehot.astype(BF16), table, preferred_element_type=F32)
        picked = picked.astype(BF16).reshape(table.shape[0], 2, 2, table.shape[2], 16)
        return picked.transpose(0, 1, 3, 2, 4)

    down, up, ff_part = pick(adapter_down), pick(adapter_up), pick(ff_adapters)
    cross = jnp.stack([down[:, :, 4], up[:, :, 4]], axis=2)
    low_rank = jnp.concatenate(
        [
            down[:, :, :4].reshape(rows, 256),
            up[:, :, :4].reshape(rows, 256),
            cross.reshape(rows, 128),
            jnp.pad(vectors, ((0, 0), (0, 120))),
        ],
        axis=1,
    )
    bias_rows = jnp.broadcast_to(fc1_bias[None], (16, ff_rows))
    ff_rank = jnp.concatenate([ff_part.reshape(ff_rows, 128), bias_rows], axis=0)
    layer_out, input_grad, early, late = layer(
        attn_weight.transpose(1, 0, 2),
        fc1_weight,
        fc2_weight,
        low_rank,
        ff_rank,
        tokens.reshape(-1, width),
        cotangent.reshape(-1, width),
        lengths,
    )
    picks = onehot.astype(F32).reshape(2, 2, ADAPTERS)
    four = late.reshape(2, 2, rows, 4, 2, 16)
    cross = early[:, :rows].reshape(2, rows, 2, 64)
    cross = jnp.stack([cross[0, :, 0], cross[1, :, 1]]).reshape(2, rows, 2, 2, 16)
    packed = early[:, rows:]
    ff_first = jnp.concatenate([packed[0, :, :64], packed[0, :, 64:]], axis=0)
    ff_second = jnp.concatenate([packed[1, :, 64:], packed[1, :, :64]], axis=0)
    ff_terms = jnp.stack([ff_first, ff_second]).reshape(2, ff_rows, 2, 2, 16)

    def spread(terms):
        return jnp.einsum("ysi,ydksr->dikr", picks, terms, precision=lax.Precision.HIGHEST)

    return (
        layer_out.reshape(tokens.shape),
        input_grad.reshape(tokens.shape),
        spread(jnp.concatenate([four[:, 0], cross[:, :, 0:1]], axis=2)),
        spread(jnp.concatenate([four[:, 1], cross[:, :, 1:2]], axis=2)),
        spread(ff_terms),
    )


def solution(mesh):
    in_specs = (
        P("fsdp", "seq", None),
        P("fsdp", "seq", None),
        P("fsdp"),
        P("fsdp"),
        P(("fsdp", "seq"), None, None),
        P(("fsdp", "seq"), None),
        P(("fsdp", "seq"), None),
        P(("fsdp", "seq"), None),
        P(("fsdp", "seq")),
        P(("fsdp", "seq"), None, None, None),
        P(("fsdp", "seq"), None, None, None),
        P(("fsdp", "seq"), None, None, None),
    )
    out_specs = (
        P("fsdp", "seq", None),
        P("fsdp", "seq", None),
        P(("fsdp", "seq"), None, None, None),
        P(("fsdp", "seq"), None, None, None),
        P(("fsdp", "seq"), None, None, None),
    )
    fast = mesh.shape["fsdp"] == 2 and mesh.shape["seq"] == HEADS
    return jax.shard_map(
        fast_device if fast else on_device, mesh=mesh, in_specs=in_specs, out_specs=out_specs, check_vma=False
    )
```

```python
from functools import partial
import math

import jax
import jax.numpy as jnp
from jax import lax
from jax.experimental import pallas as pl
from jax.experimental.pallas import tpu as pltpu
from jax.sharding import PartitionSpec as P

HEADS = 16
HEAD = 64
ADAPTERS = 8


NEG_FILL = -1e30
NORM_EPS = 1e-05


def split_heads(values_in):
    return values_in.reshape(values_in.shape[:-1] + (HEADS, HEAD))


def norm_rows(value, gain, shift):
    centered = value - jnp.mean(value, axis=-1, keepdims=True)
    scaled = centered * lax.rsqrt(jnp.mean(centered * centered, axis=-1, keepdims=True) + NORM_EPS)
    return scaled * gain + shift


def gelu_exact(value):
    return jax.nn.gelu(value, approximate=False)


def choose(onehot, table):
    return jnp.einsum("si,dikr->sdkr", onehot, table, preferred_element_type=jnp.float32).astype(
        jnp.bfloat16
    )


def unpack(gathered, onehot):
    attn_all, fc1_all, fc2_all, vector_all, bias_ff, down_all, up_all, ff_all = gathered
    return (
        attn_all,
        fc1_all,
        fc2_all,
        vector_all.astype(jnp.float32),
        bias_ff.astype(jnp.float32),
        choose(onehot, down_all),
        choose(onehot, up_all),
        choose(onehot, ff_all),
    )


def project(inputs, weight, down_table, up_table):
    frozen_part = jnp.einsum("spd,de->spe", inputs, weight, preferred_element_type=jnp.float32)
    inner_low = jnp.einsum(
        "spd,sdr->spr", inputs, down_table, preferred_element_type=jnp.float32
    ).astype(jnp.bfloat16)
    return (
        frozen_part
        + jnp.einsum("spr,ser->spe", inner_low, up_table, preferred_element_type=jnp.float32),
        inner_low,
    )


def project_back(inputs, inner_low, grad_out, weight, down_table, up_table):
    grad_inner = jnp.einsum(
        "spe,ser->spr", grad_out, up_table, preferred_element_type=jnp.float32
    ).astype(jnp.bfloat16)
    grad_in = jnp.einsum("spe,de->spd", grad_out, weight, preferred_element_type=jnp.float32)
    grad_in = grad_in + jnp.einsum(
        "spr,sdr->spd", grad_inner, down_table, preferred_element_type=jnp.float32
    )
    grad_up = jnp.einsum("spe,spr->ser", grad_out, inner_low, preferred_element_type=jnp.float32)
    grad_down = jnp.einsum("spd,spr->sdr", inputs, grad_inner, preferred_element_type=jnp.float32)
    return (grad_in, grad_down, grad_up)


def block_scores(query_heads, key_block, key_start, lengths):
    block_rows = key_block.shape[1]
    scores = jnp.einsum(
        "sqhd,skhd->shqk", query_heads, split_heads(key_block), preferred_element_type=jnp.float32
    )
    valid_keys = (key_start + jnp.arange(block_rows))[None, :] < lengths[:, None]
    return jnp.where(valid_keys[:, None, None, :], scores, NEG_FILL)


def score_grads(scores, logsum, row_delta, grad_heads, value_heads):
    probs = jnp.exp(scores - logsum[..., None])
    grad_probs = jnp.einsum(
        "sqhd,skhd->shqk", grad_heads, value_heads, preferred_element_type=jnp.float32
    )
    grad_scores = (probs * (grad_probs - row_delta[..., None])).astype(jnp.bfloat16)
    return (grad_scores, probs.astype(jnp.bfloat16))


def attend(query, all_keys, all_values, lengths):
    seq_span = all_keys.shape[1]
    block_rows = math.gcd(seq_span, 512)
    blocks = seq_span // block_rows
    query_heads = split_heads(query)
    slot_count, query_rows = (query.shape[0], query.shape[1])
    stats_shape = (slot_count, HEADS, query_rows)

    def stats_step(running, step_index):
        row_top, row_total = running
        offset = step_index * block_rows
        scores = block_scores(
            query_heads, lax.dynamic_slice_in_dim(all_keys, offset, block_rows, 1), offset, lengths
        )
        new_top = jnp.maximum(row_top, jnp.max(scores, axis=-1))
        row_total = row_total * jnp.exp(row_top - new_top) + jnp.sum(
            jnp.exp(scores - new_top[..., None]), axis=-1
        )
        return ((new_top, row_total), None)

    start_top = jnp.full(stats_shape, NEG_FILL, jnp.float32)
    (row_top, row_total), _ = lax.scan(
        stats_step, (start_top, jnp.zeros(stats_shape, jnp.float32)), jnp.arange(blocks)
    )
    logsum = row_top + jnp.log(row_total)

    def mix_step(running, step_index):
        offset = step_index * block_rows
        scores = block_scores(
            query_heads, lax.dynamic_slice_in_dim(all_keys, offset, block_rows, 1), offset, lengths
        )
        weights_low = jnp.exp(scores - logsum[..., None]).astype(jnp.bfloat16)
        value_heads = split_heads(lax.dynamic_slice_in_dim(all_values, offset, block_rows, 1))
        return (
            running
            + jnp.einsum(
                "shqk,skhd->sqhd", weights_low, value_heads, preferred_element_type=jnp.float32
            ),
            None,
        )

    mixed_heads, _ = lax.scan(
        mix_step, jnp.zeros(query_heads.shape, jnp.float32), jnp.arange(blocks)
    )
    return (mixed_heads.reshape(query.shape), logsum)


def query_side(query, all_keys, all_values, grad_low, logsum, row_delta, lengths):
    seq_span = all_keys.shape[1]
    block_rows = math.gcd(seq_span, 512)
    blocks = seq_span // block_rows
    query_heads = split_heads(query)
    grad_heads = split_heads(grad_low)
    slot_count = query.shape[0]
    width = query.shape[2]

    def step(running, step_index):
        offset = step_index * block_rows
        key_block = lax.dynamic_slice_in_dim(all_keys, offset, block_rows, 1)
        value_block = lax.dynamic_slice_in_dim(all_values, offset, block_rows, 1)
        scores = block_scores(query_heads, key_block, offset, lengths)
        grad_scores, weights_low = score_grads(
            scores, logsum, row_delta, grad_heads, split_heads(value_block)
        )
        grad_acc = running[0] + jnp.einsum(
            "shqk,skhd->sqhd",
            grad_scores,
            split_heads(key_block),
            preferred_element_type=jnp.float32,
        )
        key_part = jnp.einsum(
            "shqk,sqhd->skhd", grad_scores, query_heads, preferred_element_type=jnp.float32
        ).reshape(slot_count, block_rows, width)
        value_part = jnp.einsum(
            "shqk,sqhd->skhd", weights_low, grad_heads, preferred_element_type=jnp.float32
        ).reshape(slot_count, block_rows, width)
        key_buffer = lax.dynamic_update_slice_in_dim(running[1], key_part, offset, 1)
        value_buffer = lax.dynamic_update_slice_in_dim(running[2], value_part, offset, 1)
        return ((grad_acc, key_buffer, value_buffer), None)

    start = (jnp.zeros(query_heads.shape, jnp.float32),)
    empty = jnp.zeros((slot_count, seq_span, width), jnp.float32)
    start = start + (empty, empty)
    result, _ = lax.scan(step, start, jnp.arange(blocks))
    return (result[0].reshape(query.shape), result[1:])


def sum_by_adapter(picks, terms):
    return jnp.einsum("si,sdkr->dikr", picks, terms, precision=lax.Precision.HIGHEST)


def on_device(
    tokens,
    cotangent,
    lengths,
    adapter_ids,
    attn_weight,
    fc1_weight,
    fc2_weight,
    vectors,
    fc1_bias,
    adapter_down,
    adapter_up,
    ff_adapters,
):
    slot_count, slot_rows, width = tokens.shape
    row_start = lax.axis_index("seq") * slot_rows
    positions = row_start + jnp.arange(slot_rows)
    live_rows = (positions[None, :] < lengths[:, None]).astype(jnp.float32)[..., None]
    matches = adapter_ids[:, None] == jnp.arange(ADAPTERS)[None, :]
    onehot_low = matches.astype(jnp.bfloat16)
    onehot_full = matches.astype(jnp.float32)
    gathered = (
        lax.all_gather(attn_weight, ("fsdp", "seq"), axis=0, tiled=True),
        lax.all_gather(fc1_weight, ("fsdp", "seq"), axis=0, tiled=True),
        lax.all_gather(fc2_weight, ("fsdp", "seq"), axis=0, tiled=True),
        lax.all_gather(vectors, ("fsdp", "seq"), axis=0, tiled=True),
        lax.all_gather(fc1_bias, ("fsdp", "seq"), axis=0, tiled=True),
        lax.all_gather(adapter_down, ("fsdp", "seq"), axis=0, tiled=True),
        lax.all_gather(adapter_up, ("fsdp", "seq"), axis=0, tiled=True),
        lax.all_gather(ff_adapters, ("fsdp", "seq"), axis=0, tiled=True),
    )
    attn_all, fc1_all, fc2_all, vector_cols, bias_ff, down_pick, up_pick, ff_pick = unpack(
        gathered, onehot_low
    )
    query_pre, inner_query = project(
        tokens, attn_all[:, 0, :], down_pick[:, :, 0], up_pick[:, :, 0]
    )
    query = ((query_pre + vector_cols[:, 0]) * 0.125).astype(jnp.bfloat16)
    key_pre, inner_key = project(tokens, attn_all[:, 1, :], down_pick[:, :, 1], up_pick[:, :, 1])
    keys = key_pre.astype(jnp.bfloat16)
    value_pre, inner_value = project(
        tokens, attn_all[:, 2, :], down_pick[:, :, 2], up_pick[:, :, 2]
    )
    values = (value_pre + vector_cols[:, 1]).astype(jnp.bfloat16)
    all_keys, all_values = (
        lax.all_gather(keys, "seq", axis=1, tiled=True),
        lax.all_gather(values, "seq", axis=1, tiled=True),
    )
    attended, logsum = attend(query, all_keys, all_values, lengths)
    mixed = attended.astype(jnp.bfloat16)
    branch_pre, inner_branch = project(
        mixed, attn_all[:, 3, :], down_pick[:, :, 3], up_pick[:, :, 3]
    )
    first_sum = tokens.astype(jnp.float32) + branch_pre + vector_cols[:, 2]
    normed, first_back = jax.vjp(
        partial(norm_rows, gain=vector_cols[:, 4], shift=vector_cols[:, 5]), first_sum
    )
    normed_low = normed.astype(jnp.bfloat16)
    hidden_pre, inner_hidden = project(normed_low, fc1_all, down_pick[:, :, 4], ff_pick[:, :, 0])
    activated, gelu_back = jax.vjp(gelu_exact, hidden_pre + bias_ff)
    activated_low = activated.astype(jnp.bfloat16)
    out_pre, inner_out = project(activated_low, fc2_all, ff_pick[:, :, 1], up_pick[:, :, 4])
    second = normed + out_pre + vector_cols[:, 3]
    final, second_back = jax.vjp(
        partial(norm_rows, gain=vector_cols[:, 6], shift=vector_cols[:, 7]), second
    )
    layer_out = (final * live_rows).astype(jnp.bfloat16)
    regathered = (
        lax.all_gather(attn_weight, ("fsdp", "seq"), axis=0, tiled=True),
        lax.all_gather(fc1_weight, ("fsdp", "seq"), axis=0, tiled=True),
        lax.all_gather(fc2_weight, ("fsdp", "seq"), axis=0, tiled=True),
        lax.all_gather(vectors, ("fsdp", "seq"), axis=0, tiled=True),
        lax.all_gather(fc1_bias, ("fsdp", "seq"), axis=0, tiled=True),
        lax.all_gather(adapter_down, ("fsdp", "seq"), axis=0, tiled=True),
        lax.all_gather(adapter_up, ("fsdp", "seq"), axis=0, tiled=True),
        lax.all_gather(ff_adapters, ("fsdp", "seq"), axis=0, tiled=True),
    )
    attn_all, fc1_all, fc2_all, vector_cols, bias_ff, down_pick, up_pick, ff_pick = unpack(
        regathered, onehot_low
    )
    grad_final = cotangent.astype(jnp.float32) * live_rows
    (grad_second,) = second_back(grad_final)
    grad_out_low = grad_second.astype(jnp.bfloat16)
    grad_activated, down_of_fc2, up_of_fc2 = project_back(
        activated_low, inner_out, grad_out_low, fc2_all, ff_pick[:, :, 1], up_pick[:, :, 4]
    )
    (grad_hidden,) = gelu_back(grad_activated)
    grad_hidden_low = grad_hidden.astype(jnp.bfloat16)
    grad_normed, down_of_fc1, up_of_fc1 = project_back(
        normed_low, inner_hidden, grad_hidden_low, fc1_all, down_pick[:, :, 4], ff_pick[:, :, 0]
    )
    (grad_first,) = first_back(grad_normed + grad_second)
    grad_branch_low = grad_first.astype(jnp.bfloat16)
    grad_mixed, down_of_out, up_of_out = project_back(
        mixed,
        inner_branch,
        grad_branch_low,
        attn_all[:, 3, :],
        down_pick[:, :, 3],
        up_pick[:, :, 3],
    )
    grad_mixed_low = grad_mixed.astype(jnp.bfloat16)
    row_delta = jnp.einsum(
        "sqhd,sqhd->shq", split_heads(grad_mixed_low.astype(jnp.float32)), split_heads(attended)
    )
    grad_query, parts = query_side(
        query, all_keys, all_values, grad_mixed_low, logsum, row_delta, lengths
    )
    grad_keys, grad_values = (
        lax.psum_scatter(
            parts[0].astype(jnp.bfloat16), "seq", scatter_dimension=1, tiled=True
        ).astype(jnp.float32),
        lax.psum_scatter(
            parts[1].astype(jnp.bfloat16), "seq", scatter_dimension=1, tiled=True
        ).astype(jnp.float32),
    )
    grad_query_low = grad_query.astype(jnp.bfloat16) * 0.125
    grad_keys_low = grad_keys.astype(jnp.bfloat16)
    grad_values_low = grad_values.astype(jnp.bfloat16)
    grad_from_query, down_of_query, up_of_query = project_back(
        tokens, inner_query, grad_query_low, attn_all[:, 0, :], down_pick[:, :, 0], up_pick[:, :, 0]
    )
    grad_from_key, down_of_key, up_of_key = project_back(
        tokens, inner_key, grad_keys_low, attn_all[:, 1, :], down_pick[:, :, 1], up_pick[:, :, 1]
    )
    grad_from_value, down_of_value, up_of_value = project_back(
        tokens,
        inner_value,
        grad_values_low,
        attn_all[:, 2, :],
        down_pick[:, :, 2],
        up_pick[:, :, 2],
    )
    input_grad = (grad_from_query + grad_from_key + grad_from_value + grad_first).astype(
        jnp.bfloat16
    )
    down_terms = jnp.stack(
        (down_of_query, down_of_key, down_of_value, down_of_out, down_of_fc1), axis=2
    )
    up_terms = jnp.stack((up_of_query, up_of_key, up_of_value, up_of_out, up_of_fc2), axis=2)
    ff_terms = jnp.stack((up_of_fc1, down_of_fc2), axis=2)
    down_table = sum_by_adapter(onehot_full, down_terms)
    up_table = sum_by_adapter(onehot_full, up_terms)
    ff_table = sum_by_adapter(onehot_full, ff_terms)
    down_grad, up_grad, ff_grad = (
        lax.psum_scatter(down_table, ("fsdp", "seq"), scatter_dimension=0, tiled=True),
        lax.psum_scatter(up_table, ("fsdp", "seq"), scatter_dimension=0, tiled=True),
        lax.psum_scatter(ff_table, ("fsdp", "seq"), scatter_dimension=0, tiled=True),
    )
    return (layer_out, input_grad, down_grad, up_grad, ff_grad)


MESH = pl.DeviceIdType.MESH
CHUNKS = 26
ROUTES = 11
ALL2, ALL4 = pl.ds(0, 2), pl.ds(0, 4)


class Spot:
    def __init__(self):
        self.y = lax.axis_index("fsdp")
        self.s = lax.axis_index("seq")
        self.z = self.s // 4
        self.x = (self.s // 2) % 2
        self.c = self.s % 2

    def at(self, dy=0, dz=0, dx=0, dc=0):
        y = (self.y + dy) % 2
        z = (self.z + dz) % 4
        x = (self.x + dx) % 2
        c = (self.c + dc) % 2
        return (y, (z * 2 + x) * 2 + c)


def enter(spot):
    barrier = pltpu.get_barrier_semaphore()
    for step in range(1, 16):
        peer = (spot.y, (spot.s + step) % 16)
        pl.semaphore_signal(barrier, inc=1, device_id=peer, device_id_type=MESH)
    pl.semaphore_signal(barrier, inc=1, device_id=spot.at(dy=1), device_id_type=MESH)
    pl.semaphore_wait(barrier, 16)


class Gather:
    def __init__(self, spot, parts, ways, others, send, recv):
        self.spot, self.parts, self.ways, self.others = spot, parts, ways, others
        self.send, self.recv = send, recv
        self.started = []

    def block(self, k, dy=0, dz=0, dx=0, dc=0):
        p = self.spot
        places = ((p.y, dy, 2), (p.z, dz, 4), (p.x, dx, 2), (p.c, dc, 2))
        return self.parts[k].at[tuple((place + d) % n if isinstance(d, int) else d for place, d, n in places)]

    def copy(self, source, target, k, route, peer):
        return pltpu.make_async_remote_copy(
            src_ref=source,
            dst_ref=target,
            send_sem=self.send.at[k, route],
            recv_sem=self.recv.at[k, route],
            device_id=peer,
            device_id_type=MESH,
        )

    def push(self, ref, k, route, source=None, **hop):
        copy = self.copy(ref if source is None else source, ref, k, route, self.spot.at(**hop))
        copy.start()
        self.started.append(copy)

    def arrive(self, ref, k, route):
        self.copy(ref, ref, k, route, self.spot.at(dc=1)).wait_recv()

    def first(self, k):
        if self.ways[k] == "z":
            for d in range(1, 4):
                self.push(self.block(k), k, d - 1, dz=d)
        else:
            self.push(self.block(k), k, 0, self.others.get(k), **{"d" + self.ways[k]: 1})

    def second(self, k):
        if self.ways[k] == "z":
            for d in range(1, 4):
                self.arrive(self.block(k, dz=4 - d), k, d - 1)
            line = self.block(k, dz=ALL4)
            self.push(line, k, 3, dx=1)
            self.push(line, k, 4, dy=1)
            self.push(line, k, 5, dc=1)
        else:
            self.arrive(self.block(k, **{"d" + self.ways[k]: 1}), k, 0)
            for d in range(1, 4):
                self.push(self.block(k, **{"d" + self.ways[k]: ALL2}), k, d, dz=d)

    def third(self, k):
        if self.ways[k] == "z":
            self.arrive(self.block(k, dz=ALL4, dx=1), k, 3)
            self.push(self.block(k, dz=pl.ds(0, 2), dx=1), k, 6, dy=1)
            self.arrive(self.block(k, dz=ALL4, dy=1), k, 4)
            self.push(self.block(k, dz=pl.ds(2, 2), dy=1), k, 7, dx=1)
            self.push(self.block(k, dz=ALL4, dx=1), k, 8, dc=1)
            self.push(self.block(k, dz=ALL4, dy=1), k, 9, dc=1)
        else:
            near, far = "d" + self.ways[k], "dy" if self.ways[k] == "x" else "dx"
            for d in range(1, 4):
                self.arrive(self.block(k, **{near: ALL2, "dz": 4 - d}), k, d)
            plane = self.block(k, **{near: ALL2, "dz": ALL4})
            self.push(plane, k, 4, **{far: 1})
            self.push(plane, k, 5, dc=1)

    def fourth(self, k):
        if self.ways[k] == "z":
            self.arrive(self.block(k, dz=pl.ds(0, 2), dx=1, dy=1), k, 6)
            self.arrive(self.block(k, dz=pl.ds(2, 2), dx=1, dy=1), k, 7)
            self.push(self.block(k, dz=ALL4, dx=1, dy=1), k, 10, dc=1)
        else:
            near, far = "d" + self.ways[k], "dy" if self.ways[k] == "x" else "dx"
            plane = self.block(k, **{near: ALL2, "dz": ALL4, far: 1})
            self.arrive(plane, k, 4)
            self.push(plane, k, 6, dc=1)

    def ready(self, k):
        if self.ways[k] == "z":
            for route, dx, dy in ((5, 0, 0), (8, 1, 0), (9, 0, 1), (10, 1, 1)):
                self.arrive(self.block(k, dz=ALL4, dx=dx, dy=dy, dc=1), k, route)
        else:
            near, far = "d" + self.ways[k], "dy" if self.ways[k] == "x" else "dx"
            for route in range(2):
                self.arrive(self.block(k, **{near: ALL2, "dz": ALL4, far: route, "dc": 1}), k, 5 + route)

    def step(self, t):
        for late, move in enumerate((self.first, self.second, self.third, self.fourth, self.ready)):
            if 0 <= t - late < len(self.parts):
                move(t - late)

    def finish(self):
        for copy in self.started:
            copy.wait_send()


F32, BF16 = jnp.float32, jnp.bfloat16
ORDER = (0, 1, 24, 25) + tuple(range(2, 24))
WAYS = "zzyyzzzzzzzzzzzzzzzzzzzzzz"
EARLY, LATE = 80, 64


def dot(left, right):
    return jnp.dot(left, right, preferred_element_type=F32)


def dot_nt(left, right):
    return lax.dot_general(left, right, (((1,), (1,)), ((), ())), preferred_element_type=F32)


def dot_tn(left, right):
    return lax.dot_general(left, right, (((0,), (0,)), ((), ())), preferred_element_type=F32)


def lanes(shape):
    return lax.broadcasted_iota(jnp.int32, shape, len(shape) - 1)


def half(value, slot):
    low_half = lanes(value.shape) < HEAD
    zero = jnp.zeros_like(value)
    return jnp.where(low_half, value, zero) if slot == 0 else jnp.where(low_half, zero, value)


def pair(first, second):
    return jnp.where(lanes(first.shape) < HEAD, first, second)


def swap(value):
    return pltpu.roll(value, HEAD, 1)


def heads_to_rows(heads, rows, factor):
    for p in range(HEADS // 2):
        even = heads[2 * p].astype(F32) * factor
        odd = heads[2 * p + 1].astype(F32) * factor
        rows[0:64, p * 128 : p * 128 + 128] = pair(even, swap(odd)).astype(BF16)
        rows[64:128, p * 128 : p * 128 + 128] = pair(swap(even), odd).astype(BF16)


class Exchange:
    def __init__(self, spot, out, into, send, recv):
        self.spot, self.out, self.into, self.send, self.recv = spot, out, into, send, recv

    def copy(self, unit, step, source, target, peer):
        return pltpu.make_async_remote_copy(
            src_ref=self.out.at[unit, source],
            dst_ref=self.into.at[unit, target],
            send_sem=self.send.at[unit, step],
            recv_sem=self.recv.at[unit, step],
            device_id=(self.spot.y, peer),
            device_id_type=MESH,
        )

    def start(self, unit, block):
        me = self.spot.s

        def body(i, carry):
            peer = block * 4 + i

            @pl.when(peer != me)
            def _():
                self.copy(unit, (peer + 16 - me) % 16, peer, me, peer).start()

            return carry

        lax.fori_loop(0, 4, body, 0)

    def keep(self, unit):
        self.into[unit, self.spot.s] = self.out[unit, self.spot.s]

    def wait_block(self, unit, block):
        me = self.spot.s

        def body(i, carry):
            peer = block * 4 + i

            @pl.when(peer != me)
            def _():
                self.copy(unit, (me + 16 - peer) % 16, peer, peer, peer).wait_recv()

            return carry

        lax.fori_loop(0, 4, body, 0)

    def wait(self, unit):
        me = self.spot.s

        def body(step, carry):
            peer = (me + 16 - step) % 16
            self.copy(unit, step, peer, peer, peer).wait_recv()
            return carry

        lax.fori_loop(1, 16, body, 0)

    def finish(self, units):
        me = self.spot.s

        def body(step, carry):
            for unit in range(units):
                self.copy(unit, step, (me + step) % 16, me, (me + step) % 16).wait_send()
            return carry

        lax.fori_loop(1, 16, body, 0)


class Scatter:
    def __init__(self, spot, wide, own, core_in, core_sum, x_in, x_sum, into, send, recv):
        self.spot, self.wide = spot, wide
        self.own, self.core_in, self.core_sum = own, core_in, core_sum
        self.x_in, self.x_sum, self.into = x_in, x_sum, into
        self.send, self.recv = send, recv
        self.started = []

    def push(self, source, target, peer):
        route = len(self.started)
        copy = pltpu.make_async_remote_copy(
            src_ref=source,
            dst_ref=target,
            send_sem=self.send.at[route],
            recv_sem=self.recv.at[route],
            device_id=peer,
            device_id_type=MESH,
        )
        copy.start()
        self.started.append(copy)

    def first(self):
        p = self.spot
        self.push(self.own.at[:, :, :, 1 - p.c], self.core_in, p.at(dc=1))

    def second(self):
        p = self.spot
        self.started[0].wait_recv()
        self.core_sum[...] = (self.own[:, :, :, p.c].astype(F32) + self.core_in[...].astype(F32)).astype(BF16)
        if not self.wide:
            self.push(self.core_sum.at[:, :, 1 - p.x], self.x_in, p.at(dx=1))

    def third(self):
        p = self.spot
        if not self.wide:
            self.started[1].wait_recv()
            self.x_sum[...] = (self.core_sum[:, :, p.x].astype(F32) + self.x_in[...].astype(F32)).astype(BF16)
        for dy in range(2):
            for dz in range(4):
                for dx in range(2 if self.wide else 1):
                    if dy + dz + dx == 0:
                        continue
                    y, z, x = (p.y + dy) % 2, (p.z + dz) % 4, (p.x + dx) % 2
                    source = self.core_sum.at[y, z, x] if self.wide else self.x_sum.at[y, z]
                    self.push(source, self.into.at[dy, dz, dx], p.at(dy=dy, dz=dz, dx=dx))

    def fourth(self):
        p = self.spot
        for copy in self.started[1 if self.wide else 2 :]:
            copy.wait_recv()
        total = [self.core_sum[p.y, p.z, p.x] if self.wide else self.x_sum[p.y, p.z], None]
        total[0] = total[0].astype(F32)
        for dy in range(2):
            for dz in range(4):
                for dx in range(2 if self.wide else 1):
                    if dy + dz + dx == 0:
                        continue
                    term = self.into[dy, dz, dx].astype(F32)
                    total[dy] = term if total[dy] is None else total[dy] + term
        return total

    def finish(self):
        for copy in self.started:
            copy.wait_send()


def scatter_shapes(rows, wide):
    return [
        pltpu.VMEM((2, 4, 2, 2, rows, 128), BF16),
        pltpu.VMEM((2, 4, 2, rows, 128), BF16),
        pltpu.VMEM((2, 4, 2, rows, 128), BF16),
        pltpu.VMEM((2, 4, rows, 128), BF16),
        pltpu.VMEM((2, 4, rows, 128), BF16),
        pltpu.VMEM((2, 4, 2 if wide else 1, rows, 128), BF16),
        pltpu.SemaphoreType.DMA((17,)),
        pltpu.SemaphoreType.DMA((17,)),
    ]


def layer_kernel(*refs):
    it = iter(refs)

    def take(count):
        return [next(it) for _ in range(count)]

    attn, fc1, fc2, tok_far, cot_far, down_table, up_table, ff_table, vec_in, bias_in, lengths, ids = take(12)
    layer_out, input_grad, down_out, up_out, ff_out = take(5)
    wide, tall, rank_all, ff_all = take(4)
    rank_in, rank_up, rank_x, vec, ff_low, bias = take(6)
    heads_out, heads_in = take(2)
    weights_low, weights_back = take(2)
    attended, stat, tmp, sum_one, scaled_one, normed, grad_second, grad_first = take(8)
    tok, cot, mixed, normed_low, out_low, branch_low, query_low, key_low, value_low = take(9)
    slope, act, grad_hidden, inner4 = take(4)
    id_rows, table, rank_other, ff_other = take(4)
    early_refs, late_refs = take(8), take(8)
    own, send, recv, hsend, hrecv, id_sem = take(6)

    spot = Spot()
    here = (spot.y, spot.z, spot.x, spot.c)
    parts = [wide.at[k] for k in range(16)] + [tall.at[k] for k in range(8)] + [rank_all, ff_all]
    placed = {}
    for k in range(8, 16):
        placed[k] = fc1.at[:, pl.ds((k - 8) * 512, 512)]
    for k in range(16, 24):
        placed[k] = fc2.at[:, pl.ds((k - 16) * 128, 128)]
    placed = {k: pltpu.make_async_copy(source, parts[k].at[here], own.at[k - 8]) for k, source in placed.items()}
    tok_copy = pltpu.make_async_copy(tok_far, tok, own.at[16])
    cot_copy = pltpu.make_async_copy(cot_far, cot, own.at[17])
    tok_copy.start()
    for k in (0, 1):
        wide[(k,) + here] = attn[:, 0, k * 512 : k * 512 + 512]
    for copy in placed.values():
        copy.start()
    cot_copy.start()
    others = {2: rank_other, 3: ff_other}
    gather = Gather(spot, [parts[k] for k in ORDER], WAYS, others, send, recv)
    swaps = Exchange(spot, heads_out, heads_in, hsend, hrecv)
    early = Scatter(spot, False, *early_refs)
    late = Scatter(spot, True, *late_refs)
    first_row = lax.broadcasted_iota(jnp.int32, (8, 128), 0) == 0
    id_rows[spot.y] = jnp.where(first_row, ids[0], ids[1])
    enter(spot)
    gather.step(0)
    id_copy = pltpu.make_async_remote_copy(
        src_ref=id_rows.at[spot.y],
        dst_ref=id_rows.at[spot.y],
        send_sem=id_sem.at[0],
        recv_sem=id_sem.at[1],
        device_id=spot.at(dy=1),
        device_id_type=MESH,
    )
    id_copy.start()
    for j in range(1, 4):
        for k in range(2):
            wide[(2 * j + k,) + here] = attn[:, j, k * 512 : k * 512 + 512]

    def chosen(source, kind, y, slot):
        who = id_rows[y, slot : slot + 1, 0 : source.shape[3]]
        total = None
        for a in range(ADAPTERS):
            term = jnp.where(who == a, source[a, kind].astype(F32), 0.0)
            total = term if total is None else total + term
        return total

    def pick_all():
        table[...] = jnp.zeros_like(table)
        for g in range(2):
            y = (spot.y + g) % 2
            for slot in range(2):
                for j in range(4):
                    row = g * 384 + j * 32 + slot * 16
                    table[row : row + 16, 0:32] = chosen(down_table, j, y, slot)
                    table[row + 128 : row + 144, 0:32] = chosen(up_table, j, y, slot)
                row = g * 384 + 256 + slot * 16
                table[row : row + 16, 0:32] = chosen(down_table, 4, y, slot)
                table[row + 32 : row + 48, 0:32] = chosen(up_table, 4, y, slot)
                for kind in range(2):
                    row = 768 + g * 64 + kind * 32 + slot * 16
                    table[row : row + 16, :] = chosen(ff_table, kind, y, slot)
        for n in range(3):
            cols = slice(n * 128, n * 128 + 128)
            rank_all[here + (slice(None), cols)] = table[cols, :].T[0:32].astype(BF16)
            rank_other[:, cols] = table[384 + n * 128 : 512 + n * 128, :].T[0:32].astype(BF16)
        turned = table[768:896, :].T
        ff_all[here + (slice(0, 64),)] = pair(turned[0:64], swap(turned[64:128])).astype(BF16)
        ff_other[0:64] = pair(swap(turned[0:64]), turned[64:128]).astype(BF16)
        table[0:8, 0:32] = vec_in[...].astype(F32)
        table[0:8, 32:128] = jnp.zeros((8, 96), F32)
        columns = pltpu.roll(table[0:8, :], (spot.s % 4) * 32, 1)
        rows = jnp.concatenate([jnp.broadcast_to(bias_in[...].astype(F32), (8, 128)), columns], axis=0)
        ff_all[here + (slice(64, 80),)] = rows.astype(BF16)
        ff_other[64:80] = rows.astype(BF16)

    lane = lanes((128, 128))
    row_slot = lax.broadcasted_iota(jnp.int32, (128, 128), 0) >= 64
    slot_lane = ((lane & 16) != 0) == row_slot
    kind4 = [slot_lane & ((lane >> 5) == j) for j in range(4)]
    kind_ff = [slot_lane & ((lane >> 5) == k) for k in range(2)]

    def only(mask, value):
        return jnp.where(mask, value, jnp.zeros_like(value))

    def square(k, t):
        halves = [wide[2 * k + i, t // 2, pl.ds((t % 2) * 2, 2)].reshape(256, 512) for i in range(2)]
        return jnp.concatenate(halves, axis=1)

    def columns(k, n):
        return wide[2 * k + n // 2, :, :, :, :, :, tile(n % 2)].reshape(1024, 256)

    def tile(n, size=256):
        return pl.ds(pl.multiple_of(n * size, size), size)

    def unpack_rank():
        rank_in[...] = rank_all[:, :, :, :, :, 0:128].reshape(1024, 128)
        rank_up[...] = rank_all[:, :, :, :, :, 128:256].reshape(1024, 128)
        rank_x[...] = rank_all[:, :, :, :, :, 256:384].reshape(1024, 128)

    def ff_rows(first, count):
        return ff_low[pl.ds(first, count)].reshape(count * 128, 128)

    def unpack_ff():
        columns_of = {}
        packed = ff_all[:, :, :, :, 0:64, :].reshape(32, 64, 128)
        ff_low[:, 0] = packed
        ff_low[:, 1] = swap(packed.astype(F32).reshape(2048, 128)).astype(BF16).reshape(32, 64, 128)
        for o in range(32):
            y, z, x, c = o // 16, (o // 4) % 4, (o // 2) % 2, o % 2
            rows = ff_all[y, z, x, c, 64:80, :].astype(F32)
            bias[:, o * 128 : o * 128 + 128] = rows[0:8]
            columns_of[o // 4] = rows[8:16] if o % 4 == 0 else columns_of[o // 4] + rows[8:16]
        for n in range(8):
            vec[:, n * 128 : n * 128 + 128] = columns_of[n]

    def to_heads(unit, block, value):
        for p in range(2):
            first = value[0:64, p * 128 : p * 128 + 128]
            second = value[64:128, p * 128 : p * 128 + 128]
            heads_out[unit, block * 4 + 2 * p] = pair(first, swap(second)).astype(BF16)
            heads_out[unit, block * 4 + 2 * p + 1] = pair(swap(first), second).astype(BF16)
        swaps.start(unit, block)

    def turn(body):
        def shifted(t, carry):
            body((spot.z + t) % 4)
            return carry

        lax.fori_loop(0, 4, shifted, 0)

    def project_in(j):
        inner = only(kind4[j], inner4[...])

        def body(n):
            cols = tile(n)
            value = dot(tok[...], columns(j, n)) + dot_nt(inner, rank_up[cols, :])
            if j == 0:
                value = (value + vec[0:1, cols]) * 0.125
            if j == 2:
                value = value + vec[1:2, cols]
            to_heads(j, n, value)

        turn(body)
        swaps.keep(j)

    def attention(t):
        if t == 0:
            for j in range(3):
                swaps.wait(j)
        block = (spot.z + t) % 4
        keys = heads_in[1].reshape(1024, 128)
        values = heads_in[2].reshape(1024, 128)
        rows = tile(block)
        query = heads_in[0, pl.ds(block * 4, 4)].reshape(256, 128)
        results, stats = [], []
        for slot in range(2):
            scores = dot_nt(half(query, slot), keys)
            scores = jnp.where(lanes(scores.shape) < lengths[slot], scores, NEG_FILL)
            top = jnp.max(scores, axis=-1, keepdims=True)
            shifted = jnp.exp(scores - top)
            total = jnp.sum(shifted, axis=-1, keepdims=True)
            low = (shifted * (1.0 / total)).astype(BF16)
            weights_low[slot, rows, :] = low
            results.append(dot(low, values))
            stats.append(jnp.broadcast_to(top + jnp.log(total), (256, 128)))
        result = pair(results[0], results[1])
        attended[rows, :] = result
        heads_out[3, pl.ds(block * 4, 4)] = result.astype(BF16).reshape(4, 64, 128)
        stat[rows, :] = pair(stats[0], stats[1])
        swaps.start(3, block)
        if t == 3:
            swaps.keep(3)

    def attention_turned(first):
        logsum = stat[...].T
        queries = heads_in[0].reshape(1024, 128)
        turned = [logsum[0:1], logsum[64:65]]

        def body(t, carry):
            rows = tile(t)
            keys = heads_in[1, pl.ds(t * 4, 4)].reshape(256, 128)
            for slot in range(2):
                scores = dot_nt(half(keys, slot), queries)
                weights = jnp.exp(scores - turned[slot])
                place = lax.broadcasted_iota(jnp.int32, weights.shape, 0) + t * 256
                weights = jnp.where(place < lengths[slot], weights, 0.0)
                weights_back[slot, rows, :] = weights.astype(BF16)
            return carry

        lax.fori_loop(first, first + 2, body, 0)

    def normalize(value):
        centered = value - jnp.mean(value, axis=-1, keepdims=True)
        spread = lax.rsqrt(jnp.mean(centered * centered, axis=-1, keepdims=True) + NORM_EPS)
        return centered * spread, spread

    def normalize_back(grad, scaled, spread):
        shift = jnp.mean(grad, axis=-1, keepdims=True)
        along = jnp.mean(grad * scaled, axis=-1, keepdims=True)
        return spread * (grad - shift - scaled * along)

    saved = {}

    def branch():
        swaps.wait(3)
        heads_to_rows(heads_in.at[3], mixed, 1.0)
        saved["o"] = only(kind4[3], dot(mixed[...], rank_in[...])).astype(BF16)

        def body(n, carry):
            cols = tile(n)
            value = dot(mixed[...], columns(3, n)) + dot_nt(saved["o"], rank_up[cols, :])
            sum_one[:, cols] = tok[:, cols].astype(F32) + value + vec[2:3, cols]
            return carry

        lax.fori_loop(0, 4, body, 0)
        scaled, saved["spread_one"] = normalize(sum_one[...])
        scaled_one[...] = scaled
        value = scaled * vec[4:5] + vec[5:6]
        normed[...] = value
        normed_low[...] = value.astype(BF16)
        saved["hidden"] = only(kind_ff[0], dot(normed_low[...], rank_x[...])).astype(BF16)

    def expand(k):
        def body(i, carry):
            n = k * 2 + i
            cols = tile(n)
            value = dot(normed_low[...], wide[8 + k, :, :, :, :, :, tile(i)].reshape(1024, 256))
            value = value + dot_nt(saved["hidden"], ff_rows(n * 2, 2)) + bias[0:1, cols]
            share = 0.5 * (1.0 + lax.erf(value * math.sqrt(0.5)))
            act[:, cols] = (value * share).astype(BF16)
            bell = jnp.exp(-0.5 * value * value) * (1.0 / math.sqrt(2.0 * math.pi))
            slope[:, cols] = share + value * bell
            return carry

        lax.fori_loop(0, 2, body, 0)

    def contract(q):
        if q == 0:
            saved["out"] = only(kind_ff[1], dot(act[...], ff_rows(0, 32))).astype(BF16)
        cols = slice(q * 256, q * 256 + 256)
        weight = jnp.concatenate([tall[2 * q + i].reshape(4096, 128) for i in range(2)], axis=1)
        value = dot(act[...], weight) + dot_nt(saved["out"], rank_x[cols, :])
        tmp[:, cols] = normed[:, cols] + value + vec[3:4, cols]

    def outer():
        rows = lax.broadcasted_iota(jnp.int32, (128, 1), 0)
        place = spot.s * 64 + (rows & 63)
        limit = jnp.where(rows < 64, lengths[0], lengths[1])
        live = (place < limit).astype(F32)
        scaled, spread = normalize(tmp[...])
        layer_out[...] = (live * (scaled * vec[6:7] + vec[7:8])).astype(BF16)
        grad = normalize_back(live * cot[...].astype(F32) * vec[6:7], scaled, spread)
        grad_second[...] = grad
        out_low[...] = grad.astype(BF16)
        saved["g_out"] = only(kind_ff[1], dot(out_low[...], rank_x[...])).astype(BF16)

    def hidden_back():
        def body(t, carry):
            rows = tile(t, 512)
            value = dot_nt(saved["g_out"], ff_rows(t * 4, 4))
            for q in range(4):
                pieces = [tall[2 * q + i, t // 4, t % 4].reshape(512, 128) for i in range(2)]
                piece = jnp.concatenate(pieces, axis=1)
                value = value + dot_nt(out_low[:, q * 256 : q * 256 + 256], piece)
            grad_hidden[:, rows] = (value * slope[:, rows]).astype(BF16)
            return carry

        lax.fori_loop(0, 8, body, 0)
        saved["g_hidden"] = only(kind_ff[0], dot(grad_hidden[...], ff_rows(0, 32))).astype(BF16)

    def normed_back():
        def body(t, carry):
            rows = tile(t)
            value = dot_nt(saved["g_hidden"], rank_x[rows, :]) + grad_second[:, rows]
            for q in range(4):
                value = value + dot_nt(grad_hidden[:, q * 1024 : q * 1024 + 1024], square(4 + q, t))
            tmp[:, rows] = value
            return carry

        lax.fori_loop(0, 4, body, 0)
        grad = normalize_back(tmp[...] * vec[4:5], scaled_one[...], saved["spread_one"])
        grad_first[...] = grad
        branch_low[...] = grad.astype(BF16)
        saved["g_o"] = only(kind4[3], dot(branch_low[...], rank_up[...])).astype(BF16)

    def mixed_back():
        def body(n):
            value = dot_nt(branch_low[...], square(3, n)) + dot_nt(saved["g_o"], rank_in[tile(n), :])
            to_heads(4, n, value)

        turn(body)
        swaps.keep(4)

    def early_grads():
        own_grads = early.own
        value = dot_tn(normed_low[...], saved["g_hidden"]) + dot_tn(out_low[...], saved["out"])
        value = value.reshape(32, 2, 16, 128)
        value = value[:, 0] + swap(value[:, 1].reshape(512, 128)).reshape(32, 16, 128)
        own_grads[:, :, :, :, 0:16, :] = value.astype(BF16).reshape(2, 4, 2, 2, 16, 128)
        for y in range(2):
            for z in range(4):
                cols = slice((y * 4 + z) * 512, (y * 4 + z) * 512 + 512)
                value = dot_tn(grad_hidden[:, cols], saved["hidden"]) + dot_tn(act[:, cols], saved["g_out"])
                value = value.reshape(4, 128, 128)
                for o in range(4):
                    packed = value[o, 0:64] + swap(value[o, 64:128])
                    own_grads[y, z, o // 2, o % 2, 16:80, :] = packed.astype(BF16)

    def query_back(t):
        block = (spot.z + 4 - t) % 4
        swaps.wait_block(4, block)
        rows = tile(block)
        keys = heads_in[1].reshape(1024, 128)
        values = heads_in[2].reshape(1024, 128)
        grad_block = heads_in[4, pl.ds(block * 4, 4)].reshape(256, 128)
        product = grad_block.astype(F32) * attended[rows, :]
        parts_, deltas = [], []
        for slot in range(2):
            delta = jnp.sum(half(product, slot), axis=-1, keepdims=True)
            grad_probs = dot_nt(half(grad_block, slot), values)
            weights = weights_low[slot, rows, :].astype(F32)
            grad_scores = (weights * (grad_probs - delta)).astype(BF16)
            parts_.append(dot(grad_scores, keys))
            deltas.append(jnp.broadcast_to(delta, (256, 128)))
        heads_out[5, pl.ds(block * 4, 4)] = pair(*parts_).astype(BF16).reshape(4, 64, 128)
        stat[rows, :] = pair(*deltas)
        swaps.start(5, block)
        if t == 3:
            swaps.keep(5)

    def key_back():
        queries = heads_in[0].reshape(1024, 128)
        grads = heads_in[4].reshape(1024, 128)
        turned = stat[...].T
        turned = [turned[0:1], turned[64:65]]

        def body(block):
            rows = tile(block)
            value_block = heads_in[2, pl.ds(block * 4, 4)].reshape(256, 128)
            key_parts, value_parts = [], []
            for slot in range(2):
                weights = weights_back[slot, rows, :]
                grad_probs = dot_nt(half(value_block, slot), grads)
                grad_scores = (weights.astype(F32) * (grad_probs - turned[slot])).astype(BF16)
                key_parts.append(dot(grad_scores, queries))
                value_parts.append(dot(weights, grads))
            heads_out[6, pl.ds(block * 4, 4)] = pair(*key_parts).astype(BF16).reshape(4, 64, 128)
            heads_out[7, pl.ds(block * 4, 4)] = pair(*value_parts).astype(BF16).reshape(4, 64, 128)
            swaps.start(6, block)
            swaps.start(7, block)

        turn(body)
        swaps.keep(6)
        swaps.keep(7)

    def inputs_back():
        swaps.wait(5)
        heads_to_rows(heads_in.at[5], query_low, 0.125)
        swaps.wait(6)
        heads_to_rows(heads_in.at[6], key_low, 1.0)
        swaps.wait(7)
        heads_to_rows(heads_in.at[7], value_low, 1.0)
        grads = (query_low, key_low, value_low)
        inner = jnp.zeros((128, 128), F32)
        for j in range(3):
            inner = jnp.where(kind4[j], dot(grads[j][...], rank_up[...]), inner)
        saved["g_in"] = inner.astype(BF16)
        value = dot_tn(tok[...], saved["g_in"]) + dot_tn(mixed[...], saved["g_o"])
        late.own[:, :, :, :, 0:32, :] = value.astype(BF16).reshape(2, 4, 2, 2, 32, 128)
        value = dot_tn(branch_low[...], saved["o"])
        for j in range(3):
            value = value + dot_tn(grads[j][...], only(kind4[j], inner4[...]))
        late.own[:, :, :, :, 32:64, :] = value.astype(BF16).reshape(2, 4, 2, 2, 32, 128)

    def tokens_back(t):
        rows = pl.ds(t * 256, 256)
        value = dot_nt(saved["g_in"], rank_in[rows, :]) + grad_first[:, rows]
        for j, grad in enumerate((query_low, key_low, value_low)):
            value = value + dot_nt(grad[...], square(j, t))
        input_grad[:, rows] = value.astype(BF16)

    def results(early_sum, late_sum):
        turned, ff_turned = [], []
        for dy in range(2):
            cross = jnp.concatenate([early_sum[dy][0:16], swap(early_sum[dy][0:16])], axis=0)
            table[0:64, :] = late_sum[dy]
            table[64:96, :] = cross
            table[96:128, :] = jnp.zeros((32, 128), F32)
            turned.append(table[0:128, :].T)
            packed = early_sum[dy][16:80]
            ff_turned.append(jnp.concatenate([packed, swap(packed)], axis=0).T)
        for a in range(ADAPTERS):
            who = [id_rows[(spot.y + dy) % 2, 0:2, :] == a for dy in range(2)]
            share = [match.astype(F32) for match in who]

            def gathered(source, first):
                total = None
                for dy in range(2):
                    for s in range(2):
                        row = first + s * 16
                        term = share[dy][s : s + 1] * source[dy][row : row + 16, :]
                        total = term if total is None else total + term
                return total

            for j in range(4):
                value = gathered(turned, j * 32)
                down_out[a, j] = value[:, 0:32]
                up_out[a, j] = value[:, 32:64]
            down_out[a, 4] = gathered(turned, 0)[:, 64:96]
            up_out[a, 4] = gathered(turned, 32)[:, 64:96]
            for kind in range(2):
                ff_out[a, kind] = gathered(ff_turned, kind * 32)

    waited = set()

    def here_by(last):
        for k in ORDER[: last + 1]:
            if k in placed and k not in waited:
                placed[k].wait()
                waited.add(k)

    for t in range(1, CHUNKS + 4):
        if t == 2:
            id_copy.wait_recv()
            pick_all()
        here_by(min(t, CHUNKS - 1))
        gather.step(t)
        if t == 7:
            tok_copy.wait()
            unpack_rank()
            unpack_ff()
            inner4[...] = dot(tok[...], rank_in[...]).astype(BF16)
        if t in (7, 9, 11):
            project_in((t - 7) // 2)
        if 14 <= t <= 17:
            attention(t - 14)
        if 18 <= t <= 19:
            attention_turned((t - 18) * 2)
        if t == 20:
            branch()
        if 21 <= t <= 24:
            expand(2 * t - 42)
            expand(2 * t - 41)
        if t == 27:
            contract(0)
        if t >= 27:
            contract(t - 26)
    cot_copy.wait()
    outer()
    hidden_back()
    normed_back()
    mixed_back()
    early_grads()
    early.first()
    for t in range(4):
        query_back(t)
    early.second()
    key_back()
    early.third()
    inputs_back()
    late.first()
    tokens_back(0)
    late.second()
    late.third()
    for t in range(1, 4):
        tokens_back(t)
    results(early.fourth(), late.fourth())
    id_copy.wait_send()
    gather.finish()
    swaps.finish(8)
    early.finish()
    late.finish()


def hand_on_kernel(*refs):
    count = len(refs) // 2
    for k in range(count):
        refs[count + k][...] = refs[k][...]


def hand_on(arrays):
    near = pl.BlockSpec(memory_space=pltpu.VMEM)
    return pl.pallas_call(
        hand_on_kernel,
        out_shape=[jax.ShapeDtypeStruct(array.shape, array.dtype) for array in arrays],
        in_specs=[near] * len(arrays),
        out_specs=[near] * len(arrays),
        name="hand_on",
    )(*arrays)


def layer(attn, fc1, fc2, tok, cot, down, up, ff, vec, bias, lengths, ids):
    lead = (2, 4, 2, 2)
    anywhere = pl.BlockSpec(memory_space=pl.ANY)
    near = pl.BlockSpec(memory_space=pltpu.VMEM)
    scalar = pl.BlockSpec(memory_space=pltpu.SMEM)

    def buffer(*shape, dtype=BF16):
        return pltpu.VMEM(shape, dtype)

    scratch = [
        buffer(16, *lead, 32, 512),
        buffer(8, *lead, 128, 128),
        buffer(*lead, 32, 384),
        buffer(*lead, 80, 128),
    ]
    scratch += [buffer(1024, 128)] * 3 + [buffer(8, 1024, dtype=F32), buffer(32, 2, 64, 128)]
    scratch += [buffer(8, 4096, dtype=F32)]
    scratch += [buffer(8, 16, 64, 128)] * 2
    scratch += [buffer(2, 1024, 1024)] * 2
    scratch += [buffer(1024, 128, dtype=F32)] * 2
    scratch += [buffer(128, 1024, dtype=F32)] * 6
    scratch += [buffer(128, 1024)] * 9
    scratch += [buffer(128, 4096, dtype=F32), buffer(128, 4096), buffer(128, 4096), buffer(128, 128)]
    scratch += [buffer(2, 8, 128, dtype=jnp.int32), buffer(896, 128, dtype=F32)]
    scratch += [buffer(32, 384), buffer(80, 128)]
    scratch += scatter_shapes(EARLY, False) + scatter_shapes(LATE, True)
    scratch += [pltpu.SemaphoreType.DMA((18,))]
    scratch += [pltpu.SemaphoreType.DMA((CHUNKS, ROUTES))] * 2
    scratch += [pltpu.SemaphoreType.DMA((8, 16))] * 2
    scratch += [pltpu.SemaphoreType.DMA((2,))]
    return pl.pallas_call(
        layer_kernel,
        out_shape=[
            jax.ShapeDtypeStruct(tok.shape, BF16),
            jax.ShapeDtypeStruct(tok.shape, BF16),
            jax.ShapeDtypeStruct(down.shape, F32),
            jax.ShapeDtypeStruct(up.shape, F32),
            jax.ShapeDtypeStruct(ff.shape, F32),
        ],
        in_specs=[near] + [anywhere] * 4 + [near] * 5 + [scalar] * 2,
        out_specs=[near] * 5,
        scratch_shapes=scratch,
        compiler_params=pltpu.CompilerParams(
            collective_id=0, has_side_effects=True, vmem_limit_bytes=63 * 2**20
        ),
        name="layer",
    )(attn, fc1, fc2, tok, cot, down, up, ff, vec, bias, lengths, ids)


def fast_device(
    tokens,
    cotangent,
    lengths,
    adapter_ids,
    attn_weight,
    fc1_weight,
    fc2_weight,
    vectors,
    fc1_bias,
    adapter_down,
    adapter_up,
    ff_adapters,
):
    width = tokens.shape[2]
    outs = layer(
        attn_weight,
        fc1_weight,
        fc2_weight,
        tokens.reshape(-1, width),
        cotangent.reshape(-1, width),
        adapter_down.transpose(1, 2, 3, 0),
        adapter_up.transpose(1, 2, 3, 0),
        ff_adapters.transpose(1, 2, 3, 0),
        vectors.T,
        fc1_bias[None],
        lengths,
        adapter_ids,
    )
    outs = hand_on(outs)
    grads = [grad.transpose(3, 0, 1, 2) for grad in outs[2:]]
    return (outs[0].reshape(tokens.shape), outs[1].reshape(tokens.shape), *grads)


def solution(mesh):
    in_specs = (
        P("fsdp", "seq", None),
        P("fsdp", "seq", None),
        P("fsdp"),
        P("fsdp"),
        P(("fsdp", "seq"), None, None),
        P(("fsdp", "seq"), None),
        P(("fsdp", "seq"), None),
        P(("fsdp", "seq"), None),
        P(("fsdp", "seq")),
        P(("fsdp", "seq"), None, None, None),
        P(("fsdp", "seq"), None, None, None),
        P(("fsdp", "seq"), None, None, None),
    )
    out_specs = (
        P("fsdp", "seq", None),
        P("fsdp", "seq", None),
        P(("fsdp", "seq"), None, None, None),
        P(("fsdp", "seq"), None, None, None),
        P(("fsdp", "seq"), None, None, None),
    )
    fast = mesh.shape["fsdp"] == 2 and mesh.shape["seq"] == HEADS
    return jax.shard_map(
        fast_device if fast else on_device, mesh=mesh, in_specs=in_specs, out_specs=out_specs, check_vma=False
    )
```

```python
from functools import partial
import math

import jax
import jax.numpy as jnp
from jax import lax
from jax.experimental import pallas as pl
from jax.experimental.pallas import tpu as pltpu
from jax.sharding import PartitionSpec as P

HEADS = 16
HEAD = 64
ADAPTERS = 8


NEG_FILL = -1e30
NORM_EPS = 1e-05


def split_heads(values_in):
    return values_in.reshape(values_in.shape[:-1] + (HEADS, HEAD))


def norm_rows(value, gain, shift):
    centered = value - jnp.mean(value, axis=-1, keepdims=True)
    scaled = centered * lax.rsqrt(jnp.mean(centered * centered, axis=-1, keepdims=True) + NORM_EPS)
    return scaled * gain + shift


def gelu_exact(value):
    return jax.nn.gelu(value, approximate=False)


def choose(onehot, table):
    return jnp.einsum("si,dikr->sdkr", onehot, table, preferred_element_type=jnp.float32).astype(
        jnp.bfloat16
    )


def unpack(gathered, onehot):
    attn_all, fc1_all, fc2_all, vector_all, bias_ff, down_all, up_all, ff_all = gathered
    return (
        attn_all,
        fc1_all,
        fc2_all,
        vector_all.astype(jnp.float32),
        bias_ff.astype(jnp.float32),
        choose(onehot, down_all),
        choose(onehot, up_all),
        choose(onehot, ff_all),
    )


def project(inputs, weight, down_table, up_table):
    frozen_part = jnp.einsum("spd,de->spe", inputs, weight, preferred_element_type=jnp.float32)
    inner_low = jnp.einsum(
        "spd,sdr->spr", inputs, down_table, preferred_element_type=jnp.float32
    ).astype(jnp.bfloat16)
    return (
        frozen_part
        + jnp.einsum("spr,ser->spe", inner_low, up_table, preferred_element_type=jnp.float32),
        inner_low,
    )


def project_back(inputs, inner_low, grad_out, weight, down_table, up_table):
    grad_inner = jnp.einsum(
        "spe,ser->spr", grad_out, up_table, preferred_element_type=jnp.float32
    ).astype(jnp.bfloat16)
    grad_in = jnp.einsum("spe,de->spd", grad_out, weight, preferred_element_type=jnp.float32)
    grad_in = grad_in + jnp.einsum(
        "spr,sdr->spd", grad_inner, down_table, preferred_element_type=jnp.float32
    )
    grad_up = jnp.einsum("spe,spr->ser", grad_out, inner_low, preferred_element_type=jnp.float32)
    grad_down = jnp.einsum("spd,spr->sdr", inputs, grad_inner, preferred_element_type=jnp.float32)
    return (grad_in, grad_down, grad_up)


def block_scores(query_heads, key_block, key_start, lengths):
    block_rows = key_block.shape[1]
    scores = jnp.einsum(
        "sqhd,skhd->shqk", query_heads, split_heads(key_block), preferred_element_type=jnp.float32
    )
    valid_keys = (key_start + jnp.arange(block_rows))[None, :] < lengths[:, None]
    return jnp.where(valid_keys[:, None, None, :], scores, NEG_FILL)


def score_grads(scores, logsum, row_delta, grad_heads, value_heads):
    probs = jnp.exp(scores - logsum[..., None])
    grad_probs = jnp.einsum(
        "sqhd,skhd->shqk", grad_heads, value_heads, preferred_element_type=jnp.float32
    )
    grad_scores = (probs * (grad_probs - row_delta[..., None])).astype(jnp.bfloat16)
    return (grad_scores, probs.astype(jnp.bfloat16))


def attend(query, all_keys, all_values, lengths):
    seq_span = all_keys.shape[1]
    block_rows = math.gcd(seq_span, 512)
    blocks = seq_span // block_rows
    query_heads = split_heads(query)
    slot_count, query_rows = (query.shape[0], query.shape[1])
    stats_shape = (slot_count, HEADS, query_rows)

    def stats_step(running, step_index):
        row_top, row_total = running
        offset = step_index * block_rows
        scores = block_scores(
            query_heads, lax.dynamic_slice_in_dim(all_keys, offset, block_rows, 1), offset, lengths
        )
        new_top = jnp.maximum(row_top, jnp.max(scores, axis=-1))
        row_total = row_total * jnp.exp(row_top - new_top) + jnp.sum(
            jnp.exp(scores - new_top[..., None]), axis=-1
        )
        return ((new_top, row_total), None)

    start_top = jnp.full(stats_shape, NEG_FILL, jnp.float32)
    (row_top, row_total), _ = lax.scan(
        stats_step, (start_top, jnp.zeros(stats_shape, jnp.float32)), jnp.arange(blocks)
    )
    logsum = row_top + jnp.log(row_total)

    def mix_step(running, step_index):
        offset = step_index * block_rows
        scores = block_scores(
            query_heads, lax.dynamic_slice_in_dim(all_keys, offset, block_rows, 1), offset, lengths
        )
        weights_low = jnp.exp(scores - logsum[..., None]).astype(jnp.bfloat16)
        value_heads = split_heads(lax.dynamic_slice_in_dim(all_values, offset, block_rows, 1))
        return (
            running
            + jnp.einsum(
                "shqk,skhd->sqhd", weights_low, value_heads, preferred_element_type=jnp.float32
            ),
            None,
        )

    mixed_heads, _ = lax.scan(
        mix_step, jnp.zeros(query_heads.shape, jnp.float32), jnp.arange(blocks)
    )
    return (mixed_heads.reshape(query.shape), logsum)


def query_side(query, all_keys, all_values, grad_low, logsum, row_delta, lengths):
    seq_span = all_keys.shape[1]
    block_rows = math.gcd(seq_span, 512)
    blocks = seq_span // block_rows
    query_heads = split_heads(query)
    grad_heads = split_heads(grad_low)
    slot_count = query.shape[0]
    width = query.shape[2]

    def step(running, step_index):
        offset = step_index * block_rows
        key_block = lax.dynamic_slice_in_dim(all_keys, offset, block_rows, 1)
        value_block = lax.dynamic_slice_in_dim(all_values, offset, block_rows, 1)
        scores = block_scores(query_heads, key_block, offset, lengths)
        grad_scores, weights_low = score_grads(
            scores, logsum, row_delta, grad_heads, split_heads(value_block)
        )
        grad_acc = running[0] + jnp.einsum(
            "shqk,skhd->sqhd",
            grad_scores,
            split_heads(key_block),
            preferred_element_type=jnp.float32,
        )
        key_part = jnp.einsum(
            "shqk,sqhd->skhd", grad_scores, query_heads, preferred_element_type=jnp.float32
        ).reshape(slot_count, block_rows, width)
        value_part = jnp.einsum(
            "shqk,sqhd->skhd", weights_low, grad_heads, preferred_element_type=jnp.float32
        ).reshape(slot_count, block_rows, width)
        key_buffer = lax.dynamic_update_slice_in_dim(running[1], key_part, offset, 1)
        value_buffer = lax.dynamic_update_slice_in_dim(running[2], value_part, offset, 1)
        return ((grad_acc, key_buffer, value_buffer), None)

    start = (jnp.zeros(query_heads.shape, jnp.float32),)
    empty = jnp.zeros((slot_count, seq_span, width), jnp.float32)
    start = start + (empty, empty)
    result, _ = lax.scan(step, start, jnp.arange(blocks))
    return (result[0].reshape(query.shape), result[1:])


def sum_by_adapter(picks, terms):
    return jnp.einsum("si,sdkr->dikr", picks, terms, precision=lax.Precision.HIGHEST)


def on_device(
    tokens,
    cotangent,
    lengths,
    adapter_ids,
    attn_weight,
    fc1_weight,
    fc2_weight,
    vectors,
    fc1_bias,
    adapter_down,
    adapter_up,
    ff_adapters,
):
    slot_count, slot_rows, width = tokens.shape
    row_start = lax.axis_index("seq") * slot_rows
    positions = row_start + jnp.arange(slot_rows)
    live_rows = (positions[None, :] < lengths[:, None]).astype(jnp.float32)[..., None]
    matches = adapter_ids[:, None] == jnp.arange(ADAPTERS)[None, :]
    onehot_low = matches.astype(jnp.bfloat16)
    onehot_full = matches.astype(jnp.float32)
    gathered = (
        lax.all_gather(attn_weight, ("fsdp", "seq"), axis=0, tiled=True),
        lax.all_gather(fc1_weight, ("fsdp", "seq"), axis=0, tiled=True),
        lax.all_gather(fc2_weight, ("fsdp", "seq"), axis=0, tiled=True),
        lax.all_gather(vectors, ("fsdp", "seq"), axis=0, tiled=True),
        lax.all_gather(fc1_bias, ("fsdp", "seq"), axis=0, tiled=True),
        lax.all_gather(adapter_down, ("fsdp", "seq"), axis=0, tiled=True),
        lax.all_gather(adapter_up, ("fsdp", "seq"), axis=0, tiled=True),
        lax.all_gather(ff_adapters, ("fsdp", "seq"), axis=0, tiled=True),
    )
    attn_all, fc1_all, fc2_all, vector_cols, bias_ff, down_pick, up_pick, ff_pick = unpack(
        gathered, onehot_low
    )
    query_pre, inner_query = project(
        tokens, attn_all[:, 0, :], down_pick[:, :, 0], up_pick[:, :, 0]
    )
    query = ((query_pre + vector_cols[:, 0]) * 0.125).astype(jnp.bfloat16)
    key_pre, inner_key = project(tokens, attn_all[:, 1, :], down_pick[:, :, 1], up_pick[:, :, 1])
    keys = key_pre.astype(jnp.bfloat16)
    value_pre, inner_value = project(
        tokens, attn_all[:, 2, :], down_pick[:, :, 2], up_pick[:, :, 2]
    )
    values = (value_pre + vector_cols[:, 1]).astype(jnp.bfloat16)
    all_keys, all_values = (
        lax.all_gather(keys, "seq", axis=1, tiled=True),
        lax.all_gather(values, "seq", axis=1, tiled=True),
    )
    attended, logsum = attend(query, all_keys, all_values, lengths)
    mixed = attended.astype(jnp.bfloat16)
    branch_pre, inner_branch = project(
        mixed, attn_all[:, 3, :], down_pick[:, :, 3], up_pick[:, :, 3]
    )
    first_sum = tokens.astype(jnp.float32) + branch_pre + vector_cols[:, 2]
    normed, first_back = jax.vjp(
        partial(norm_rows, gain=vector_cols[:, 4], shift=vector_cols[:, 5]), first_sum
    )
    normed_low = normed.astype(jnp.bfloat16)
    hidden_pre, inner_hidden = project(normed_low, fc1_all, down_pick[:, :, 4], ff_pick[:, :, 0])
    activated, gelu_back = jax.vjp(gelu_exact, hidden_pre + bias_ff)
    activated_low = activated.astype(jnp.bfloat16)
    out_pre, inner_out = project(activated_low, fc2_all, ff_pick[:, :, 1], up_pick[:, :, 4])
    second = normed + out_pre + vector_cols[:, 3]
    final, second_back = jax.vjp(
        partial(norm_rows, gain=vector_cols[:, 6], shift=vector_cols[:, 7]), second
    )
    layer_out = (final * live_rows).astype(jnp.bfloat16)
    regathered = (
        lax.all_gather(attn_weight, ("fsdp", "seq"), axis=0, tiled=True),
        lax.all_gather(fc1_weight, ("fsdp", "seq"), axis=0, tiled=True),
        lax.all_gather(fc2_weight, ("fsdp", "seq"), axis=0, tiled=True),
        lax.all_gather(vectors, ("fsdp", "seq"), axis=0, tiled=True),
        lax.all_gather(fc1_bias, ("fsdp", "seq"), axis=0, tiled=True),
        lax.all_gather(adapter_down, ("fsdp", "seq"), axis=0, tiled=True),
        lax.all_gather(adapter_up, ("fsdp", "seq"), axis=0, tiled=True),
        lax.all_gather(ff_adapters, ("fsdp", "seq"), axis=0, tiled=True),
    )
    attn_all, fc1_all, fc2_all, vector_cols, bias_ff, down_pick, up_pick, ff_pick = unpack(
        regathered, onehot_low
    )
    grad_final = cotangent.astype(jnp.float32) * live_rows
    (grad_second,) = second_back(grad_final)
    grad_out_low = grad_second.astype(jnp.bfloat16)
    grad_activated, down_of_fc2, up_of_fc2 = project_back(
        activated_low, inner_out, grad_out_low, fc2_all, ff_pick[:, :, 1], up_pick[:, :, 4]
    )
    (grad_hidden,) = gelu_back(grad_activated)
    grad_hidden_low = grad_hidden.astype(jnp.bfloat16)
    grad_normed, down_of_fc1, up_of_fc1 = project_back(
        normed_low, inner_hidden, grad_hidden_low, fc1_all, down_pick[:, :, 4], ff_pick[:, :, 0]
    )
    (grad_first,) = first_back(grad_normed + grad_second)
    grad_branch_low = grad_first.astype(jnp.bfloat16)
    grad_mixed, down_of_out, up_of_out = project_back(
        mixed,
        inner_branch,
        grad_branch_low,
        attn_all[:, 3, :],
        down_pick[:, :, 3],
        up_pick[:, :, 3],
    )
    grad_mixed_low = grad_mixed.astype(jnp.bfloat16)
    row_delta = jnp.einsum(
        "sqhd,sqhd->shq", split_heads(grad_mixed_low.astype(jnp.float32)), split_heads(attended)
    )
    grad_query, parts = query_side(
        query, all_keys, all_values, grad_mixed_low, logsum, row_delta, lengths
    )
    grad_keys, grad_values = (
        lax.psum_scatter(
            parts[0].astype(jnp.bfloat16), "seq", scatter_dimension=1, tiled=True
        ).astype(jnp.float32),
        lax.psum_scatter(
            parts[1].astype(jnp.bfloat16), "seq", scatter_dimension=1, tiled=True
        ).astype(jnp.float32),
    )
    grad_query_low = grad_query.astype(jnp.bfloat16) * 0.125
    grad_keys_low = grad_keys.astype(jnp.bfloat16)
    grad_values_low = grad_values.astype(jnp.bfloat16)
    grad_from_query, down_of_query, up_of_query = project_back(
        tokens, inner_query, grad_query_low, attn_all[:, 0, :], down_pick[:, :, 0], up_pick[:, :, 0]
    )
    grad_from_key, down_of_key, up_of_key = project_back(
        tokens, inner_key, grad_keys_low, attn_all[:, 1, :], down_pick[:, :, 1], up_pick[:, :, 1]
    )
    grad_from_value, down_of_value, up_of_value = project_back(
        tokens,
        inner_value,
        grad_values_low,
        attn_all[:, 2, :],
        down_pick[:, :, 2],
        up_pick[:, :, 2],
    )
    input_grad = (grad_from_query + grad_from_key + grad_from_value + grad_first).astype(
        jnp.bfloat16
    )
    down_terms = jnp.stack(
        (down_of_query, down_of_key, down_of_value, down_of_out, down_of_fc1), axis=2
    )
    up_terms = jnp.stack((up_of_query, up_of_key, up_of_value, up_of_out, up_of_fc2), axis=2)
    ff_terms = jnp.stack((up_of_fc1, down_of_fc2), axis=2)
    down_table = sum_by_adapter(onehot_full, down_terms)
    up_table = sum_by_adapter(onehot_full, up_terms)
    ff_table = sum_by_adapter(onehot_full, ff_terms)
    down_grad, up_grad, ff_grad = (
        lax.psum_scatter(down_table, ("fsdp", "seq"), scatter_dimension=0, tiled=True),
        lax.psum_scatter(up_table, ("fsdp", "seq"), scatter_dimension=0, tiled=True),
        lax.psum_scatter(ff_table, ("fsdp", "seq"), scatter_dimension=0, tiled=True),
    )
    return (layer_out, input_grad, down_grad, up_grad, ff_grad)


MESH = pl.DeviceIdType.MESH
CHUNKS = 26
DEPTH = 8
ALL2, ALL4 = pl.ds(0, 2), pl.ds(0, 4)


class Spot:
    def __init__(self):
        self.y = lax.axis_index("fsdp")
        self.s = lax.axis_index("seq")
        self.z = self.s // 4
        self.x = (self.s // 2) % 2
        self.c = self.s % 2

    def at(self, dy=0, dz=0, dx=0, dc=0):
        y = (self.y + dy) % 2
        z = (self.z + dz) % 4
        x = (self.x + dx) % 2
        c = (self.c + dc) % 2
        return (y, (z * 2 + x) * 2 + c)


def enter(spot):
    barrier = pltpu.get_barrier_semaphore()
    for step in range(1, 16):
        peer = (spot.y, (spot.s + step) % 16)
        pl.semaphore_signal(barrier, inc=1, device_id=peer, device_id_type=MESH)
    pl.semaphore_signal(barrier, inc=1, device_id=spot.at(dy=1), device_id_type=MESH)
    pl.semaphore_wait(barrier, 16)


class Gather:
    def __init__(self, spot, parts, ways, others, send, recv):
        self.spot, self.parts, self.ways, self.others = spot, parts, ways, others
        self.send, self.recv = send, recv

    def block(self, k, dy=0, dz=0, dx=0, dc=0):
        p = self.spot
        places = ((p.y, dy, 2), (p.z, dz, 4), (p.x, dx, 2), (p.c, dc, 2))
        return self.parts[k].at[tuple((place + d) % n if isinstance(d, int) else d for place, d, n in places)]

    def copy(self, source, target, k, out, into, peer):
        return pltpu.make_async_remote_copy(
            src_ref=source,
            dst_ref=target,
            send_sem=self.send.at[k % DEPTH, out],
            recv_sem=self.recv.at[k % DEPTH, into],
            device_id=peer,
            device_id_type=MESH,
        )

    def push(self, ref, k, out, into, source=None, **hop):
        self.copy(ref if source is None else source, ref, k, out, into, self.spot.at(**hop)).start()

    def arrive(self, like, k, into):
        self.copy(like, like, k, 0, into, self.spot.at(dc=1)).wait_recv()

    def retire(self, k):
        if self.ways[k] == "z":
            pieces = ((1, 3, 1), (2, 3, 2), (2, 3, 2), (1, 4, 1))
        else:
            pieces = ((1, 1, 1), (2, 3, 1), (2, 4, 2), (2, 4, 1))
        for out, (ys, zs, xs) in enumerate(pieces):
            like = self.parts[k].at[pl.ds(0, ys), pl.ds(0, zs), pl.ds(0, xs), 0]
            self.copy(like, like, k, out, 0, self.spot.at(dc=1)).wait_send()

    def first(self, k):
        if k >= DEPTH:
            self.retire(k - DEPTH)
        if self.ways[k] == "z":
            for d in range(1, 4):
                self.push(self.block(k), k, 0, 0, dz=d)
        else:
            self.push(self.block(k), k, 0, 0, self.others.get(k), **{"d" + self.ways[k]: 1})

    def second(self, k):
        if self.ways[k] == "z":
            self.arrive(self.block(k, dz=pl.ds(0, 3)), k, 0)
            line = self.block(k, dz=ALL4)
            self.push(line, k, 1, 1, dx=1)
            self.push(line, k, 1, 2, dy=1)
            self.push(line, k, 1, 4, dc=1)
        else:
            self.arrive(self.block(k), k, 0)
            for d in range(1, 4):
                self.push(self.block(k, **{"d" + self.ways[k]: ALL2}), k, 1, 1, dz=d)

    def third(self, k):
        if self.ways[k] == "z":
            self.arrive(self.block(k, dz=ALL4), k, 1)
            self.push(self.block(k, dz=pl.ds(0, 2), dx=1), k, 2, 3, dy=1)
            self.arrive(self.block(k, dz=ALL4), k, 2)
            self.push(self.block(k, dz=pl.ds(2, 2), dy=1), k, 2, 3, dx=1)
            self.push(self.block(k, dz=ALL4, dx=1), k, 2, 4, dc=1)
            self.push(self.block(k, dz=ALL4, dy=1), k, 2, 4, dc=1)
        else:
            near, far = "d" + self.ways[k], "dy" if self.ways[k] == "x" else "dx"
            self.arrive(self.block(k, **{near: ALL2, "dz": pl.ds(0, 3)}), k, 1)
            plane = self.block(k, **{near: ALL2, "dz": ALL4})
            self.push(plane, k, 2, 2, **{far: 1})
            self.push(plane, k, 2, 4, dc=1)

    def fourth(self, k):
        if self.ways[k] == "z":
            self.arrive(self.block(k, dz=ALL4), k, 3)
            self.push(self.block(k, dz=ALL4, dx=1, dy=1), k, 3, 4, dc=1)
        else:
            near, far = "d" + self.ways[k], "dy" if self.ways[k] == "x" else "dx"
            self.arrive(self.block(k, **{near: ALL2, "dz": ALL4}), k, 2)
            self.push(self.block(k, **{near: ALL2, "dz": ALL4, far: 1}), k, 3, 4, dc=1)

    def ready(self, k):
        self.arrive(self.block(k, dy=ALL2, dz=ALL4, dx=ALL2), k, 4)

    def step(self, t):
        for late, move in enumerate((self.first, self.second, self.third, self.fourth, self.ready)):
            if 0 <= t - late < len(self.parts):
                move(t - late)

    def finish(self):
        for k in range(len(self.parts) - DEPTH, len(self.parts)):
            self.retire(k)


F32, BF16 = jnp.float32, jnp.bfloat16
ORDER = (0, 1, 24, 25) + tuple(range(2, 24))
WAYS = "zzyyzzzzzzzzzzzzzzzzzzzzzz"
EARLY, LATE = 80, 64


def dot(left, right):
    return jnp.dot(left, right, preferred_element_type=F32)


def dot_nt(left, right):
    return lax.dot_general(left, right, (((1,), (1,)), ((), ())), preferred_element_type=F32)


def dot_tn(left, right):
    return lax.dot_general(left, right, (((0,), (0,)), ((), ())), preferred_element_type=F32)


def lanes(shape):
    return lax.broadcasted_iota(jnp.int32, shape, len(shape) - 1)


def half(value, slot):
    low_half = lanes(value.shape) < HEAD
    zero = jnp.zeros_like(value)
    return jnp.where(low_half, value, zero) if slot == 0 else jnp.where(low_half, zero, value)


def pair(first, second):
    return jnp.where(lanes(first.shape) < HEAD, first, second)


def swap(value):
    return pltpu.roll(value, HEAD, 1)


def heads_to_rows(heads, rows, factor):
    for p in range(HEADS // 2):
        even = heads[2 * p].astype(F32) * factor
        odd = heads[2 * p + 1].astype(F32) * factor
        rows[0:64, p * 128 : p * 128 + 128] = pair(even, swap(odd)).astype(BF16)
        rows[64:128, p * 128 : p * 128 + 128] = pair(swap(even), odd).astype(BF16)


class Exchange:
    def __init__(self, spot, out, into, send, recv):
        self.spot, self.out, self.into, self.send, self.recv = spot, out, into, send, recv

    def copy(self, unit, source, target, block, peer):
        return pltpu.make_async_remote_copy(
            src_ref=source,
            dst_ref=target,
            send_sem=self.send.at[unit, block],
            recv_sem=self.recv.at[unit, self.spot.z],
            device_id=(self.spot.y, peer),
            device_id_type=MESH,
        )

    def start(self, unit, block):
        me = self.spot.s

        def body(i, carry):
            peer = block * 4 + i

            @pl.when(peer != me)
            def _():
                self.copy(unit, self.out.at[unit, peer], self.into.at[unit, me], block, peer).start()

            return carry

        lax.fori_loop(0, 4, body, 0)

    def keep(self, unit):
        self.into[unit, self.spot.s] = self.out[unit, self.spot.s]

    def like(self, unit, far):
        return self.into.at[unit, pl.ds(0, 4 if far else 3)]

    def wait_block(self, unit, far):
        block = (self.spot.z + far) % 4
        like = self.like(unit, far)
        pltpu.make_async_copy(like, like, self.recv.at[unit, block]).wait()

    def wait(self, unit):
        for far in range(4):
            self.wait_block(unit, far)

    def finish(self, units):
        for unit in range(units):
            for far in range(4):
                like = self.like(unit, far)
                pltpu.make_async_copy(like, like, self.send.at[unit, (self.spot.z + far) % 4]).wait()


class Scatter:
    def __init__(self, spot, wide, own, core_in, core_sum, x_in, x_sum, into, send, recv):
        self.spot, self.wide = spot, wide
        self.own, self.core_in, self.core_sum = own, core_in, core_sum
        self.x_in, self.x_sum, self.into = x_in, x_sum, into
        self.send, self.recv = send, recv

    def copy(self, source, target, route, peer):
        return pltpu.make_async_remote_copy(
            src_ref=source,
            dst_ref=target,
            send_sem=self.send.at[route],
            recv_sem=self.recv.at[route],
            device_id=peer,
            device_id_type=MESH,
        )

    def first(self):
        p = self.spot
        self.hop = self.copy(self.own.at[:, :, :, 1 - p.c], self.core_in, 0, p.at(dc=1))
        self.hop.start()

    def second(self):
        p = self.spot
        self.hop.wait()
        self.core_sum[...] = (self.own[:, :, :, p.c].astype(F32) + self.core_in[...].astype(F32)).astype(BF16)
        if not self.wide:
            self.hop = self.copy(self.core_sum.at[:, :, 1 - p.x], self.x_in, 1, p.at(dx=1))
            self.hop.start()

    def distances(self):
        every = [(dy, dz, dx) for dy in range(2) for dz in range(4) for dx in range(2 if self.wide else 1)]
        return every[1:]

    def third(self):
        p = self.spot
        if not self.wide:
            self.hop.wait()
            self.x_sum[...] = (self.core_sum[:, :, p.x].astype(F32) + self.x_in[...].astype(F32)).astype(BF16)
        for n, (dy, dz, dx) in enumerate(self.distances()):
            y, z, x = (p.y + dy) % 2, (p.z + dz) % 4, (p.x + dx) % 2
            source = self.core_sum.at[y, z, x] if self.wide else self.x_sum.at[y, z]
            self.copy(source, self.into.at[n], 2, p.at(dy=dy, dz=dz, dx=dx)).start()

    def fourth(self):
        p = self.spot
        self.copy(self.into, self.into, 2, p.at(dc=1)).wait()
        total = [self.core_sum[p.y, p.z, p.x] if self.wide else self.x_sum[p.y, p.z], None]
        total[0] = total[0].astype(F32)
        for n, (dy, _, _) in enumerate(self.distances()):
            term = self.into[n].astype(F32)
            total[dy] = term if total[dy] is None else total[dy] + term
        return total


def scatter_shapes(rows, wide):
    return [
        pltpu.VMEM((2, 4, 2, 2, rows, 128), BF16),
        pltpu.VMEM((2, 4, 2, rows, 128), BF16),
        pltpu.VMEM((2, 4, 2, rows, 128), BF16),
        pltpu.VMEM((2, 4, rows, 128), BF16),
        pltpu.VMEM((2, 4, rows, 128), BF16),
        pltpu.VMEM((15 if wide else 7, rows, 128), BF16),
        pltpu.SemaphoreType.DMA((3,)),
        pltpu.SemaphoreType.DMA((3,)),
    ]


def layer_kernel(*refs):
    it = iter(refs)

    def take(count):
        return [next(it) for _ in range(count)]

    attn, fc1, fc2, tok_far, cot_far, down_table, up_table, ff_table, vec_in, bias_in, lengths, ids = take(12)
    layer_out, input_grad, down_out, up_out, ff_out = take(5)
    wide, tall, rank_all, ff_all = take(4)
    rank_in, rank_up, rank_x, vec, ff_low, bias = take(6)
    heads_out, heads_in = take(2)
    weights_low, weights_back = take(2)
    attended, stat, tmp, sum_one, scaled_one, normed, grad_second, grad_first = take(8)
    tok, cot, mixed, normed_low, out_low, branch_low, query_low, key_low, value_low = take(9)
    slope, act, grad_hidden, inner4 = take(4)
    id_rows, table, rank_other, ff_other = take(4)
    early_refs, late_refs = take(8), take(8)
    own, send, recv, hsend, hrecv, id_sem = take(6)

    spot = Spot()
    here = (spot.y, spot.z, spot.x, spot.c)
    parts = [wide.at[k] for k in range(16)] + [tall.at[k] for k in range(8)] + [rank_all, ff_all]
    placed = []
    for k in range(8):
        placed.append(pltpu.make_async_copy(fc1.at[:, pl.ds(k * 512, 512)], parts[8 + k].at[here], own.at[0]))
        placed.append(pltpu.make_async_copy(fc2.at[:, pl.ds(k * 128, 128)], parts[16 + k].at[here], own.at[1]))
    tok_copy = pltpu.make_async_copy(tok_far, tok, own.at[2])
    cot_copy = pltpu.make_async_copy(cot_far, cot, own.at[3])
    tok_copy.start()
    for k in (0, 1):
        wide[(k,) + here] = attn[:, 0, k * 512 : k * 512 + 512]
    for copy in placed:
        copy.start()
    cot_copy.start()
    others = {2: rank_other, 3: ff_other}
    gather = Gather(spot, [parts[k] for k in ORDER], WAYS, others, send, recv)
    swaps = Exchange(spot, heads_out, heads_in, hsend, hrecv)
    early = Scatter(spot, False, *early_refs)
    late = Scatter(spot, True, *late_refs)
    first_row = lax.broadcasted_iota(jnp.int32, (8, 128), 0) == 0
    id_rows[spot.y] = jnp.where(first_row, ids[0], ids[1])
    enter(spot)
    gather.step(0)
    id_copy = pltpu.make_async_remote_copy(
        src_ref=id_rows.at[spot.y],
        dst_ref=id_rows.at[spot.y],
        send_sem=id_sem.at[0],
        recv_sem=id_sem.at[1],
        device_id=spot.at(dy=1),
        device_id_type=MESH,
    )
    id_copy.start()
    for j in range(1, 4):
        for k in range(2):
            wide[(2 * j + k,) + here] = attn[:, j, k * 512 : k * 512 + 512]

    def chosen(source, kind, y, slot):
        who = id_rows[y, slot : slot + 1, 0 : source.shape[3]]
        total = None
        for a in range(ADAPTERS):
            term = jnp.where(who == a, source[a, kind].astype(F32), 0.0)
            total = term if total is None else total + term
        return total

    def pick_all():
        table[...] = jnp.zeros_like(table)
        for g in range(2):
            y = (spot.y + g) % 2
            for slot in range(2):
                for j in range(4):
                    row = g * 384 + j * 32 + slot * 16
                    table[row : row + 16, 0:32] = chosen(down_table, j, y, slot)
                    table[row + 128 : row + 144, 0:32] = chosen(up_table, j, y, slot)
                row = g * 384 + 256 + slot * 16
                table[row : row + 16, 0:32] = chosen(down_table, 4, y, slot)
                table[row + 32 : row + 48, 0:32] = chosen(up_table, 4, y, slot)
                for kind in range(2):
                    row = 768 + g * 64 + kind * 32 + slot * 16
                    table[row : row + 16, :] = chosen(ff_table, kind, y, slot)
        for n in range(3):
            cols = slice(n * 128, n * 128 + 128)
            rank_all[here + (slice(None), cols)] = table[cols, :].T[0:32].astype(BF16)
            rank_other[:, cols] = table[384 + n * 128 : 512 + n * 128, :].T[0:32].astype(BF16)
        turned = table[768:896, :].T
        ff_all[here + (slice(0, 64),)] = pair(turned[0:64], swap(turned[64:128])).astype(BF16)
        ff_other[0:64] = pair(swap(turned[0:64]), turned[64:128]).astype(BF16)
        table[0:8, 0:32] = vec_in[...].astype(F32)
        table[0:8, 32:128] = jnp.zeros((8, 96), F32)
        columns = pltpu.roll(table[0:8, :], (spot.s % 4) * 32, 1)
        rows = jnp.concatenate([jnp.broadcast_to(bias_in[...].astype(F32), (8, 128)), columns], axis=0)
        ff_all[here + (slice(64, 80),)] = rows.astype(BF16)
        ff_other[64:80] = rows.astype(BF16)

    lane = lanes((128, 128))
    row_slot = lax.broadcasted_iota(jnp.int32, (128, 128), 0) >= 64
    slot_lane = ((lane & 16) != 0) == row_slot
    kind4 = [slot_lane & ((lane >> 5) == j) for j in range(4)]
    kind_ff = [slot_lane & ((lane >> 5) == k) for k in range(2)]

    def only(mask, value):
        return jnp.where(mask, value, jnp.zeros_like(value))

    def square(k, t):
        halves = [wide[2 * k + i, t // 2, pl.ds((t % 2) * 2, 2)].reshape(256, 512) for i in range(2)]
        return jnp.concatenate(halves, axis=1)

    def columns(k, n):
        return wide[2 * k + n // 2, :, :, :, :, :, tile(n % 2)].reshape(1024, 256)

    def tile(n, size=256):
        return pl.ds(pl.multiple_of(n * size, size), size)

    def unpack_rank():
        rank_in[...] = rank_all[:, :, :, :, :, 0:128].reshape(1024, 128)
        rank_up[...] = rank_all[:, :, :, :, :, 128:256].reshape(1024, 128)
        rank_x[...] = rank_all[:, :, :, :, :, 256:384].reshape(1024, 128)

    def ff_rows(first, count):
        return ff_low[pl.ds(first, count)].reshape(count * 128, 128)

    def unpack_ff():
        columns_of = {}
        packed = ff_all[:, :, :, :, 0:64, :].reshape(32, 64, 128)
        ff_low[:, 0] = packed
        ff_low[:, 1] = swap(packed.astype(F32).reshape(2048, 128)).astype(BF16).reshape(32, 64, 128)
        for o in range(32):
            y, z, x, c = o // 16, (o // 4) % 4, (o // 2) % 2, o % 2
            rows = ff_all[y, z, x, c, 64:80, :].astype(F32)
            bias[:, o * 128 : o * 128 + 128] = rows[0:8]
            columns_of[o // 4] = rows[8:16] if o % 4 == 0 else columns_of[o // 4] + rows[8:16]
        for n in range(8):
            vec[:, n * 128 : n * 128 + 128] = columns_of[n]

    def to_heads(unit, block, value):
        for p in range(2):
            first = value[0:64, p * 128 : p * 128 + 128]
            second = value[64:128, p * 128 : p * 128 + 128]
            heads_out[unit, block * 4 + 2 * p] = pair(first, swap(second)).astype(BF16)
            heads_out[unit, block * 4 + 2 * p + 1] = pair(swap(first), second).astype(BF16)
        swaps.start(unit, block)

    def turn(body):
        def shifted(t, carry):
            body((spot.z + t) % 4)
            return carry

        lax.fori_loop(0, 4, shifted, 0)

    def project_in(j):
        inner = only(kind4[j], inner4[...])

        def body(n):
            cols = tile(n)
            value = dot(tok[...], columns(j, n)) + dot_nt(inner, rank_up[cols, :])
            if j == 0:
                value = (value + vec[0:1, cols]) * 0.125
            if j == 2:
                value = value + vec[1:2, cols]
            to_heads(j, n, value)

        turn(body)
        swaps.keep(j)

    def attention(t):
        if t == 0:
            for j in range(3):
                swaps.wait(j)
        block = (spot.z + t) % 4
        keys = heads_in[1].reshape(1024, 128)
        values = heads_in[2].reshape(1024, 128)
        rows = tile(block)
        query = heads_in[0, pl.ds(block * 4, 4)].reshape(256, 128)
        results, stats = [], []
        for slot in range(2):
            scores = dot_nt(half(query, slot), keys)
            scores = jnp.where(lanes(scores.shape) < lengths[slot], scores, NEG_FILL)
            top = jnp.max(scores, axis=-1, keepdims=True)
            shifted = jnp.exp(scores - top)
            total = jnp.sum(shifted, axis=-1, keepdims=True)
            low = (shifted * (1.0 / total)).astype(BF16)
            weights_low[slot, rows, :] = low
            results.append(dot(low, values))
            stats.append(jnp.broadcast_to(top + jnp.log(total), (256, 128)))
        result = pair(results[0], results[1])
        attended[rows, :] = result
        heads_out[3, pl.ds(block * 4, 4)] = result.astype(BF16).reshape(4, 64, 128)
        stat[rows, :] = pair(stats[0], stats[1])
        swaps.start(3, block)
        if t == 3:
            swaps.keep(3)

    def attention_turned(first):
        logsum = stat[...].T
        queries = heads_in[0].reshape(1024, 128)
        turned = [logsum[0:1], logsum[64:65]]

        def body(t, carry):
            rows = tile(t)
            keys = heads_in[1, pl.ds(t * 4, 4)].reshape(256, 128)
            for slot in range(2):
                scores = dot_nt(half(keys, slot), queries)
                weights = jnp.exp(scores - turned[slot])
                place = lax.broadcasted_iota(jnp.int32, weights.shape, 0) + t * 256
                weights = jnp.where(place < lengths[slot], weights, 0.0)
                weights_back[slot, rows, :] = weights.astype(BF16)
            return carry

        lax.fori_loop(first, first + 2, body, 0)

    def normalize(value):
        centered = value - jnp.mean(value, axis=-1, keepdims=True)
        spread = lax.rsqrt(jnp.mean(centered * centered, axis=-1, keepdims=True) + NORM_EPS)
        return centered * spread, spread

    def normalize_back(grad, scaled, spread):
        shift = jnp.mean(grad, axis=-1, keepdims=True)
        along = jnp.mean(grad * scaled, axis=-1, keepdims=True)
        return spread * (grad - shift - scaled * along)

    saved = {}

    def branch():
        swaps.wait(3)
        heads_to_rows(heads_in.at[3], mixed, 1.0)
        saved["o"] = only(kind4[3], dot(mixed[...], rank_in[...])).astype(BF16)

        def body(n, carry):
            cols = tile(n)
            value = dot(mixed[...], columns(3, n)) + dot_nt(saved["o"], rank_up[cols, :])
            sum_one[:, cols] = tok[:, cols].astype(F32) + value + vec[2:3, cols]
            return carry

        lax.fori_loop(0, 4, body, 0)
        scaled, saved["spread_one"] = normalize(sum_one[...])
        scaled_one[...] = scaled
        value = scaled * vec[4:5] + vec[5:6]
        normed[...] = value
        normed_low[...] = value.astype(BF16)
        saved["hidden"] = only(kind_ff[0], dot(normed_low[...], rank_x[...])).astype(BF16)

    def expand(k):
        def body(i, carry):
            n = k * 2 + i
            cols = tile(n)
            value = dot(normed_low[...], wide[8 + k, :, :, :, :, :, tile(i)].reshape(1024, 256))
            value = value + dot_nt(saved["hidden"], ff_rows(n * 2, 2)) + bias[0:1, cols]
            share = 0.5 * (1.0 + lax.erf(value * math.sqrt(0.5)))
            act[:, cols] = (value * share).astype(BF16)
            bell = jnp.exp(-0.5 * value * value) * (1.0 / math.sqrt(2.0 * math.pi))
            slope[:, cols] = share + value * bell
            return carry

        lax.fori_loop(0, 2, body, 0)

    def contract(q):
        if q == 0:
            saved["out"] = only(kind_ff[1], dot(act[...], ff_rows(0, 32))).astype(BF16)
        cols = slice(q * 256, q * 256 + 256)
        weight = jnp.concatenate([tall[2 * q + i].reshape(4096, 128) for i in range(2)], axis=1)
        value = dot(act[...], weight) + dot_nt(saved["out"], rank_x[cols, :])
        tmp[:, cols] = normed[:, cols] + value + vec[3:4, cols]

    def outer():
        rows = lax.broadcasted_iota(jnp.int32, (128, 1), 0)
        place = spot.s * 64 + (rows & 63)
        limit = jnp.where(rows < 64, lengths[0], lengths[1])
        live = (place < limit).astype(F32)
        scaled, spread = normalize(tmp[...])
        layer_out[...] = (live * (scaled * vec[6:7] + vec[7:8])).astype(BF16)
        grad = normalize_back(live * cot[...].astype(F32) * vec[6:7], scaled, spread)
        grad_second[...] = grad
        out_low[...] = grad.astype(BF16)
        saved["g_out"] = only(kind_ff[1], dot(out_low[...], rank_x[...])).astype(BF16)

    def hidden_back():
        def body(t, carry):
            rows = tile(t, 512)
            value = dot_nt(saved["g_out"], ff_rows(t * 4, 4))
            for q in range(4):
                pieces = [tall[2 * q + i, t // 4, t % 4].reshape(512, 128) for i in range(2)]
                piece = jnp.concatenate(pieces, axis=1)
                value = value + dot_nt(out_low[:, q * 256 : q * 256 + 256], piece)
            grad_hidden[:, rows] = (value * slope[:, rows]).astype(BF16)
            return carry

        lax.fori_loop(0, 8, body, 0)
        saved["g_hidden"] = only(kind_ff[0], dot(grad_hidden[...], ff_rows(0, 32))).astype(BF16)

    def normed_back():
        def body(t, carry):
            rows = tile(t)
            value = dot_nt(saved["g_hidden"], rank_x[rows, :]) + grad_second[:, rows]
            for q in range(4):
                value = value + dot_nt(grad_hidden[:, q * 1024 : q * 1024 + 1024], square(4 + q, t))
            tmp[:, rows] = value
            return carry

        lax.fori_loop(0, 4, body, 0)
        grad = normalize_back(tmp[...] * vec[4:5], scaled_one[...], saved["spread_one"])
        grad_first[...] = grad
        branch_low[...] = grad.astype(BF16)
        saved["g_o"] = only(kind4[3], dot(branch_low[...], rank_up[...])).astype(BF16)

    def mixed_back():
        def body(n):
            value = dot_nt(branch_low[...], square(3, n)) + dot_nt(saved["g_o"], rank_in[tile(n), :])
            to_heads(4, n, value)

        turn(body)
        swaps.keep(4)

    def early_grads():
        own_grads = early.own
        value = dot_tn(normed_low[...], saved["g_hidden"]) + dot_tn(out_low[...], saved["out"])
        value = value.reshape(32, 2, 16, 128)
        value = value[:, 0] + swap(value[:, 1].reshape(512, 128)).reshape(32, 16, 128)
        own_grads[:, :, :, :, 0:16, :] = value.astype(BF16).reshape(2, 4, 2, 2, 16, 128)
        for y in range(2):
            for z in range(4):
                cols = slice((y * 4 + z) * 512, (y * 4 + z) * 512 + 512)
                value = dot_tn(grad_hidden[:, cols], saved["hidden"]) + dot_tn(act[:, cols], saved["g_out"])
                value = value.reshape(4, 128, 128)
                for o in range(4):
                    packed = value[o, 0:64] + swap(value[o, 64:128])
                    own_grads[y, z, o // 2, o % 2, 16:80, :] = packed.astype(BF16)

    def query_back(t):
        block = (spot.z + 4 - t) % 4
        swaps.wait_block(4, (4 - t) % 4)
        rows = tile(block)
        keys = heads_in[1].reshape(1024, 128)
        values = heads_in[2].reshape(1024, 128)
        grad_block = heads_in[4, pl.ds(block * 4, 4)].reshape(256, 128)
        product = grad_block.astype(F32) * attended[rows, :]
        parts_, deltas = [], []
        for slot in range(2):
            delta = jnp.sum(half(product, slot), axis=-1, keepdims=True)
            grad_probs = dot_nt(half(grad_block, slot), values)
            weights = weights_low[slot, rows, :].astype(F32)
            grad_scores = (weights * (grad_probs - delta)).astype(BF16)
            parts_.append(dot(grad_scores, keys))
            deltas.append(jnp.broadcast_to(delta, (256, 128)))
        heads_out[5, pl.ds(block * 4, 4)] = pair(*parts_).astype(BF16).reshape(4, 64, 128)
        stat[rows, :] = pair(*deltas)
        swaps.start(5, block)
        if t == 3:
            swaps.keep(5)

    def key_back():
        queries = heads_in[0].reshape(1024, 128)
        grads = heads_in[4].reshape(1024, 128)
        turned = stat[...].T
        turned = [turned[0:1], turned[64:65]]

        def body(block):
            rows = tile(block)
            value_block = heads_in[2, pl.ds(block * 4, 4)].reshape(256, 128)
            key_parts, value_parts = [], []
            for slot in range(2):
                weights = weights_back[slot, rows, :]
                grad_probs = dot_nt(half(value_block, slot), grads)
                grad_scores = (weights.astype(F32) * (grad_probs - turned[slot])).astype(BF16)
                key_parts.append(dot(grad_scores, queries))
                value_parts.append(dot(weights, grads))
            heads_out[6, pl.ds(block * 4, 4)] = pair(*key_parts).astype(BF16).reshape(4, 64, 128)
            heads_out[7, pl.ds(block * 4, 4)] = pair(*value_parts).astype(BF16).reshape(4, 64, 128)
            swaps.start(6, block)
            swaps.start(7, block)

        turn(body)
        swaps.keep(6)
        swaps.keep(7)

    def inputs_back():
        swaps.wait(5)
        heads_to_rows(heads_in.at[5], query_low, 0.125)
        swaps.wait(6)
        heads_to_rows(heads_in.at[6], key_low, 1.0)
        swaps.wait(7)
        heads_to_rows(heads_in.at[7], value_low, 1.0)
        grads = (query_low, key_low, value_low)
        inner = jnp.zeros((128, 128), F32)
        for j in range(3):
            inner = jnp.where(kind4[j], dot(grads[j][...], rank_up[...]), inner)
        saved["g_in"] = inner.astype(BF16)
        value = dot_tn(tok[...], saved["g_in"]) + dot_tn(mixed[...], saved["g_o"])
        late.own[:, :, :, :, 0:32, :] = value.astype(BF16).reshape(2, 4, 2, 2, 32, 128)
        value = dot_tn(branch_low[...], saved["o"])
        for j in range(3):
            value = value + dot_tn(grads[j][...], only(kind4[j], inner4[...]))
        late.own[:, :, :, :, 32:64, :] = value.astype(BF16).reshape(2, 4, 2, 2, 32, 128)

    def tokens_back(t):
        rows = pl.ds(t * 256, 256)
        value = dot_nt(saved["g_in"], rank_in[rows, :]) + grad_first[:, rows]
        for j, grad in enumerate((query_low, key_low, value_low)):
            value = value + dot_nt(grad[...], square(j, t))
        input_grad[:, rows] = value.astype(BF16)

    def results(early_sum, late_sum):
        turned, ff_turned = [], []
        for dy in range(2):
            cross = jnp.concatenate([early_sum[dy][0:16], swap(early_sum[dy][0:16])], axis=0)
            table[0:64, :] = late_sum[dy]
            table[64:96, :] = cross
            table[96:128, :] = jnp.zeros((32, 128), F32)
            turned.append(table[0:128, :].T)
            packed = early_sum[dy][16:80]
            ff_turned.append(jnp.concatenate([packed, swap(packed)], axis=0).T)
        for a in range(ADAPTERS):
            who = [id_rows[(spot.y + dy) % 2, 0:2, :] == a for dy in range(2)]
            share = [match.astype(F32) for match in who]

            def gathered(source, first):
                total = None
                for dy in range(2):
                    for s in range(2):
                        row = first + s * 16
                        term = share[dy][s : s + 1] * source[dy][row : row + 16, :]
                        total = term if total is None else total + term
                return total

            for j in range(4):
                value = gathered(turned, j * 32)
                down_out[a, j] = value[:, 0:32]
                up_out[a, j] = value[:, 32:64]
            down_out[a, 4] = gathered(turned, 0)[:, 64:96]
            up_out[a, 4] = gathered(turned, 32)[:, 64:96]
            for kind in range(2):
                ff_out[a, kind] = gathered(ff_turned, kind * 32)

    for t in range(1, CHUNKS + 4):
        if t == 2:
            id_copy.wait_recv()
            pick_all()
        if t == 4:
            for n, like in enumerate((wide.at[(pl.ds(8, 8),) + here], tall.at[(pl.ds(0, 8),) + here])):
                pltpu.make_async_copy(like, like, own.at[n]).wait()
        gather.step(t)
        if t == 7:
            tok_copy.wait()
            unpack_rank()
            unpack_ff()
            inner4[...] = dot(tok[...], rank_in[...]).astype(BF16)
        if t in (7, 9, 11):
            project_in((t - 7) // 2)
        if 14 <= t <= 17:
            attention(t - 14)
        if 18 <= t <= 19:
            attention_turned((t - 18) * 2)
        if t == 20:
            branch()
        if 21 <= t <= 24:
            expand(2 * t - 42)
            expand(2 * t - 41)
        if t == 27:
            contract(0)
        if t >= 27:
            contract(t - 26)
    cot_copy.wait()
    outer()
    hidden_back()
    normed_back()
    mixed_back()
    early_grads()
    early.first()
    for t in range(4):
        query_back(t)
    early.second()
    key_back()
    early.third()
    inputs_back()
    late.first()
    tokens_back(0)
    late.second()
    late.third()
    for t in range(1, 4):
        tokens_back(t)
    results(early.fourth(), late.fourth())
    id_copy.wait_send()
    gather.finish()
    swaps.finish(8)


def hand_on_kernel(*refs):
    count = len(refs) // 2
    for k in range(count):
        refs[count + k][...] = refs[k][...]


def hand_on(arrays):
    near = pl.BlockSpec(memory_space=pltpu.VMEM)
    return pl.pallas_call(
        hand_on_kernel,
        out_shape=[jax.ShapeDtypeStruct(array.shape, array.dtype) for array in arrays],
        in_specs=[near] * len(arrays),
        out_specs=[near] * len(arrays),
        name="hand_on",
    )(*arrays)


def layer(attn, fc1, fc2, tok, cot, down, up, ff, vec, bias, lengths, ids):
    lead = (2, 4, 2, 2)
    anywhere = pl.BlockSpec(memory_space=pl.ANY)
    near = pl.BlockSpec(memory_space=pltpu.VMEM)
    scalar = pl.BlockSpec(memory_space=pltpu.SMEM)

    def buffer(*shape, dtype=BF16):
        return pltpu.VMEM(shape, dtype)

    scratch = [
        buffer(16, *lead, 32, 512),
        buffer(8, *lead, 128, 128),
        buffer(*lead, 32, 384),
        buffer(*lead, 80, 128),
    ]
    scratch += [buffer(1024, 128)] * 3 + [buffer(8, 1024, dtype=F32), buffer(32, 2, 64, 128)]
    scratch += [buffer(8, 4096, dtype=F32)]
    scratch += [buffer(8, 16, 64, 128)] * 2
    scratch += [buffer(2, 1024, 1024)] * 2
    scratch += [buffer(1024, 128, dtype=F32)] * 2
    scratch += [buffer(128, 1024, dtype=F32)] * 6
    scratch += [buffer(128, 1024)] * 9
    scratch += [buffer(128, 4096, dtype=F32), buffer(128, 4096), buffer(128, 4096), buffer(128, 128)]
    scratch += [buffer(2, 8, 128, dtype=jnp.int32), buffer(896, 128, dtype=F32)]
    scratch += [buffer(32, 384), buffer(80, 128)]
    scratch += scatter_shapes(EARLY, False) + scatter_shapes(LATE, True)
    scratch += [pltpu.SemaphoreType.DMA((4,))]
    scratch += [pltpu.SemaphoreType.DMA((DEPTH, 4)), pltpu.SemaphoreType.DMA((DEPTH, 5))]
    scratch += [pltpu.SemaphoreType.DMA((8, 4))] * 2
    scratch += [pltpu.SemaphoreType.DMA((2,))]
    return pl.pallas_call(
        layer_kernel,
        out_shape=[
            jax.ShapeDtypeStruct(tok.shape, BF16),
            jax.ShapeDtypeStruct(tok.shape, BF16),
            jax.ShapeDtypeStruct(down.shape, F32),
            jax.ShapeDtypeStruct(up.shape, F32),
            jax.ShapeDtypeStruct(ff.shape, F32),
        ],
        in_specs=[near] + [anywhere] * 4 + [near] * 5 + [scalar] * 2,
        out_specs=[near] * 5,
        scratch_shapes=scratch,
        compiler_params=pltpu.CompilerParams(
            collective_id=0, has_side_effects=True, vmem_limit_bytes=63 * 2**20
        ),
        name="layer",
    )(attn, fc1, fc2, tok, cot, down, up, ff, vec, bias, lengths, ids)


def fast_device(
    tokens,
    cotangent,
    lengths,
    adapter_ids,
    attn_weight,
    fc1_weight,
    fc2_weight,
    vectors,
    fc1_bias,
    adapter_down,
    adapter_up,
    ff_adapters,
):
    width = tokens.shape[2]
    outs = layer(
        attn_weight,
        fc1_weight,
        fc2_weight,
        tokens.reshape(-1, width),
        cotangent.reshape(-1, width),
        adapter_down.transpose(1, 2, 3, 0),
        adapter_up.transpose(1, 2, 3, 0),
        ff_adapters.transpose(1, 2, 3, 0),
        vectors.T,
        fc1_bias[None],
        lengths,
        adapter_ids,
    )
    outs = hand_on(outs)
    grads = [grad.transpose(3, 0, 1, 2) for grad in outs[2:]]
    return (outs[0].reshape(tokens.shape), outs[1].reshape(tokens.shape), *grads)


def solution(mesh):
    in_specs = (
        P("fsdp", "seq", None),
        P("fsdp", "seq", None),
        P("fsdp"),
        P("fsdp"),
        P(("fsdp", "seq"), None, None),
        P(("fsdp", "seq"), None),
        P(("fsdp", "seq"), None),
        P(("fsdp", "seq"), None),
        P(("fsdp", "seq")),
        P(("fsdp", "seq"), None, None, None),
        P(("fsdp", "seq"), None, None, None),
        P(("fsdp", "seq"), None, None, None),
    )
    out_specs = (
        P("fsdp", "seq", None),
        P("fsdp", "seq", None),
        P(("fsdp", "seq"), None, None, None),
        P(("fsdp", "seq"), None, None, None),
        P(("fsdp", "seq"), None, None, None),
    )
    fast = mesh.shape["fsdp"] == 2 and mesh.shape["seq"] == HEADS
    return jax.shard_map(
        fast_device if fast else on_device, mesh=mesh, in_specs=in_specs, out_specs=out_specs, check_vma=False
    )
```

```python
from functools import partial
import math

import jax
import jax.numpy as jnp
from jax import lax
from jax.experimental import pallas as pl
from jax.experimental.pallas import tpu as pltpu
from jax.sharding import PartitionSpec as P

HEADS = 16
HEAD = 64
ADAPTERS = 8


NEG_FILL = -1e30
NORM_EPS = 1e-05


def split_heads(values_in):
    return values_in.reshape(values_in.shape[:-1] + (HEADS, HEAD))


def norm_rows(value, gain, shift):
    centered = value - jnp.mean(value, axis=-1, keepdims=True)
    scaled = centered * lax.rsqrt(jnp.mean(centered * centered, axis=-1, keepdims=True) + NORM_EPS)
    return scaled * gain + shift


def gelu_exact(value):
    return jax.nn.gelu(value, approximate=False)


def choose(onehot, table):
    return jnp.einsum("si,dikr->sdkr", onehot, table, preferred_element_type=jnp.float32).astype(
        jnp.bfloat16
    )


def unpack(gathered, onehot):
    attn_all, fc1_all, fc2_all, vector_all, bias_ff, down_all, up_all, ff_all = gathered
    return (
        attn_all,
        fc1_all,
        fc2_all,
        vector_all.astype(jnp.float32),
        bias_ff.astype(jnp.float32),
        choose(onehot, down_all),
        choose(onehot, up_all),
        choose(onehot, ff_all),
    )


def project(inputs, weight, down_table, up_table):
    frozen_part = jnp.einsum("spd,de->spe", inputs, weight, preferred_element_type=jnp.float32)
    inner_low = jnp.einsum(
        "spd,sdr->spr", inputs, down_table, preferred_element_type=jnp.float32
    ).astype(jnp.bfloat16)
    return (
        frozen_part
        + jnp.einsum("spr,ser->spe", inner_low, up_table, preferred_element_type=jnp.float32),
        inner_low,
    )


def project_back(inputs, inner_low, grad_out, weight, down_table, up_table):
    grad_inner = jnp.einsum(
        "spe,ser->spr", grad_out, up_table, preferred_element_type=jnp.float32
    ).astype(jnp.bfloat16)
    grad_in = jnp.einsum("spe,de->spd", grad_out, weight, preferred_element_type=jnp.float32)
    grad_in = grad_in + jnp.einsum(
        "spr,sdr->spd", grad_inner, down_table, preferred_element_type=jnp.float32
    )
    grad_up = jnp.einsum("spe,spr->ser", grad_out, inner_low, preferred_element_type=jnp.float32)
    grad_down = jnp.einsum("spd,spr->sdr", inputs, grad_inner, preferred_element_type=jnp.float32)
    return (grad_in, grad_down, grad_up)


def block_scores(query_heads, key_block, key_start, lengths):
    block_rows = key_block.shape[1]
    scores = jnp.einsum(
        "sqhd,skhd->shqk", query_heads, split_heads(key_block), preferred_element_type=jnp.float32
    )
    valid_keys = (key_start + jnp.arange(block_rows))[None, :] < lengths[:, None]
    return jnp.where(valid_keys[:, None, None, :], scores, NEG_FILL)


def score_grads(scores, logsum, row_delta, grad_heads, value_heads):
    probs = jnp.exp(scores - logsum[..., None])
    grad_probs = jnp.einsum(
        "sqhd,skhd->shqk", grad_heads, value_heads, preferred_element_type=jnp.float32
    )
    grad_scores = (probs * (grad_probs - row_delta[..., None])).astype(jnp.bfloat16)
    return (grad_scores, probs.astype(jnp.bfloat16))


def attend(query, all_keys, all_values, lengths):
    seq_span = all_keys.shape[1]
    block_rows = math.gcd(seq_span, 512)
    blocks = seq_span // block_rows
    query_heads = split_heads(query)
    slot_count, query_rows = (query.shape[0], query.shape[1])
    stats_shape = (slot_count, HEADS, query_rows)

    def stats_step(running, step_index):
        row_top, row_total = running
        offset = step_index * block_rows
        scores = block_scores(
            query_heads, lax.dynamic_slice_in_dim(all_keys, offset, block_rows, 1), offset, lengths
        )
        new_top = jnp.maximum(row_top, jnp.max(scores, axis=-1))
        row_total = row_total * jnp.exp(row_top - new_top) + jnp.sum(
            jnp.exp(scores - new_top[..., None]), axis=-1
        )
        return ((new_top, row_total), None)

    start_top = jnp.full(stats_shape, NEG_FILL, jnp.float32)
    (row_top, row_total), _ = lax.scan(
        stats_step, (start_top, jnp.zeros(stats_shape, jnp.float32)), jnp.arange(blocks)
    )
    logsum = row_top + jnp.log(row_total)

    def mix_step(running, step_index):
        offset = step_index * block_rows
        scores = block_scores(
            query_heads, lax.dynamic_slice_in_dim(all_keys, offset, block_rows, 1), offset, lengths
        )
        weights_low = jnp.exp(scores - logsum[..., None]).astype(jnp.bfloat16)
        value_heads = split_heads(lax.dynamic_slice_in_dim(all_values, offset, block_rows, 1))
        return (
            running
            + jnp.einsum(
                "shqk,skhd->sqhd", weights_low, value_heads, preferred_element_type=jnp.float32
            ),
            None,
        )

    mixed_heads, _ = lax.scan(
        mix_step, jnp.zeros(query_heads.shape, jnp.float32), jnp.arange(blocks)
    )
    return (mixed_heads.reshape(query.shape), logsum)


def query_side(query, all_keys, all_values, grad_low, logsum, row_delta, lengths):
    seq_span = all_keys.shape[1]
    block_rows = math.gcd(seq_span, 512)
    blocks = seq_span // block_rows
    query_heads = split_heads(query)
    grad_heads = split_heads(grad_low)
    slot_count = query.shape[0]
    width = query.shape[2]

    def step(running, step_index):
        offset = step_index * block_rows
        key_block = lax.dynamic_slice_in_dim(all_keys, offset, block_rows, 1)
        value_block = lax.dynamic_slice_in_dim(all_values, offset, block_rows, 1)
        scores = block_scores(query_heads, key_block, offset, lengths)
        grad_scores, weights_low = score_grads(
            scores, logsum, row_delta, grad_heads, split_heads(value_block)
        )
        grad_acc = running[0] + jnp.einsum(
            "shqk,skhd->sqhd",
            grad_scores,
            split_heads(key_block),
            preferred_element_type=jnp.float32,
        )
        key_part = jnp.einsum(
            "shqk,sqhd->skhd", grad_scores, query_heads, preferred_element_type=jnp.float32
        ).reshape(slot_count, block_rows, width)
        value_part = jnp.einsum(
            "shqk,sqhd->skhd", weights_low, grad_heads, preferred_element_type=jnp.float32
        ).reshape(slot_count, block_rows, width)
        key_buffer = lax.dynamic_update_slice_in_dim(running[1], key_part, offset, 1)
        value_buffer = lax.dynamic_update_slice_in_dim(running[2], value_part, offset, 1)
        return ((grad_acc, key_buffer, value_buffer), None)

    start = (jnp.zeros(query_heads.shape, jnp.float32),)
    empty = jnp.zeros((slot_count, seq_span, width), jnp.float32)
    start = start + (empty, empty)
    result, _ = lax.scan(step, start, jnp.arange(blocks))
    return (result[0].reshape(query.shape), result[1:])


def sum_by_adapter(picks, terms):
    return jnp.einsum("si,sdkr->dikr", picks, terms, precision=lax.Precision.HIGHEST)


def on_device(
    tokens,
    cotangent,
    lengths,
    adapter_ids,
    attn_weight,
    fc1_weight,
    fc2_weight,
    vectors,
    fc1_bias,
    adapter_down,
    adapter_up,
    ff_adapters,
):
    slot_count, slot_rows, width = tokens.shape
    row_start = lax.axis_index("seq") * slot_rows
    positions = row_start + jnp.arange(slot_rows)
    live_rows = (positions[None, :] < lengths[:, None]).astype(jnp.float32)[..., None]
    matches = adapter_ids[:, None] == jnp.arange(ADAPTERS)[None, :]
    onehot_low = matches.astype(jnp.bfloat16)
    onehot_full = matches.astype(jnp.float32)
    gathered = (
        lax.all_gather(attn_weight, ("fsdp", "seq"), axis=0, tiled=True),
        lax.all_gather(fc1_weight, ("fsdp", "seq"), axis=0, tiled=True),
        lax.all_gather(fc2_weight, ("fsdp", "seq"), axis=0, tiled=True),
        lax.all_gather(vectors, ("fsdp", "seq"), axis=0, tiled=True),
        lax.all_gather(fc1_bias, ("fsdp", "seq"), axis=0, tiled=True),
        lax.all_gather(adapter_down, ("fsdp", "seq"), axis=0, tiled=True),
        lax.all_gather(adapter_up, ("fsdp", "seq"), axis=0, tiled=True),
        lax.all_gather(ff_adapters, ("fsdp", "seq"), axis=0, tiled=True),
    )
    attn_all, fc1_all, fc2_all, vector_cols, bias_ff, down_pick, up_pick, ff_pick = unpack(
        gathered, onehot_low
    )
    query_pre, inner_query = project(
        tokens, attn_all[:, 0, :], down_pick[:, :, 0], up_pick[:, :, 0]
    )
    query = ((query_pre + vector_cols[:, 0]) * 0.125).astype(jnp.bfloat16)
    key_pre, inner_key = project(tokens, attn_all[:, 1, :], down_pick[:, :, 1], up_pick[:, :, 1])
    keys = key_pre.astype(jnp.bfloat16)
    value_pre, inner_value = project(
        tokens, attn_all[:, 2, :], down_pick[:, :, 2], up_pick[:, :, 2]
    )
    values = (value_pre + vector_cols[:, 1]).astype(jnp.bfloat16)
    all_keys, all_values = (
        lax.all_gather(keys, "seq", axis=1, tiled=True),
        lax.all_gather(values, "seq", axis=1, tiled=True),
    )
    attended, logsum = attend(query, all_keys, all_values, lengths)
    mixed = attended.astype(jnp.bfloat16)
    branch_pre, inner_branch = project(
        mixed, attn_all[:, 3, :], down_pick[:, :, 3], up_pick[:, :, 3]
    )
    first_sum = tokens.astype(jnp.float32) + branch_pre + vector_cols[:, 2]
    normed, first_back = jax.vjp(
        partial(norm_rows, gain=vector_cols[:, 4], shift=vector_cols[:, 5]), first_sum
    )
    normed_low = normed.astype(jnp.bfloat16)
    hidden_pre, inner_hidden = project(normed_low, fc1_all, down_pick[:, :, 4], ff_pick[:, :, 0])
    activated, gelu_back = jax.vjp(gelu_exact, hidden_pre + bias_ff)
    activated_low = activated.astype(jnp.bfloat16)
    out_pre, inner_out = project(activated_low, fc2_all, ff_pick[:, :, 1], up_pick[:, :, 4])
    second = normed + out_pre + vector_cols[:, 3]
    final, second_back = jax.vjp(
        partial(norm_rows, gain=vector_cols[:, 6], shift=vector_cols[:, 7]), second
    )
    layer_out = (final * live_rows).astype(jnp.bfloat16)
    regathered = (
        lax.all_gather(attn_weight, ("fsdp", "seq"), axis=0, tiled=True),
        lax.all_gather(fc1_weight, ("fsdp", "seq"), axis=0, tiled=True),
        lax.all_gather(fc2_weight, ("fsdp", "seq"), axis=0, tiled=True),
        lax.all_gather(vectors, ("fsdp", "seq"), axis=0, tiled=True),
        lax.all_gather(fc1_bias, ("fsdp", "seq"), axis=0, tiled=True),
        lax.all_gather(adapter_down, ("fsdp", "seq"), axis=0, tiled=True),
        lax.all_gather(adapter_up, ("fsdp", "seq"), axis=0, tiled=True),
        lax.all_gather(ff_adapters, ("fsdp", "seq"), axis=0, tiled=True),
    )
    attn_all, fc1_all, fc2_all, vector_cols, bias_ff, down_pick, up_pick, ff_pick = unpack(
        regathered, onehot_low
    )
    grad_final = cotangent.astype(jnp.float32) * live_rows
    (grad_second,) = second_back(grad_final)
    grad_out_low = grad_second.astype(jnp.bfloat16)
    grad_activated, down_of_fc2, up_of_fc2 = project_back(
        activated_low, inner_out, grad_out_low, fc2_all, ff_pick[:, :, 1], up_pick[:, :, 4]
    )
    (grad_hidden,) = gelu_back(grad_activated)
    grad_hidden_low = grad_hidden.astype(jnp.bfloat16)
    grad_normed, down_of_fc1, up_of_fc1 = project_back(
        normed_low, inner_hidden, grad_hidden_low, fc1_all, down_pick[:, :, 4], ff_pick[:, :, 0]
    )
    (grad_first,) = first_back(grad_normed + grad_second)
    grad_branch_low = grad_first.astype(jnp.bfloat16)
    grad_mixed, down_of_out, up_of_out = project_back(
        mixed,
        inner_branch,
        grad_branch_low,
        attn_all[:, 3, :],
        down_pick[:, :, 3],
        up_pick[:, :, 3],
    )
    grad_mixed_low = grad_mixed.astype(jnp.bfloat16)
    row_delta = jnp.einsum(
        "sqhd,sqhd->shq", split_heads(grad_mixed_low.astype(jnp.float32)), split_heads(attended)
    )
    grad_query, parts = query_side(
        query, all_keys, all_values, grad_mixed_low, logsum, row_delta, lengths
    )
    grad_keys, grad_values = (
        lax.psum_scatter(
            parts[0].astype(jnp.bfloat16), "seq", scatter_dimension=1, tiled=True
        ).astype(jnp.float32),
        lax.psum_scatter(
            parts[1].astype(jnp.bfloat16), "seq", scatter_dimension=1, tiled=True
        ).astype(jnp.float32),
    )
    grad_query_low = grad_query.astype(jnp.bfloat16) * 0.125
    grad_keys_low = grad_keys.astype(jnp.bfloat16)
    grad_values_low = grad_values.astype(jnp.bfloat16)
    grad_from_query, down_of_query, up_of_query = project_back(
        tokens, inner_query, grad_query_low, attn_all[:, 0, :], down_pick[:, :, 0], up_pick[:, :, 0]
    )
    grad_from_key, down_of_key, up_of_key = project_back(
        tokens, inner_key, grad_keys_low, attn_all[:, 1, :], down_pick[:, :, 1], up_pick[:, :, 1]
    )
    grad_from_value, down_of_value, up_of_value = project_back(
        tokens,
        inner_value,
        grad_values_low,
        attn_all[:, 2, :],
        down_pick[:, :, 2],
        up_pick[:, :, 2],
    )
    input_grad = (grad_from_query + grad_from_key + grad_from_value + grad_first).astype(
        jnp.bfloat16
    )
    down_terms = jnp.stack(
        (down_of_query, down_of_key, down_of_value, down_of_out, down_of_fc1), axis=2
    )
    up_terms = jnp.stack((up_of_query, up_of_key, up_of_value, up_of_out, up_of_fc2), axis=2)
    ff_terms = jnp.stack((up_of_fc1, down_of_fc2), axis=2)
    down_table = sum_by_adapter(onehot_full, down_terms)
    up_table = sum_by_adapter(onehot_full, up_terms)
    ff_table = sum_by_adapter(onehot_full, ff_terms)
    down_grad, up_grad, ff_grad = (
        lax.psum_scatter(down_table, ("fsdp", "seq"), scatter_dimension=0, tiled=True),
        lax.psum_scatter(up_table, ("fsdp", "seq"), scatter_dimension=0, tiled=True),
        lax.psum_scatter(ff_table, ("fsdp", "seq"), scatter_dimension=0, tiled=True),
    )
    return (layer_out, input_grad, down_grad, up_grad, ff_grad)


MESH = pl.DeviceIdType.MESH
CHUNKS = 26
DEPTH = 8
ALL2, ALL4 = pl.ds(0, 2), pl.ds(0, 4)


class Spot:
    def __init__(self):
        self.y = lax.axis_index("fsdp")
        self.s = lax.axis_index("seq")
        self.z = self.s // 4
        self.x = (self.s // 2) % 2
        self.c = self.s % 2
        self.pair_z = self.z + 1 - 2 * (self.z % 2)
        self.inner = (self.z + 1) // 2 == 1

    def at(self, dy=0, dz=0, dx=0, dc=0):
        y = (self.y + dy) % 2
        z = (self.z + dz) % 4
        x = (self.x + dx) % 2
        c = (self.c + dc) % 2
        return (y, (z * 2 + x) * 2 + c)


def enter(spot):
    barrier = pltpu.get_barrier_semaphore()
    for step in range(1, 16):
        peer = (spot.y, (spot.s + step) % 16)
        pl.semaphore_signal(barrier, inc=1, device_id=peer, device_id_type=MESH)
    pl.semaphore_signal(barrier, inc=1, device_id=spot.at(dy=1), device_id_type=MESH)
    pl.semaphore_wait(barrier, 16)


class Gather:
    def __init__(self, spot, parts, ways, others, send, recv):
        self.spot, self.parts, self.ways, self.others = spot, parts, ways, others
        self.send, self.recv = send, recv

    def block(self, k, dy=0, dz=0, dx=0, dc=0):
        p = self.spot
        places = ((p.y, dy, 2), (p.z, dz, 4), (p.x, dx, 2), (p.c, dc, 2))
        return self.parts[k].at[tuple((place + d) % n if isinstance(d, int) else d for place, d, n in places)]

    def copy(self, source, target, k, out, into, peer):
        return pltpu.make_async_remote_copy(
            src_ref=source,
            dst_ref=target,
            send_sem=self.send.at[k % DEPTH, out],
            recv_sem=self.recv.at[k % DEPTH, into],
            device_id=peer,
            device_id_type=MESH,
        )

    def push(self, ref, k, out, into, source=None, **hop):
        self.copy(ref if source is None else source, ref, k, out, into, self.spot.at(**hop)).start()

    def arrive(self, like, k, into):
        self.copy(like, like, k, 0, into, self.spot.at(dc=1)).wait_recv()

    def retire(self, k):
        if self.ways[k] == "z":
            pieces = ((1, 3, 1), (2, 3, 2), (2, 3, 2), (1, 4, 1))
        elif self.ways[k] == "h":
            pieces = ((1, 1, 1), (2, 3, 2), (2, 3, 2), (1, 4, 1))

            @pl.when(self.spot.inner)
            def _():
                for out in (4, 5):
                    like = self.pair_of(k, 0)
                    self.copy(like, like, k, out, 0, self.spot.at(dc=1)).wait_send()

        else:
            pieces = ((1, 1, 1), (2, 3, 1), (2, 4, 2), (2, 4, 1))
        for out, (ys, zs, xs) in enumerate(pieces):
            like = self.parts[k].at[pl.ds(0, ys), pl.ds(0, zs), pl.ds(0, xs), 0]
            self.copy(like, like, k, out, 0, self.spot.at(dc=1)).wait_send()

    def pair_of(self, k, far):
        p = self.spot
        return self.parts[k].at[p.y, pl.ds(((p.z // 2 + far) % 2) * 2, 2), p.x, p.c]

    def hand(self, k):
        self.arrive(self.block(k), k, 0)

        @pl.when(self.spot.inner)
        def _():
            self.push_to(self.pair_of(k, 0), k, 4, 5, 3 - self.spot.z)

    def pass_on(self, k):
        @pl.when(self.spot.inner)
        def _():
            self.arrive(self.pair_of(k, 1), k, 5)
            self.push_to(self.pair_of(k, 1), k, 5, 5, self.spot.pair_z)

    def push_to(self, ref, k, out, into, z):
        p = self.spot
        self.copy(ref, ref, k, out, into, (p.y, (z * 2 + p.x) * 2 + p.c)).start()

    def first(self, k):
        if k >= DEPTH:
            self.retire(k - DEPTH)
        if self.ways[k] == "h":
            self.push_to(self.block(k), k, 0, 0, self.spot.pair_z)
        elif self.ways[k] == "z":
            for d in range(1, 4):
                self.push(self.block(k), k, 0, 0, dz=d)
        else:
            self.push(self.block(k), k, 0, 0, self.others.get(k), **{"d" + self.ways[k]: 1})

    def second(self, k):
        if self.ways[k] in "zh":
            if self.ways[k] == "z":
                self.arrive(self.block(k, dz=pl.ds(0, 3)), k, 0)
            else:

                @pl.when(jnp.logical_not(self.spot.inner))
                def _():
                    self.arrive(self.pair_of(k, 1), k, 5)

            line = self.block(k, dz=ALL4)
            self.push(line, k, 1, 1, dx=1)
            self.push(line, k, 1, 2, dy=1)
            self.push(line, k, 1, 4, dc=1)
        else:
            self.arrive(self.block(k), k, 0)
            for d in range(1, 4):
                self.push(self.block(k, **{"d" + self.ways[k]: ALL2}), k, 1, 1, dz=d)

    def third(self, k):
        if self.ways[k] in "zh":
            cut = 3 if k in SHIFTED else 2
            self.arrive(self.block(k, dz=ALL4), k, 1)
            self.push(self.block(k, dz=pl.ds(0, cut), dx=1), k, 2, 3, dy=1)
            self.arrive(self.block(k, dz=ALL4), k, 2)
            self.push(self.block(k, dz=pl.ds(cut, 4 - cut), dy=1), k, 2, 3, dx=1)
            self.push(self.block(k, dz=ALL4, dx=1), k, 2, 4, dc=1)
            self.push(self.block(k, dz=ALL4, dy=1), k, 2, 4, dc=1)
        else:
            near, far = "d" + self.ways[k], "dy" if self.ways[k] == "x" else "dx"
            self.arrive(self.block(k, **{near: ALL2, "dz": pl.ds(0, 3)}), k, 1)
            plane = self.block(k, **{near: ALL2, "dz": ALL4})
            self.push(plane, k, 2, 2, **{far: 1})
            self.push(plane, k, 2, 4, dc=1)

    def fourth(self, k):
        if self.ways[k] in "zh":
            self.arrive(self.block(k, dz=ALL4), k, 3)
            self.push(self.block(k, dz=ALL4, dx=1, dy=1), k, 3, 4, dc=1)
        else:
            near, far = "d" + self.ways[k], "dy" if self.ways[k] == "x" else "dx"
            self.arrive(self.block(k, **{near: ALL2, "dz": ALL4}), k, 2)
            self.push(self.block(k, **{near: ALL2, "dz": ALL4, far: 1}), k, 3, 4, dc=1)

    def ready(self, k):
        self.arrive(self.block(k, dy=ALL2, dz=ALL4, dx=ALL2), k, 4)

    def step(self, t):
        moves = ((0, self.first), (1, self.second), (2, self.third), (3, self.fourth), (4, self.ready))
        hops = ((-2, self.first), (-1, self.hand), (0, self.pass_on)) + moves[1:]
        order = [(late, k, move) for k, way in enumerate(self.ways) for late, move in (hops if way == "h" else moves)]
        for late, k, move in sorted(order, key=lambda entry: (entry[0], entry[1])):
            if k + late == t:
                move(k)

    def finish(self):
        for k in range(len(self.parts) - DEPTH, len(self.parts)):
            self.retire(k)


F32, BF16 = jnp.float32, jnp.bfloat16
ORDER = (0, 1, 24, 25) + tuple(range(2, 24))
WAYS = "zzyyzz" + "h" * 20
SHIFTED = (6, 7, 8, 9, 10, 12, 13, 16)
EARLY, LATE = 80, 64


def dot(left, right):
    return jnp.dot(left, right, preferred_element_type=F32)


def dot_nt(left, right):
    return lax.dot_general(left, right, (((1,), (1,)), ((), ())), preferred_element_type=F32)


def dot_tn(left, right):
    return lax.dot_general(left, right, (((0,), (0,)), ((), ())), preferred_element_type=F32)


def lanes(shape):
    return lax.broadcasted_iota(jnp.int32, shape, len(shape) - 1)


def half(value, slot):
    low_half = lanes(value.shape) < HEAD
    zero = jnp.zeros_like(value)
    return jnp.where(low_half, value, zero) if slot == 0 else jnp.where(low_half, zero, value)


def pair(first, second):
    return jnp.where(lanes(first.shape) < HEAD, first, second)


def swap(value):
    return pltpu.roll(value, HEAD, 1)


def heads_to_rows(heads, rows, factor):
    for p in range(HEADS // 2):
        even = heads[2 * p].astype(F32) * factor
        odd = heads[2 * p + 1].astype(F32) * factor
        rows[0:64, p * 128 : p * 128 + 128] = pair(even, swap(odd)).astype(BF16)
        rows[64:128, p * 128 : p * 128 + 128] = pair(swap(even), odd).astype(BF16)


class Exchange:
    def __init__(self, spot, out, into, send, recv):
        self.spot, self.out, self.into, self.send, self.recv = spot, out, into, send, recv

    def copy(self, unit, source, target, block, peer):
        return pltpu.make_async_remote_copy(
            src_ref=source,
            dst_ref=target,
            send_sem=self.send.at[unit, block],
            recv_sem=self.recv.at[unit, self.spot.z],
            device_id=(self.spot.y, peer),
            device_id_type=MESH,
        )

    def start(self, unit, block):
        me = self.spot.s

        def body(i, carry):
            peer = block * 4 + i

            @pl.when(peer != me)
            def _():
                self.copy(unit, self.out.at[unit, peer], self.into.at[unit, me], block, peer).start()

            return carry

        lax.fori_loop(0, 4, body, 0)

    def keep(self, unit):
        self.into[unit, self.spot.s] = self.out[unit, self.spot.s]

    def like(self, unit, far):
        return self.into.at[unit, pl.ds(0, 4 if far else 3)]

    def wait_block(self, unit, far):
        block = (self.spot.z + far) % 4
        like = self.like(unit, far)
        pltpu.make_async_copy(like, like, self.recv.at[unit, block]).wait()

    def wait(self, unit):
        for far in range(4):
            self.wait_block(unit, far)

    def finish(self, units):
        for unit in range(units):
            for far in range(4):
                like = self.like(unit, far)
                pltpu.make_async_copy(like, like, self.send.at[unit, (self.spot.z + far) % 4]).wait()


class Scatter:
    def __init__(self, spot, wide, own, core_in, core_sum, x_in, x_sum, into, send, recv):
        self.spot, self.wide = spot, wide
        self.own, self.core_in, self.core_sum = own, core_in, core_sum
        self.x_in, self.x_sum, self.into = x_in, x_sum, into
        self.send, self.recv = send, recv

    def copy(self, source, target, route, peer):
        return pltpu.make_async_remote_copy(
            src_ref=source,
            dst_ref=target,
            send_sem=self.send.at[route],
            recv_sem=self.recv.at[route],
            device_id=peer,
            device_id_type=MESH,
        )

    def first(self):
        p = self.spot
        self.hop = self.copy(self.own.at[:, :, :, 1 - p.c], self.core_in, 0, p.at(dc=1))
        self.hop.start()

    def second(self):
        p = self.spot
        self.hop.wait()
        self.core_sum[...] = (self.own[:, :, :, p.c].astype(F32) + self.core_in[...].astype(F32)).astype(BF16)
        if not self.wide:
            self.hop = self.copy(self.core_sum.at[:, :, 1 - p.x], self.x_in, 1, p.at(dx=1))
            self.hop.start()

    def distances(self):
        every = [(dy, dz, dx) for dy in range(2) for dz in range(4) for dx in range(2 if self.wide else 1)]
        return every[1:]

    def third(self):
        p = self.spot
        if not self.wide:
            self.hop.wait()
            self.x_sum[...] = (self.core_sum[:, :, p.x].astype(F32) + self.x_in[...].astype(F32)).astype(BF16)
        for n, (dy, dz, dx) in enumerate(self.distances()):
            y, z, x = (p.y + dy) % 2, (p.z + dz) % 4, (p.x + dx) % 2
            source = self.core_sum.at[y, z, x] if self.wide else self.x_sum.at[y, z]
            self.copy(source, self.into.at[n], 2, p.at(dy=dy, dz=dz, dx=dx)).start()

    def fourth(self):
        p = self.spot
        self.copy(self.into, self.into, 2, p.at(dc=1)).wait()
        total = [self.core_sum[p.y, p.z, p.x] if self.wide else self.x_sum[p.y, p.z], None]
        total[0] = total[0].astype(F32)
        for n, (dy, _, _) in enumerate(self.distances()):
            term = self.into[n].astype(F32)
            total[dy] = term if total[dy] is None else total[dy] + term
        return total


def scatter_shapes(rows, wide):
    return [
        pltpu.VMEM((2, 4, 2, 2, rows, 128), BF16),
        pltpu.VMEM((2, 4, 2, rows, 128), BF16),
        pltpu.VMEM((2, 4, 2, rows, 128), BF16),
        pltpu.VMEM((2, 4, rows, 128), BF16),
        pltpu.VMEM((2, 4, rows, 128), BF16),
        pltpu.VMEM((15 if wide else 7, rows, 128), BF16),
        pltpu.SemaphoreType.DMA((3,)),
        pltpu.SemaphoreType.DMA((3,)),
    ]


def layer_kernel(*refs):
    it = iter(refs)

    def take(count):
        return [next(it) for _ in range(count)]

    attn, fc1, fc2, tok_far, cot_far, down_table, up_table, ff_table, vec_in, bias_in, lengths, ids = take(12)
    layer_out, input_grad, down_out, up_out, ff_out = take(5)
    wide, tall, rank_all, ff_all = take(4)
    rank_in, rank_up, rank_x, vec, ff_low, bias = take(6)
    heads_out, heads_in = take(2)
    weights_low, weights_back = take(2)
    attended, stat, tmp, sum_one, scaled_one, normed, grad_second, grad_first = take(8)
    tok, cot, mixed, normed_low, out_low, branch_low, query_low, key_low, value_low = take(9)
    slope, act, grad_hidden, inner4 = take(4)
    id_rows, table, rank_other, ff_other = take(4)
    early_refs, late_refs = take(8), take(8)
    own, send, recv, hsend, hrecv, id_sem = take(6)

    spot = Spot()
    here = (spot.y, spot.z, spot.x, spot.c)
    parts = [wide.at[k] for k in range(16)] + [tall.at[k] for k in range(8)] + [rank_all, ff_all]
    placed = []
    for k in range(8):
        placed.append(pltpu.make_async_copy(fc1.at[:, pl.ds(k * 512, 512)], parts[8 + k].at[here], own.at[0]))
        placed.append(pltpu.make_async_copy(fc2.at[:, pl.ds(k * 128, 128)], parts[16 + k].at[here], own.at[1]))
    tok_copy = pltpu.make_async_copy(tok_far, tok, own.at[2])
    cot_copy = pltpu.make_async_copy(cot_far, cot, own.at[3])
    tok_copy.start()
    for k in (0, 1):
        wide[(k,) + here] = attn[:, 0, k * 512 : k * 512 + 512]
    for copy in placed:
        copy.start()
    cot_copy.start()
    others = {2: rank_other, 3: ff_other}
    gather = Gather(spot, [parts[k] for k in ORDER], WAYS, others, send, recv)
    swaps = Exchange(spot, heads_out, heads_in, hsend, hrecv)
    early = Scatter(spot, False, *early_refs)
    late = Scatter(spot, True, *late_refs)
    first_row = lax.broadcasted_iota(jnp.int32, (8, 128), 0) == 0
    id_rows[spot.y] = jnp.where(first_row, ids[0], ids[1])
    enter(spot)
    gather.step(0)
    id_copy = pltpu.make_async_remote_copy(
        src_ref=id_rows.at[spot.y],
        dst_ref=id_rows.at[spot.y],
        send_sem=id_sem.at[0],
        recv_sem=id_sem.at[1],
        device_id=spot.at(dy=1),
        device_id_type=MESH,
    )
    id_copy.start()
    for j in range(1, 4):
        for k in range(2):
            wide[(2 * j + k,) + here] = attn[:, j, k * 512 : k * 512 + 512]

    def chosen(source, kind, y, slot):
        who = id_rows[y, slot : slot + 1, 0 : source.shape[3]]
        total = None
        for a in range(ADAPTERS):
            term = jnp.where(who == a, source[a, kind].astype(F32), 0.0)
            total = term if total is None else total + term
        return total

    def pick_all():
        table[...] = jnp.zeros_like(table)
        for g in range(2):
            y = (spot.y + g) % 2
            for slot in range(2):
                for j in range(4):
                    row = g * 384 + j * 32 + slot * 16
                    table[row : row + 16, 0:32] = chosen(down_table, j, y, slot)
                    table[row + 128 : row + 144, 0:32] = chosen(up_table, j, y, slot)
                row = g * 384 + 256 + slot * 16
                table[row : row + 16, 0:32] = chosen(down_table, 4, y, slot)
                table[row + 32 : row + 48, 0:32] = chosen(up_table, 4, y, slot)
                for kind in range(2):
                    row = 768 + g * 64 + kind * 32 + slot * 16
                    table[row : row + 16, :] = chosen(ff_table, kind, y, slot)
        for n in range(3):
            cols = slice(n * 128, n * 128 + 128)
            rank_all[here + (slice(None), cols)] = table[cols, :].T[0:32].astype(BF16)
            rank_other[:, cols] = table[384 + n * 128 : 512 + n * 128, :].T[0:32].astype(BF16)
        turned = table[768:896, :].T
        ff_all[here + (slice(0, 64),)] = pair(turned[0:64], swap(turned[64:128])).astype(BF16)
        ff_other[0:64] = pair(swap(turned[0:64]), turned[64:128]).astype(BF16)
        table[0:8, 0:32] = vec_in[...].astype(F32)
        table[0:8, 32:128] = jnp.zeros((8, 96), F32)
        columns = pltpu.roll(table[0:8, :], (spot.s % 4) * 32, 1)
        rows = jnp.concatenate([jnp.broadcast_to(bias_in[...].astype(F32), (8, 128)), columns], axis=0)
        ff_all[here + (slice(64, 80),)] = rows.astype(BF16)
        ff_other[64:80] = rows.astype(BF16)

    lane = lanes((128, 128))
    row_slot = lax.broadcasted_iota(jnp.int32, (128, 128), 0) >= 64
    slot_lane = ((lane & 16) != 0) == row_slot
    kind4 = [slot_lane & ((lane >> 5) == j) for j in range(4)]
    kind_ff = [slot_lane & ((lane >> 5) == k) for k in range(2)]

    def only(mask, value):
        return jnp.where(mask, value, jnp.zeros_like(value))

    def square(k, t):
        halves = [wide[2 * k + i, t // 2, pl.ds((t % 2) * 2, 2)].reshape(256, 512) for i in range(2)]
        return jnp.concatenate(halves, axis=1)

    def columns(k, n):
        return wide[2 * k + n // 2, :, :, :, :, :, tile(n % 2)].reshape(1024, 256)

    def tile(n, size=256):
        return pl.ds(pl.multiple_of(n * size, size), size)

    def unpack_rank():
        rank_in[...] = rank_all[:, :, :, :, :, 0:128].reshape(1024, 128)
        rank_up[...] = rank_all[:, :, :, :, :, 128:256].reshape(1024, 128)
        rank_x[...] = rank_all[:, :, :, :, :, 256:384].reshape(1024, 128)

    def ff_rows(first, count):
        return ff_low[pl.ds(first, count)].reshape(count * 128, 128)

    def unpack_ff():
        columns_of = {}
        packed = ff_all[:, :, :, :, 0:64, :].reshape(32, 64, 128)
        ff_low[:, 0] = packed
        ff_low[:, 1] = swap(packed.astype(F32).reshape(2048, 128)).astype(BF16).reshape(32, 64, 128)
        for o in range(32):
            y, z, x, c = o // 16, (o // 4) % 4, (o // 2) % 2, o % 2
            rows = ff_all[y, z, x, c, 64:80, :].astype(F32)
            bias[:, o * 128 : o * 128 + 128] = rows[0:8]
            columns_of[o // 4] = rows[8:16] if o % 4 == 0 else columns_of[o // 4] + rows[8:16]
        for n in range(8):
            vec[:, n * 128 : n * 128 + 128] = columns_of[n]

    def to_heads(unit, block, value):
        for p in range(2):
            first = value[0:64, p * 128 : p * 128 + 128]
            second = value[64:128, p * 128 : p * 128 + 128]
            heads_out[unit, block * 4 + 2 * p] = pair(first, swap(second)).astype(BF16)
            heads_out[unit, block * 4 + 2 * p + 1] = pair(swap(first), second).astype(BF16)
        swaps.start(unit, block)

    def turn(body):
        def shifted(t, carry):
            body((spot.z + t) % 4)
            return carry

        lax.fori_loop(0, 4, shifted, 0)

    def project_in(j):
        inner = only(kind4[j], inner4[...])

        def body(n):
            cols = tile(n)
            value = dot(tok[...], columns(j, n)) + dot_nt(inner, rank_up[cols, :])
            if j == 0:
                value = (value + vec[0:1, cols]) * 0.125
            if j == 2:
                value = value + vec[1:2, cols]
            to_heads(j, n, value)

        turn(body)
        swaps.keep(j)

    def attention(t):
        if t == 0:
            for j in range(3):
                swaps.wait(j)
        block = (spot.z + t) % 4
        keys = heads_in[1].reshape(1024, 128)
        values = heads_in[2].reshape(1024, 128)
        rows = tile(block)
        query = heads_in[0, pl.ds(block * 4, 4)].reshape(256, 128)
        results, stats = [], []
        for slot in range(2):
            scores = dot_nt(half(query, slot), keys)
            scores = jnp.where(lanes(scores.shape) < lengths[slot], scores, NEG_FILL)
            top = jnp.max(scores, axis=-1, keepdims=True)
            shifted = jnp.exp(scores - top)
            total = jnp.sum(shifted, axis=-1, keepdims=True)
            low = (shifted * (1.0 / total)).astype(BF16)
            weights_low[slot, rows, :] = low
            results.append(dot(low, values))
            stats.append(jnp.broadcast_to(top + jnp.log(total), (256, 128)))
        result = pair(results[0], results[1])
        attended[rows, :] = result
        heads_out[3, pl.ds(block * 4, 4)] = result.astype(BF16).reshape(4, 64, 128)
        stat[rows, :] = pair(stats[0], stats[1])
        swaps.start(3, block)
        if t == 3:
            swaps.keep(3)

    def attention_turned(first):
        logsum = stat[...].T
        queries = heads_in[0].reshape(1024, 128)
        turned = [logsum[0:1], logsum[64:65]]

        def body(t, carry):
            rows = tile(t)
            keys = heads_in[1, pl.ds(t * 4, 4)].reshape(256, 128)
            for slot in range(2):
                scores = dot_nt(half(keys, slot), queries)
                weights = jnp.exp(scores - turned[slot])
                place = lax.broadcasted_iota(jnp.int32, weights.shape, 0) + t * 256
                weights = jnp.where(place < lengths[slot], weights, 0.0)
                weights_back[slot, rows, :] = weights.astype(BF16)
            return carry

        lax.fori_loop(first, first + 2, body, 0)

    def normalize(value):
        centered = value - jnp.mean(value, axis=-1, keepdims=True)
        spread = lax.rsqrt(jnp.mean(centered * centered, axis=-1, keepdims=True) + NORM_EPS)
        return centered * spread, spread

    def normalize_back(grad, scaled, spread):
        shift = jnp.mean(grad, axis=-1, keepdims=True)
        along = jnp.mean(grad * scaled, axis=-1, keepdims=True)
        return spread * (grad - shift - scaled * along)

    saved = {}

    def branch():
        swaps.wait(3)
        heads_to_rows(heads_in.at[3], mixed, 1.0)
        saved["o"] = only(kind4[3], dot(mixed[...], rank_in[...])).astype(BF16)

        def body(n, carry):
            cols = tile(n)
            value = dot(mixed[...], columns(3, n)) + dot_nt(saved["o"], rank_up[cols, :])
            sum_one[:, cols] = tok[:, cols].astype(F32) + value + vec[2:3, cols]
            return carry

        lax.fori_loop(0, 4, body, 0)
        scaled, saved["spread_one"] = normalize(sum_one[...])
        scaled_one[...] = scaled
        value = scaled * vec[4:5] + vec[5:6]
        normed[...] = value
        normed_low[...] = value.astype(BF16)
        saved["hidden"] = only(kind_ff[0], dot(normed_low[...], rank_x[...])).astype(BF16)

    def expand(k):
        def body(i, carry):
            n = k * 2 + i
            cols = tile(n)
            value = dot(normed_low[...], wide[8 + k, :, :, :, :, :, tile(i)].reshape(1024, 256))
            value = value + dot_nt(saved["hidden"], ff_rows(n * 2, 2)) + bias[0:1, cols]
            share = 0.5 * (1.0 + lax.erf(value * math.sqrt(0.5)))
            act[:, cols] = (value * share).astype(BF16)
            bell = jnp.exp(-0.5 * value * value) * (1.0 / math.sqrt(2.0 * math.pi))
            slope[:, cols] = share + value * bell
            return carry

        lax.fori_loop(0, 2, body, 0)

    def contract(q):
        if q == 0:
            saved["out"] = only(kind_ff[1], dot(act[...], ff_rows(0, 32))).astype(BF16)
        cols = slice(q * 256, q * 256 + 256)
        weight = jnp.concatenate([tall[2 * q + i].reshape(4096, 128) for i in range(2)], axis=1)
        value = dot(act[...], weight) + dot_nt(saved["out"], rank_x[cols, :])
        tmp[:, cols] = normed[:, cols] + value + vec[3:4, cols]

    def outer():
        rows = lax.broadcasted_iota(jnp.int32, (128, 1), 0)
        place = spot.s * 64 + (rows & 63)
        limit = jnp.where(rows < 64, lengths[0], lengths[1])
        live = (place < limit).astype(F32)
        scaled, spread = normalize(tmp[...])
        layer_out[...] = (live * (scaled * vec[6:7] + vec[7:8])).astype(BF16)
        grad = normalize_back(live * cot[...].astype(F32) * vec[6:7], scaled, spread)
        grad_second[...] = grad
        out_low[...] = grad.astype(BF16)
        saved["g_out"] = only(kind_ff[1], dot(out_low[...], rank_x[...])).astype(BF16)

    def hidden_back():
        def body(t, carry):
            rows = tile(t, 512)
            value = dot_nt(saved["g_out"], ff_rows(t * 4, 4))
            for q in range(4):
                pieces = [tall[2 * q + i, t // 4, t % 4].reshape(512, 128) for i in range(2)]
                piece = jnp.concatenate(pieces, axis=1)
                value = value + dot_nt(out_low[:, q * 256 : q * 256 + 256], piece)
            grad_hidden[:, rows] = (value * slope[:, rows]).astype(BF16)
            return carry

        lax.fori_loop(0, 8, body, 0)
        saved["g_hidden"] = only(kind_ff[0], dot(grad_hidden[...], ff_rows(0, 32))).astype(BF16)

    def normed_back():
        def body(t, carry):
            rows = tile(t)
            value = dot_nt(saved["g_hidden"], rank_x[rows, :]) + grad_second[:, rows]
            for q in range(4):
                value = value + dot_nt(grad_hidden[:, q * 1024 : q * 1024 + 1024], square(4 + q, t))
            tmp[:, rows] = value
            return carry

        lax.fori_loop(0, 4, body, 0)
        grad = normalize_back(tmp[...] * vec[4:5], scaled_one[...], saved["spread_one"])
        grad_first[...] = grad
        branch_low[...] = grad.astype(BF16)
        saved["g_o"] = only(kind4[3], dot(branch_low[...], rank_up[...])).astype(BF16)

    def mixed_back():
        def body(n):
            value = dot_nt(branch_low[...], square(3, n)) + dot_nt(saved["g_o"], rank_in[tile(n), :])
            to_heads(4, n, value)

        turn(body)
        swaps.keep(4)

    def early_grads():
        own_grads = early.own
        value = dot_tn(normed_low[...], saved["g_hidden"]) + dot_tn(out_low[...], saved["out"])
        value = value.reshape(32, 2, 16, 128)
        value = value[:, 0] + swap(value[:, 1].reshape(512, 128)).reshape(32, 16, 128)
        own_grads[:, :, :, :, 0:16, :] = value.astype(BF16).reshape(2, 4, 2, 2, 16, 128)
        for y in range(2):
            for z in range(4):
                cols = slice((y * 4 + z) * 512, (y * 4 + z) * 512 + 512)
                value = dot_tn(grad_hidden[:, cols], saved["hidden"]) + dot_tn(act[:, cols], saved["g_out"])
                value = value.reshape(4, 128, 128)
                for o in range(4):
                    packed = value[o, 0:64] + swap(value[o, 64:128])
                    own_grads[y, z, o // 2, o % 2, 16:80, :] = packed.astype(BF16)

    def query_back(t):
        block = (spot.z + 4 - t) % 4
        swaps.wait_block(4, (4 - t) % 4)
        rows = tile(block)
        keys = heads_in[1].reshape(1024, 128)
        values = heads_in[2].reshape(1024, 128)
        grad_block = heads_in[4, pl.ds(block * 4, 4)].reshape(256, 128)
        product = grad_block.astype(F32) * attended[rows, :]
        parts_, deltas = [], []
        for slot in range(2):
            delta = jnp.sum(half(product, slot), axis=-1, keepdims=True)
            grad_probs = dot_nt(half(grad_block, slot), values)
            weights = weights_low[slot, rows, :].astype(F32)
            grad_scores = (weights * (grad_probs - delta)).astype(BF16)
            parts_.append(dot(grad_scores, keys))
            deltas.append(jnp.broadcast_to(delta, (256, 128)))
        heads_out[5, pl.ds(block * 4, 4)] = pair(*parts_).astype(BF16).reshape(4, 64, 128)
        stat[rows, :] = pair(*deltas)
        swaps.start(5, block)
        if t == 3:
            swaps.keep(5)

    def key_back():
        queries = heads_in[0].reshape(1024, 128)
        grads = heads_in[4].reshape(1024, 128)
        turned = stat[...].T
        turned = [turned[0:1], turned[64:65]]

        def body(block):
            rows = tile(block)
            value_block = heads_in[2, pl.ds(block * 4, 4)].reshape(256, 128)
            key_parts, value_parts = [], []
            for slot in range(2):
                weights = weights_back[slot, rows, :]
                grad_probs = dot_nt(half(value_block, slot), grads)
                grad_scores = (weights.astype(F32) * (grad_probs - turned[slot])).astype(BF16)
                key_parts.append(dot(grad_scores, queries))
                value_parts.append(dot(weights, grads))
            heads_out[6, pl.ds(block * 4, 4)] = pair(*key_parts).astype(BF16).reshape(4, 64, 128)
            heads_out[7, pl.ds(block * 4, 4)] = pair(*value_parts).astype(BF16).reshape(4, 64, 128)
            swaps.start(6, block)
            swaps.start(7, block)

        turn(body)
        swaps.keep(6)
        swaps.keep(7)

    def inputs_back():
        grads = (query_low, key_low, value_low)
        inner = jnp.zeros((128, 128), F32)
        ups = dot_tn(branch_low[...], saved["o"])
        downs = dot_tn(mixed[...], saved["g_o"])
        for j, grad in enumerate(grads):
            swaps.wait(5 + j)
            heads_to_rows(heads_in.at[5 + j], grad, 0.125 if j == 0 else 1.0)
            inner = jnp.where(kind4[j], dot(grad[...], rank_up[...]), inner)
            ups = ups + dot_tn(grad[...], only(kind4[j], inner4[...]))
        saved["g_in"] = inner.astype(BF16)
        late.own[:, :, :, :, 32:64, :] = ups.astype(BF16).reshape(2, 4, 2, 2, 32, 128)
        downs = downs + dot_tn(tok[...], saved["g_in"])
        late.own[:, :, :, :, 0:32, :] = downs.astype(BF16).reshape(2, 4, 2, 2, 32, 128)

    def tokens_back(t):
        rows = pl.ds(t * 256, 256)
        value = dot_nt(saved["g_in"], rank_in[rows, :]) + grad_first[:, rows]
        for j, grad in enumerate((query_low, key_low, value_low)):
            value = value + dot_nt(grad[...], square(j, t))
        input_grad[:, rows] = value.astype(BF16)

    def results(early_sum, late_sum):
        turned, ff_turned = [], []
        for dy in range(2):
            cross = jnp.concatenate([early_sum[dy][0:16], swap(early_sum[dy][0:16])], axis=0)
            table[0:64, :] = late_sum[dy]
            table[64:96, :] = cross
            table[96:128, :] = jnp.zeros((32, 128), F32)
            turned.append(table[0:128, :].T)
            packed = early_sum[dy][16:80]
            ff_turned.append(jnp.concatenate([packed, swap(packed)], axis=0).T)
        for a in range(ADAPTERS):
            who = [id_rows[(spot.y + dy) % 2, 0:2, :] == a for dy in range(2)]
            share = [match.astype(F32) for match in who]

            def gathered(source, first):
                total = None
                for dy in range(2):
                    for s in range(2):
                        row = first + s * 16
                        term = share[dy][s : s + 1] * source[dy][row : row + 16, :]
                        total = term if total is None else total + term
                return total

            for j in range(4):
                value = gathered(turned, j * 32)
                down_out[a, j] = value[:, 0:32]
                up_out[a, j] = value[:, 32:64]
            down_out[a, 4] = gathered(turned, 0)[:, 64:96]
            up_out[a, 4] = gathered(turned, 32)[:, 64:96]
            for kind in range(2):
                ff_out[a, kind] = gathered(ff_turned, kind * 32)

    for t in range(1, CHUNKS + 4):
        if t == 2:
            id_copy.wait_recv()
            pick_all()
        if t == 4:
            for n, like in enumerate((wide.at[(pl.ds(8, 8),) + here], tall.at[(pl.ds(0, 8),) + here])):
                pltpu.make_async_copy(like, like, own.at[n]).wait()
        gather.step(t)
        if t == 7:
            tok_copy.wait()
            unpack_rank()
            unpack_ff()
            inner4[...] = dot(tok[...], rank_in[...]).astype(BF16)
        if t in (7, 9, 11):
            project_in((t - 7) // 2)
        if 14 <= t <= 17:
            attention(t - 14)
        if 18 <= t <= 19:
            attention_turned((t - 18) * 2)
        if t == 20:
            branch()
        if 21 <= t <= 24:
            expand(2 * t - 42)
            expand(2 * t - 41)
        if t == 27:
            contract(0)
        if t >= 27:
            contract(t - 26)
    cot_copy.wait()
    outer()
    hidden_back()
    normed_back()
    mixed_back()
    early_grads()
    early.first()
    for t in range(4):
        query_back(t)
    early.second()
    key_back()
    early.third()
    inputs_back()
    late.first()
    tokens_back(0)
    late.second()
    late.third()
    for t in range(1, 4):
        tokens_back(t)
    results(early.fourth(), late.fourth())
    id_copy.wait_send()
    gather.finish()
    swaps.finish(8)


def hand_on_kernel(*refs):
    count = len(refs) // 2
    for k in range(count):
        refs[count + k][...] = refs[k][...]


def hand_on(arrays):
    near = pl.BlockSpec(memory_space=pltpu.VMEM)
    return pl.pallas_call(
        hand_on_kernel,
        out_shape=[jax.ShapeDtypeStruct(array.shape, array.dtype) for array in arrays],
        in_specs=[near] * len(arrays),
        out_specs=[near] * len(arrays),
        name="hand_on",
    )(*arrays)


def layer(attn, fc1, fc2, tok, cot, down, up, ff, vec, bias, lengths, ids):
    lead = (2, 4, 2, 2)
    anywhere = pl.BlockSpec(memory_space=pl.ANY)
    near = pl.BlockSpec(memory_space=pltpu.VMEM)
    scalar = pl.BlockSpec(memory_space=pltpu.SMEM)

    def buffer(*shape, dtype=BF16):
        return pltpu.VMEM(shape, dtype)

    scratch = [
        buffer(16, *lead, 32, 512),
        buffer(8, *lead, 128, 128),
        buffer(*lead, 32, 384),
        buffer(*lead, 80, 128),
    ]
    scratch += [buffer(1024, 128)] * 3 + [buffer(8, 1024, dtype=F32), buffer(32, 2, 64, 128)]
    scratch += [buffer(8, 4096, dtype=F32)]
    scratch += [buffer(8, 16, 64, 128)] * 2
    scratch += [buffer(2, 1024, 1024)] * 2
    scratch += [buffer(1024, 128, dtype=F32)] * 2
    scratch += [buffer(128, 1024, dtype=F32)] * 6
    scratch += [buffer(128, 1024)] * 9
    scratch += [buffer(128, 4096, dtype=F32), buffer(128, 4096), buffer(128, 4096), buffer(128, 128)]
    scratch += [buffer(2, 8, 128, dtype=jnp.int32), buffer(896, 128, dtype=F32)]
    scratch += [buffer(32, 384), buffer(80, 128)]
    scratch += scatter_shapes(EARLY, False) + scatter_shapes(LATE, True)
    scratch += [pltpu.SemaphoreType.DMA((4,))]
    scratch += [pltpu.SemaphoreType.DMA((DEPTH, 6))] * 2
    scratch += [pltpu.SemaphoreType.DMA((8, 4))] * 2
    scratch += [pltpu.SemaphoreType.DMA((2,))]
    return pl.pallas_call(
        layer_kernel,
        out_shape=[
            jax.ShapeDtypeStruct(tok.shape, BF16),
            jax.ShapeDtypeStruct(tok.shape, BF16),
            jax.ShapeDtypeStruct(down.shape, F32),
            jax.ShapeDtypeStruct(up.shape, F32),
            jax.ShapeDtypeStruct(ff.shape, F32),
        ],
        in_specs=[near] + [anywhere] * 4 + [near] * 5 + [scalar] * 2,
        out_specs=[near] * 5,
        scratch_shapes=scratch,
        compiler_params=pltpu.CompilerParams(
            collective_id=0, has_side_effects=True, vmem_limit_bytes=63 * 2**20
        ),
        name="layer",
    )(attn, fc1, fc2, tok, cot, down, up, ff, vec, bias, lengths, ids)


def fast_device(
    tokens,
    cotangent,
    lengths,
    adapter_ids,
    attn_weight,
    fc1_weight,
    fc2_weight,
    vectors,
    fc1_bias,
    adapter_down,
    adapter_up,
    ff_adapters,
):
    width = tokens.shape[2]
    outs = layer(
        attn_weight,
        fc1_weight,
        fc2_weight,
        tokens.reshape(-1, width),
        cotangent.reshape(-1, width),
        adapter_down.transpose(1, 2, 3, 0),
        adapter_up.transpose(1, 2, 3, 0),
        ff_adapters.transpose(1, 2, 3, 0),
        vectors.T,
        fc1_bias[None],
        lengths,
        adapter_ids,
    )
    outs = hand_on(outs)
    grads = [grad.transpose(3, 0, 1, 2) for grad in outs[2:]]
    return (outs[0].reshape(tokens.shape), outs[1].reshape(tokens.shape), *grads)


def solution(mesh):
    in_specs = (
        P("fsdp", "seq", None),
        P("fsdp", "seq", None),
        P("fsdp"),
        P("fsdp"),
        P(("fsdp", "seq"), None, None),
        P(("fsdp", "seq"), None),
        P(("fsdp", "seq"), None),
        P(("fsdp", "seq"), None),
        P(("fsdp", "seq")),
        P(("fsdp", "seq"), None, None, None),
        P(("fsdp", "seq"), None, None, None),
        P(("fsdp", "seq"), None, None, None),
    )
    out_specs = (
        P("fsdp", "seq", None),
        P("fsdp", "seq", None),
        P(("fsdp", "seq"), None, None, None),
        P(("fsdp", "seq"), None, None, None),
        P(("fsdp", "seq"), None, None, None),
    )
    fast = mesh.shape["fsdp"] == 2 and mesh.shape["seq"] == HEADS
    return jax.shard_map(
        fast_device if fast else on_device, mesh=mesh, in_specs=in_specs, out_specs=out_specs, check_vma=False
    )
```

```python
from functools import partial
import math

import jax
import jax.numpy as jnp
from jax import lax
from jax.experimental import pallas as pl
from jax.experimental.pallas import tpu as pltpu
from jax.sharding import PartitionSpec as P

HEADS = 16
HEAD = 64
ADAPTERS = 8


NEG_FILL = -1e30
NORM_EPS = 1e-05


def split_heads(values_in):
    return values_in.reshape(values_in.shape[:-1] + (HEADS, HEAD))


def norm_rows(value, gain, shift):
    centered = value - jnp.mean(value, axis=-1, keepdims=True)
    scaled = centered * lax.rsqrt(jnp.mean(centered * centered, axis=-1, keepdims=True) + NORM_EPS)
    return scaled * gain + shift


def gelu_exact(value):
    return jax.nn.gelu(value, approximate=False)


def choose(onehot, table):
    return jnp.einsum("si,dikr->sdkr", onehot, table, preferred_element_type=jnp.float32).astype(
        jnp.bfloat16
    )


def unpack(gathered, onehot):
    attn_all, fc1_all, fc2_all, vector_all, bias_ff, down_all, up_all, ff_all = gathered
    return (
        attn_all,
        fc1_all,
        fc2_all,
        vector_all.astype(jnp.float32),
        bias_ff.astype(jnp.float32),
        choose(onehot, down_all),
        choose(onehot, up_all),
        choose(onehot, ff_all),
    )


def project(inputs, weight, down_table, up_table):
    frozen_part = jnp.einsum("spd,de->spe", inputs, weight, preferred_element_type=jnp.float32)
    inner_low = jnp.einsum(
        "spd,sdr->spr", inputs, down_table, preferred_element_type=jnp.float32
    ).astype(jnp.bfloat16)
    return (
        frozen_part
        + jnp.einsum("spr,ser->spe", inner_low, up_table, preferred_element_type=jnp.float32),
        inner_low,
    )


def project_back(inputs, inner_low, grad_out, weight, down_table, up_table):
    grad_inner = jnp.einsum(
        "spe,ser->spr", grad_out, up_table, preferred_element_type=jnp.float32
    ).astype(jnp.bfloat16)
    grad_in = jnp.einsum("spe,de->spd", grad_out, weight, preferred_element_type=jnp.float32)
    grad_in = grad_in + jnp.einsum(
        "spr,sdr->spd", grad_inner, down_table, preferred_element_type=jnp.float32
    )
    grad_up = jnp.einsum("spe,spr->ser", grad_out, inner_low, preferred_element_type=jnp.float32)
    grad_down = jnp.einsum("spd,spr->sdr", inputs, grad_inner, preferred_element_type=jnp.float32)
    return (grad_in, grad_down, grad_up)


def block_scores(query_heads, key_block, key_start, lengths):
    block_rows = key_block.shape[1]
    scores = jnp.einsum(
        "sqhd,skhd->shqk", query_heads, split_heads(key_block), preferred_element_type=jnp.float32
    )
    valid_keys = (key_start + jnp.arange(block_rows))[None, :] < lengths[:, None]
    return jnp.where(valid_keys[:, None, None, :], scores, NEG_FILL)


def score_grads(scores, logsum, row_delta, grad_heads, value_heads):
    probs = jnp.exp(scores - logsum[..., None])
    grad_probs = jnp.einsum(
        "sqhd,skhd->shqk", grad_heads, value_heads, preferred_element_type=jnp.float32
    )
    grad_scores = (probs * (grad_probs - row_delta[..., None])).astype(jnp.bfloat16)
    return (grad_scores, probs.astype(jnp.bfloat16))


def attend(query, all_keys, all_values, lengths):
    seq_span = all_keys.shape[1]
    block_rows = math.gcd(seq_span, 512)
    blocks = seq_span // block_rows
    query_heads = split_heads(query)
    slot_count, query_rows = (query.shape[0], query.shape[1])
    stats_shape = (slot_count, HEADS, query_rows)

    def stats_step(running, step_index):
        row_top, row_total = running
        offset = step_index * block_rows
        scores = block_scores(
            query_heads, lax.dynamic_slice_in_dim(all_keys, offset, block_rows, 1), offset, lengths
        )
        new_top = jnp.maximum(row_top, jnp.max(scores, axis=-1))
        row_total = row_total * jnp.exp(row_top - new_top) + jnp.sum(
            jnp.exp(scores - new_top[..., None]), axis=-1
        )
        return ((new_top, row_total), None)

    start_top = jnp.full(stats_shape, NEG_FILL, jnp.float32)
    (row_top, row_total), _ = lax.scan(
        stats_step, (start_top, jnp.zeros(stats_shape, jnp.float32)), jnp.arange(blocks)
    )
    logsum = row_top + jnp.log(row_total)

    def mix_step(running, step_index):
        offset = step_index * block_rows
        scores = block_scores(
            query_heads, lax.dynamic_slice_in_dim(all_keys, offset, block_rows, 1), offset, lengths
        )
        weights_low = jnp.exp(scores - logsum[..., None]).astype(jnp.bfloat16)
        value_heads = split_heads(lax.dynamic_slice_in_dim(all_values, offset, block_rows, 1))
        return (
            running
            + jnp.einsum(
                "shqk,skhd->sqhd", weights_low, value_heads, preferred_element_type=jnp.float32
            ),
            None,
        )

    mixed_heads, _ = lax.scan(
        mix_step, jnp.zeros(query_heads.shape, jnp.float32), jnp.arange(blocks)
    )
    return (mixed_heads.reshape(query.shape), logsum)


def query_side(query, all_keys, all_values, grad_low, logsum, row_delta, lengths):
    seq_span = all_keys.shape[1]
    block_rows = math.gcd(seq_span, 512)
    blocks = seq_span // block_rows
    query_heads = split_heads(query)
    grad_heads = split_heads(grad_low)
    slot_count = query.shape[0]
    width = query.shape[2]

    def step(running, step_index):
        offset = step_index * block_rows
        key_block = lax.dynamic_slice_in_dim(all_keys, offset, block_rows, 1)
        value_block = lax.dynamic_slice_in_dim(all_values, offset, block_rows, 1)
        scores = block_scores(query_heads, key_block, offset, lengths)
        grad_scores, weights_low = score_grads(
            scores, logsum, row_delta, grad_heads, split_heads(value_block)
        )
        grad_acc = running[0] + jnp.einsum(
            "shqk,skhd->sqhd",
            grad_scores,
            split_heads(key_block),
            preferred_element_type=jnp.float32,
        )
        key_part = jnp.einsum(
            "shqk,sqhd->skhd", grad_scores, query_heads, preferred_element_type=jnp.float32
        ).reshape(slot_count, block_rows, width)
        value_part = jnp.einsum(
            "shqk,sqhd->skhd", weights_low, grad_heads, preferred_element_type=jnp.float32
        ).reshape(slot_count, block_rows, width)
        key_buffer = lax.dynamic_update_slice_in_dim(running[1], key_part, offset, 1)
        value_buffer = lax.dynamic_update_slice_in_dim(running[2], value_part, offset, 1)
        return ((grad_acc, key_buffer, value_buffer), None)

    start = (jnp.zeros(query_heads.shape, jnp.float32),)
    empty = jnp.zeros((slot_count, seq_span, width), jnp.float32)
    start = start + (empty, empty)
    result, _ = lax.scan(step, start, jnp.arange(blocks))
    return (result[0].reshape(query.shape), result[1:])


def sum_by_adapter(picks, terms):
    return jnp.einsum("si,sdkr->dikr", picks, terms, precision=lax.Precision.HIGHEST)


def on_device(
    tokens,
    cotangent,
    lengths,
    adapter_ids,
    attn_weight,
    fc1_weight,
    fc2_weight,
    vectors,
    fc1_bias,
    adapter_down,
    adapter_up,
    ff_adapters,
):
    slot_count, slot_rows, width = tokens.shape
    row_start = lax.axis_index("seq") * slot_rows
    positions = row_start + jnp.arange(slot_rows)
    live_rows = (positions[None, :] < lengths[:, None]).astype(jnp.float32)[..., None]
    matches = adapter_ids[:, None] == jnp.arange(ADAPTERS)[None, :]
    onehot_low = matches.astype(jnp.bfloat16)
    onehot_full = matches.astype(jnp.float32)
    gathered = (
        lax.all_gather(attn_weight, ("fsdp", "seq"), axis=0, tiled=True),
        lax.all_gather(fc1_weight, ("fsdp", "seq"), axis=0, tiled=True),
        lax.all_gather(fc2_weight, ("fsdp", "seq"), axis=0, tiled=True),
        lax.all_gather(vectors, ("fsdp", "seq"), axis=0, tiled=True),
        lax.all_gather(fc1_bias, ("fsdp", "seq"), axis=0, tiled=True),
        lax.all_gather(adapter_down, ("fsdp", "seq"), axis=0, tiled=True),
        lax.all_gather(adapter_up, ("fsdp", "seq"), axis=0, tiled=True),
        lax.all_gather(ff_adapters, ("fsdp", "seq"), axis=0, tiled=True),
    )
    attn_all, fc1_all, fc2_all, vector_cols, bias_ff, down_pick, up_pick, ff_pick = unpack(
        gathered, onehot_low
    )
    query_pre, inner_query = project(
        tokens, attn_all[:, 0, :], down_pick[:, :, 0], up_pick[:, :, 0]
    )
    query = ((query_pre + vector_cols[:, 0]) * 0.125).astype(jnp.bfloat16)
    key_pre, inner_key = project(tokens, attn_all[:, 1, :], down_pick[:, :, 1], up_pick[:, :, 1])
    keys = key_pre.astype(jnp.bfloat16)
    value_pre, inner_value = project(
        tokens, attn_all[:, 2, :], down_pick[:, :, 2], up_pick[:, :, 2]
    )
    values = (value_pre + vector_cols[:, 1]).astype(jnp.bfloat16)
    all_keys, all_values = (
        lax.all_gather(keys, "seq", axis=1, tiled=True),
        lax.all_gather(values, "seq", axis=1, tiled=True),
    )
    attended, logsum = attend(query, all_keys, all_values, lengths)
    mixed = attended.astype(jnp.bfloat16)
    branch_pre, inner_branch = project(
        mixed, attn_all[:, 3, :], down_pick[:, :, 3], up_pick[:, :, 3]
    )
    first_sum = tokens.astype(jnp.float32) + branch_pre + vector_cols[:, 2]
    normed, first_back = jax.vjp(
        partial(norm_rows, gain=vector_cols[:, 4], shift=vector_cols[:, 5]), first_sum
    )
    normed_low = normed.astype(jnp.bfloat16)
    hidden_pre, inner_hidden = project(normed_low, fc1_all, down_pick[:, :, 4], ff_pick[:, :, 0])
    activated, gelu_back = jax.vjp(gelu_exact, hidden_pre + bias_ff)
    activated_low = activated.astype(jnp.bfloat16)
    out_pre, inner_out = project(activated_low, fc2_all, ff_pick[:, :, 1], up_pick[:, :, 4])
    second = normed + out_pre + vector_cols[:, 3]
    final, second_back = jax.vjp(
        partial(norm_rows, gain=vector_cols[:, 6], shift=vector_cols[:, 7]), second
    )
    layer_out = (final * live_rows).astype(jnp.bfloat16)
    regathered = (
        lax.all_gather(attn_weight, ("fsdp", "seq"), axis=0, tiled=True),
        lax.all_gather(fc1_weight, ("fsdp", "seq"), axis=0, tiled=True),
        lax.all_gather(fc2_weight, ("fsdp", "seq"), axis=0, tiled=True),
        lax.all_gather(vectors, ("fsdp", "seq"), axis=0, tiled=True),
        lax.all_gather(fc1_bias, ("fsdp", "seq"), axis=0, tiled=True),
        lax.all_gather(adapter_down, ("fsdp", "seq"), axis=0, tiled=True),
        lax.all_gather(adapter_up, ("fsdp", "seq"), axis=0, tiled=True),
        lax.all_gather(ff_adapters, ("fsdp", "seq"), axis=0, tiled=True),
    )
    attn_all, fc1_all, fc2_all, vector_cols, bias_ff, down_pick, up_pick, ff_pick = unpack(
        regathered, onehot_low
    )
    grad_final = cotangent.astype(jnp.float32) * live_rows
    (grad_second,) = second_back(grad_final)
    grad_out_low = grad_second.astype(jnp.bfloat16)
    grad_activated, down_of_fc2, up_of_fc2 = project_back(
        activated_low, inner_out, grad_out_low, fc2_all, ff_pick[:, :, 1], up_pick[:, :, 4]
    )
    (grad_hidden,) = gelu_back(grad_activated)
    grad_hidden_low = grad_hidden.astype(jnp.bfloat16)
    grad_normed, down_of_fc1, up_of_fc1 = project_back(
        normed_low, inner_hidden, grad_hidden_low, fc1_all, down_pick[:, :, 4], ff_pick[:, :, 0]
    )
    (grad_first,) = first_back(grad_normed + grad_second)
    grad_branch_low = grad_first.astype(jnp.bfloat16)
    grad_mixed, down_of_out, up_of_out = project_back(
        mixed,
        inner_branch,
        grad_branch_low,
        attn_all[:, 3, :],
        down_pick[:, :, 3],
        up_pick[:, :, 3],
    )
    grad_mixed_low = grad_mixed.astype(jnp.bfloat16)
    row_delta = jnp.einsum(
        "sqhd,sqhd->shq", split_heads(grad_mixed_low.astype(jnp.float32)), split_heads(attended)
    )
    grad_query, parts = query_side(
        query, all_keys, all_values, grad_mixed_low, logsum, row_delta, lengths
    )
    grad_keys, grad_values = (
        lax.psum_scatter(
            parts[0].astype(jnp.bfloat16), "seq", scatter_dimension=1, tiled=True
        ).astype(jnp.float32),
        lax.psum_scatter(
            parts[1].astype(jnp.bfloat16), "seq", scatter_dimension=1, tiled=True
        ).astype(jnp.float32),
    )
    grad_query_low = grad_query.astype(jnp.bfloat16) * 0.125
    grad_keys_low = grad_keys.astype(jnp.bfloat16)
    grad_values_low = grad_values.astype(jnp.bfloat16)
    grad_from_query, down_of_query, up_of_query = project_back(
        tokens, inner_query, grad_query_low, attn_all[:, 0, :], down_pick[:, :, 0], up_pick[:, :, 0]
    )
    grad_from_key, down_of_key, up_of_key = project_back(
        tokens, inner_key, grad_keys_low, attn_all[:, 1, :], down_pick[:, :, 1], up_pick[:, :, 1]
    )
    grad_from_value, down_of_value, up_of_value = project_back(
        tokens,
        inner_value,
        grad_values_low,
        attn_all[:, 2, :],
        down_pick[:, :, 2],
        up_pick[:, :, 2],
    )
    input_grad = (grad_from_query + grad_from_key + grad_from_value + grad_first).astype(
        jnp.bfloat16
    )
    down_terms = jnp.stack(
        (down_of_query, down_of_key, down_of_value, down_of_out, down_of_fc1), axis=2
    )
    up_terms = jnp.stack((up_of_query, up_of_key, up_of_value, up_of_out, up_of_fc2), axis=2)
    ff_terms = jnp.stack((up_of_fc1, down_of_fc2), axis=2)
    down_table = sum_by_adapter(onehot_full, down_terms)
    up_table = sum_by_adapter(onehot_full, up_terms)
    ff_table = sum_by_adapter(onehot_full, ff_terms)
    down_grad, up_grad, ff_grad = (
        lax.psum_scatter(down_table, ("fsdp", "seq"), scatter_dimension=0, tiled=True),
        lax.psum_scatter(up_table, ("fsdp", "seq"), scatter_dimension=0, tiled=True),
        lax.psum_scatter(ff_table, ("fsdp", "seq"), scatter_dimension=0, tiled=True),
    )
    return (layer_out, input_grad, down_grad, up_grad, ff_grad)


MESH = pl.DeviceIdType.MESH
CHUNKS = 26
DEPTH = 8
ALL2, ALL4 = pl.ds(0, 2), pl.ds(0, 4)


class Spot:
    def __init__(self):
        self.y = lax.axis_index("fsdp")
        self.s = lax.axis_index("seq")
        self.z = self.s // 4
        self.x = (self.s // 2) % 2
        self.c = self.s % 2
        self.pair_z = self.z + 1 - 2 * (self.z % 2)
        self.inner = (self.z + 1) // 2 == 1

    def at(self, dy=0, dz=0, dx=0, dc=0):
        y = (self.y + dy) % 2
        z = (self.z + dz) % 4
        x = (self.x + dx) % 2
        c = (self.c + dc) % 2
        return (y, (z * 2 + x) * 2 + c)


def enter(spot):
    barrier = pltpu.get_barrier_semaphore()
    for step in range(1, 16):
        peer = (spot.y, (spot.s + step) % 16)
        pl.semaphore_signal(barrier, inc=1, device_id=peer, device_id_type=MESH)
    pl.semaphore_signal(barrier, inc=1, device_id=spot.at(dy=1), device_id_type=MESH)
    pl.semaphore_wait(barrier, 16)


class Gather:
    def __init__(self, spot, parts, ways, others, send, recv):
        self.spot, self.parts, self.ways, self.others = spot, parts, ways, others
        self.send, self.recv = send, recv

    def block(self, k, dy=0, dz=0, dx=0, dc=0):
        p = self.spot
        places = ((p.y, dy, 2), (p.z, dz, 4), (p.x, dx, 2), (p.c, dc, 2))
        return self.parts[k].at[tuple((place + d) % n if isinstance(d, int) else d for place, d, n in places)]

    def copy(self, source, target, k, out, into, peer):
        return pltpu.make_async_remote_copy(
            src_ref=source,
            dst_ref=target,
            send_sem=self.send.at[k % DEPTH, out],
            recv_sem=self.recv.at[k % DEPTH, into],
            device_id=peer,
            device_id_type=MESH,
        )

    def push(self, ref, k, out, into, source=None, **hop):
        self.copy(ref if source is None else source, ref, k, out, into, self.spot.at(**hop)).start()

    def arrive(self, like, k, into):
        self.copy(like, like, k, 0, into, self.spot.at(dc=1)).wait_recv()

    def retire(self, k):
        if self.ways[k] == "z":
            pieces = ((1, 3, 1), (2, 3, 2), (2, 3, 2), (1, 4, 1))
        elif self.ways[k] == "h":
            pieces = ((1, 1, 1), (2, 3, 2), (2, 3, 2), (1, 4, 1))

            @pl.when(self.spot.inner)
            def _():
                for out in (4, 5):
                    like = self.pair_of(k, 0)
                    self.copy(like, like, k, out, 0, self.spot.at(dc=1)).wait_send()

        else:
            pieces = ((1, 1, 1), (2, 3, 1), (2, 4, 2), (2, 4, 1))
        for out, (ys, zs, xs) in enumerate(pieces):
            like = self.parts[k].at[pl.ds(0, ys), pl.ds(0, zs), pl.ds(0, xs), 0]
            self.copy(like, like, k, out, 0, self.spot.at(dc=1)).wait_send()

    def pair_of(self, k, far):
        p = self.spot
        return self.parts[k].at[p.y, pl.ds(((p.z // 2 + far) % 2) * 2, 2), p.x, p.c]

    def hand(self, k):
        self.arrive(self.block(k), k, 0)

        @pl.when(self.spot.inner)
        def _():
            self.push_to(self.pair_of(k, 0), k, 4, 5, 3 - self.spot.z)

    def pass_on(self, k):
        @pl.when(self.spot.inner)
        def _():
            self.arrive(self.pair_of(k, 1), k, 5)
            self.push_to(self.pair_of(k, 1), k, 5, 5, self.spot.pair_z)

    def push_to(self, ref, k, out, into, z):
        p = self.spot
        self.copy(ref, ref, k, out, into, (p.y, (z * 2 + p.x) * 2 + p.c)).start()

    def first(self, k):
        if k >= DEPTH:
            self.retire(k - DEPTH)
        if self.ways[k] == "h":
            self.push_to(self.block(k), k, 0, 0, self.spot.pair_z)
        elif self.ways[k] == "z":
            for d in range(1, 4):
                self.push(self.block(k), k, 0, 0, dz=d)
        else:
            self.push(self.block(k), k, 0, 0, self.others.get(k), **{"d" + self.ways[k]: 1})

    def second(self, k):
        if self.ways[k] in "zh":
            if self.ways[k] == "z":
                self.arrive(self.block(k, dz=pl.ds(0, 3)), k, 0)
            else:

                @pl.when(jnp.logical_not(self.spot.inner))
                def _():
                    self.arrive(self.pair_of(k, 1), k, 5)

            line = self.block(k, dz=ALL4)
            self.push(line, k, 1, 1, dx=1)
            self.push(line, k, 1, 2, dy=1)
            self.push(line, k, 1, 4, dc=1)
        else:
            self.arrive(self.block(k), k, 0)
            for d in range(1, 4):
                self.push(self.block(k, **{"d" + self.ways[k]: ALL2}), k, 1, 1, dz=d)

    def third(self, k):
        if self.ways[k] in "zh":
            cut = 3 if k in SHIFTED else 2
            self.arrive(self.block(k, dz=ALL4), k, 1)
            self.push(self.block(k, dz=pl.ds(0, cut), dx=1), k, 2, 3, dy=1)
            self.arrive(self.block(k, dz=ALL4), k, 2)
            self.push(self.block(k, dz=pl.ds(cut, 4 - cut), dy=1), k, 2, 3, dx=1)
            self.push(self.block(k, dz=ALL4, dx=1), k, 2, 4, dc=1)
            self.push(self.block(k, dz=ALL4, dy=1), k, 2, 4, dc=1)
        else:
            near, far = "d" + self.ways[k], "dy" if self.ways[k] == "x" else "dx"
            self.arrive(self.block(k, **{near: ALL2, "dz": pl.ds(0, 3)}), k, 1)
            plane = self.block(k, **{near: ALL2, "dz": ALL4})
            self.push(plane, k, 2, 2, **{far: 1})
            self.push(plane, k, 2, 4, dc=1)

    def fourth(self, k):
        if self.ways[k] in "zh":
            self.arrive(self.block(k, dz=ALL4), k, 3)
            self.push(self.block(k, dz=ALL4, dx=1, dy=1), k, 3, 4, dc=1)
        else:
            near, far = "d" + self.ways[k], "dy" if self.ways[k] == "x" else "dx"
            self.arrive(self.block(k, **{near: ALL2, "dz": ALL4}), k, 2)
            self.push(self.block(k, **{near: ALL2, "dz": ALL4, far: 1}), k, 3, 4, dc=1)

    def ready(self, k):
        self.arrive(self.block(k, dy=ALL2, dz=ALL4, dx=ALL2), k, 4)

    def step(self, t):
        moves = ((0, self.first), (1, self.second), (2, self.third), (3, self.fourth), (4, self.ready))
        hops = ((-2, self.first), (-1, self.hand), (0, self.pass_on)) + moves[1:]
        order = [(late, k, move) for k, way in enumerate(self.ways) for late, move in (hops if way == "h" else moves)]
        for late, k, move in sorted(order, key=lambda entry: (entry[0], entry[1])):
            if k + late == t:
                move(k)

    def finish(self):
        for k in range(len(self.parts) - DEPTH, len(self.parts)):
            self.retire(k)


F32, BF16 = jnp.float32, jnp.bfloat16
ORDER = (0, 1, 24, 25) + tuple(range(2, 24))
WAYS = "zzyyzz" + "h" * 20
SHIFTED = (6, 7, 8, 9, 10, 12, 13, 16)
EARLY, LATE = 80, 32
FAR_FIRST = (2, 1, 3, 0)


def dot(left, right):
    return jnp.dot(left, right, preferred_element_type=F32)


def dot_nt(left, right):
    return lax.dot_general(left, right, (((1,), (1,)), ((), ())), preferred_element_type=F32)


def dot_tn(left, right):
    return lax.dot_general(left, right, (((0,), (0,)), ((), ())), preferred_element_type=F32)


def lanes(shape):
    return lax.broadcasted_iota(jnp.int32, shape, len(shape) - 1)


def half(value, slot):
    low_half = lanes(value.shape) < HEAD
    zero = jnp.zeros_like(value)
    return jnp.where(low_half, value, zero) if slot == 0 else jnp.where(low_half, zero, value)


def pair(first, second):
    return jnp.where(lanes(first.shape) < HEAD, first, second)


def swap(value):
    return pltpu.roll(value, HEAD, 1)


def heads_to_rows(heads, rows, factor):
    for p in range(HEADS // 2):
        even = heads[2 * p].astype(F32) * factor
        odd = heads[2 * p + 1].astype(F32) * factor
        rows[0:64, p * 128 : p * 128 + 128] = pair(even, swap(odd)).astype(BF16)
        rows[64:128, p * 128 : p * 128 + 128] = pair(swap(even), odd).astype(BF16)


class Exchange:
    def __init__(self, spot, out, into, send, recv):
        self.spot, self.out, self.into, self.send, self.recv = spot, out, into, send, recv

    def copy(self, unit, source, target, block, peer):
        return pltpu.make_async_remote_copy(
            src_ref=source,
            dst_ref=target,
            send_sem=self.send.at[unit, block],
            recv_sem=self.recv.at[unit, self.spot.z],
            device_id=(self.spot.y, peer),
            device_id_type=MESH,
        )

    def start(self, unit, block):
        me = self.spot.s

        def body(i, carry):
            peer = block * 4 + i

            @pl.when(peer != me)
            def _():
                self.copy(unit, self.out.at[unit, peer], self.into.at[unit, me], block, peer).start()

            return carry

        lax.fori_loop(0, 4, body, 0)

    def keep(self, unit):
        self.into[unit, self.spot.s] = self.out[unit, self.spot.s]

    def like(self, unit, far):
        return self.into.at[unit, pl.ds(0, 4 if far else 3)]

    def wait_block(self, unit, far):
        block = (self.spot.z + far) % 4
        like = self.like(unit, far)
        pltpu.make_async_copy(like, like, self.recv.at[unit, block]).wait()

    def wait(self, unit):
        for far in range(4):
            self.wait_block(unit, far)

    def finish(self, units):
        for unit in range(units):
            for far in range(4):
                like = self.like(unit, far)
                pltpu.make_async_copy(like, like, self.send.at[unit, (self.spot.z + far) % 4]).wait()


class Scatter:
    def __init__(self, spot, wide, own, core_in, core_sum, x_in, x_sum, into, send, recv):
        self.spot, self.wide = spot, wide
        self.own, self.core_in, self.core_sum = own, core_in, core_sum
        self.x_in, self.x_sum, self.into = x_in, x_sum, into
        self.send, self.recv = send, recv

    def copy(self, source, target, route, peer):
        return pltpu.make_async_remote_copy(
            src_ref=source,
            dst_ref=target,
            send_sem=self.send.at[route],
            recv_sem=self.recv.at[route],
            device_id=peer,
            device_id_type=MESH,
        )

    def first(self):
        p = self.spot
        self.hop = self.copy(self.own.at[:, :, :, 1 - p.c], self.core_in, 0, p.at(dc=1))
        self.hop.start()

    def second(self):
        p = self.spot
        self.hop.wait()
        self.core_sum[...] = (self.own[:, :, :, p.c].astype(F32) + self.core_in[...].astype(F32)).astype(BF16)
        if not self.wide:
            self.hop = self.copy(self.core_sum.at[:, :, 1 - p.x], self.x_in, 1, p.at(dx=1))
            self.hop.start()

    def distances(self):
        every = [(dy, dz, dx) for dy in range(2) for dz in range(4) for dx in range(2 if self.wide else 1)]
        return every[1:]

    def third(self):
        p = self.spot
        if not self.wide:
            self.hop.wait()
            self.x_sum[...] = (self.core_sum[:, :, p.x].astype(F32) + self.x_in[...].astype(F32)).astype(BF16)
        for n, (dy, dz, dx) in enumerate(self.distances()):
            y, z, x = (p.y + dy) % 2, (p.z + dz) % 4, (p.x + dx) % 2
            source = self.core_sum.at[y, z, x] if self.wide else self.x_sum.at[y, z]
            self.copy(source, self.into.at[n], 2, p.at(dy=dy, dz=dz, dx=dx)).start()

    def fourth(self):
        p = self.spot
        self.copy(self.into, self.into, 2, p.at(dc=1)).wait()
        total = [self.core_sum[p.y, p.z, p.x] if self.wide else self.x_sum[p.y, p.z], None]
        total[0] = total[0].astype(F32)
        for n, (dy, _, _) in enumerate(self.distances()):
            term = self.into[n].astype(F32)
            total[dy] = term if total[dy] is None else total[dy] + term
        return total


def scatter_shapes(rows, wide):
    return [
        pltpu.VMEM((2, 4, 2, 2, rows, 128), BF16),
        pltpu.VMEM((2, 4, 2, rows, 128), BF16),
        pltpu.VMEM((2, 4, 2, rows, 128), BF16),
        pltpu.VMEM((2, 4, rows, 128), BF16),
        pltpu.VMEM((2, 4, rows, 128), BF16),
        pltpu.VMEM((15 if wide else 7, rows, 128), BF16),
        pltpu.SemaphoreType.DMA((3,)),
        pltpu.SemaphoreType.DMA((3,)),
    ]


def layer_kernel(*refs):
    it = iter(refs)

    def take(count):
        return [next(it) for _ in range(count)]

    attn, fc1, fc2, tok_far, cot_far, down_table, up_table, ff_table, vec_in, bias_in, lengths, ids = take(12)
    layer_out, input_grad, sums_out, ids_out = take(4)
    wide, tall, rank_all, ff_all = take(4)
    rank_in, rank_up, rank_x, vec, ff_low, bias = take(6)
    heads_out, heads_in = take(2)
    weights_low, weights_back = take(2)
    attended, stat, tmp, sum_one, scaled_one, normed, grad_second, grad_first = take(8)
    tok, cot, mixed, normed_low, out_low, branch_low, query_low, key_low, value_low = take(9)
    slope, act, grad_hidden, inner4 = take(4)
    id_rows, table, rank_other, ff_other = take(4)
    early_refs, up_refs, down_refs = take(8), take(8), take(8)
    own, send, recv, hsend, hrecv, id_sem = take(6)

    spot = Spot()
    here = (spot.y, spot.z, spot.x, spot.c)
    parts = [wide.at[k] for k in range(16)] + [tall.at[k] for k in range(8)] + [rank_all, ff_all]
    placed = [pltpu.make_async_copy(fc2, query_low, own.at[1])]
    for k in range(8):
        placed.append(pltpu.make_async_copy(fc1.at[:, pl.ds(k * 512, 512)], parts[8 + k].at[here], own.at[0]))
    tok_copy = pltpu.make_async_copy(tok_far, tok, own.at[2])
    cot_copy = pltpu.make_async_copy(cot_far, cot, own.at[3])
    tok_copy.start()
    for k in (0, 1):
        wide[(k,) + here] = attn[:, 0, k * 512 : k * 512 + 512]
    for copy in placed:
        copy.start()
    cot_copy.start()
    others = {2: rank_other, 3: ff_other}
    gather = Gather(spot, [parts[k] for k in ORDER], WAYS, others, send, recv)
    swaps = Exchange(spot, heads_out, heads_in, hsend, hrecv)
    early = Scatter(spot, False, *early_refs)
    late_up = Scatter(spot, True, *up_refs)
    late_down = Scatter(spot, True, *down_refs)
    first_row = lax.broadcasted_iota(jnp.int32, (8, 128), 0) == 0
    id_rows[spot.y] = jnp.where(first_row, ids[0], ids[1])
    enter(spot)
    gather.step(0)
    id_copy = pltpu.make_async_remote_copy(
        src_ref=id_rows.at[spot.y],
        dst_ref=id_rows.at[spot.y],
        send_sem=id_sem.at[0],
        recv_sem=id_sem.at[1],
        device_id=spot.at(dy=1),
        device_id_type=MESH,
    )
    id_copy.start()
    for j in range(1, 4):
        for k in range(2):
            wide[(2 * j + k,) + here] = attn[:, j, k * 512 : k * 512 + 512]

    def chosen(source, kind, y, slot):
        who = id_rows[y, slot : slot + 1, 0 : source.shape[3]]
        total = None
        for a in range(ADAPTERS):
            term = jnp.where(who == a, source[a, kind].astype(F32), 0.0)
            total = term if total is None else total + term
        return total

    def pick_all():
        table[...] = jnp.zeros_like(table)
        for g in range(2):
            y = (spot.y + g) % 2
            for slot in range(2):
                for j in range(4):
                    row = g * 384 + j * 32 + slot * 16
                    table[row : row + 16, 0:32] = chosen(down_table, j, y, slot)
                    table[row + 128 : row + 144, 0:32] = chosen(up_table, j, y, slot)
                row = g * 384 + 256 + slot * 16
                table[row : row + 16, 0:32] = chosen(down_table, 4, y, slot)
                table[row + 32 : row + 48, 0:32] = chosen(up_table, 4, y, slot)
                for kind in range(2):
                    row = 768 + g * 64 + kind * 32 + slot * 16
                    table[row : row + 16, :] = chosen(ff_table, kind, y, slot)
        for n in range(3):
            cols = slice(n * 128, n * 128 + 128)
            rank_all[here + (slice(None), cols)] = table[cols, :].T[0:32].astype(BF16)
            rank_other[:, cols] = table[384 + n * 128 : 512 + n * 128, :].T[0:32].astype(BF16)
        turned = table[768:896, :].T
        ff_all[here + (slice(0, 64),)] = pair(turned[0:64], swap(turned[64:128])).astype(BF16)
        ff_other[0:64] = pair(swap(turned[0:64]), turned[64:128]).astype(BF16)
        table[0:8, 0:32] = vec_in[...].astype(F32)
        table[0:8, 32:128] = jnp.zeros((8, 96), F32)
        columns = pltpu.roll(table[0:8, :], (spot.s % 4) * 32, 1)
        rows = jnp.concatenate([jnp.broadcast_to(bias_in[...].astype(F32), (8, 128)), columns], axis=0)
        ff_all[here + (slice(64, 80),)] = rows.astype(BF16)
        ff_other[64:80] = rows.astype(BF16)

    lane = lanes((128, 128))
    row_slot = lax.broadcasted_iota(jnp.int32, (128, 128), 0) >= 64
    slot_lane = ((lane & 16) != 0) == row_slot
    kind4 = [slot_lane & ((lane >> 5) == j) for j in range(4)]
    kind_ff = [slot_lane & ((lane >> 5) == k) for k in range(2)]

    def only(mask, value):
        return jnp.where(mask, value, jnp.zeros_like(value))

    def square(k, t):
        halves = [wide[2 * k + i, t // 2, pl.ds((t % 2) * 2, 2)].reshape(256, 512) for i in range(2)]
        return jnp.concatenate(halves, axis=1)

    def columns(k, n):
        return wide[2 * k + n // 2, :, :, :, :, :, tile(n % 2)].reshape(1024, 256)

    def tile(n, size=256):
        return pl.ds(pl.multiple_of(n * size, size), size)

    def unpack_rank():
        rank_in[...] = rank_all[:, :, :, :, :, 0:128].reshape(1024, 128)
        rank_up[...] = rank_all[:, :, :, :, :, 128:256].reshape(1024, 128)
        rank_x[...] = rank_all[:, :, :, :, :, 256:384].reshape(1024, 128)

    def ff_rows(first, count):
        return ff_low[pl.ds(first, count)].reshape(count * 128, 128)

    def unpack_ff():
        columns_of = {}
        packed = ff_all[:, :, :, :, 0:64, :].reshape(32, 64, 128)
        ff_low[:, 0] = packed
        ff_low[:, 1] = swap(packed.astype(F32).reshape(2048, 128)).astype(BF16).reshape(32, 64, 128)
        for o in range(32):
            y, z, x, c = o // 16, (o // 4) % 4, (o // 2) % 2, o % 2
            rows = ff_all[y, z, x, c, 64:80, :].astype(F32)
            bias[:, o * 128 : o * 128 + 128] = rows[0:8]
            columns_of[o // 4] = rows[8:16] if o % 4 == 0 else columns_of[o // 4] + rows[8:16]
        for n in range(8):
            vec[:, n * 128 : n * 128 + 128] = columns_of[n]

    def to_heads(unit, block, value):
        for p in range(2):
            first = value[0:64, p * 128 : p * 128 + 128]
            second = value[64:128, p * 128 : p * 128 + 128]
            heads_out[unit, block * 4 + 2 * p] = pair(first, swap(second)).astype(BF16)
            heads_out[unit, block * 4 + 2 * p + 1] = pair(swap(first), second).astype(BF16)
        swaps.start(unit, block)

    def turn(body, unrolled=False):
        def shifted(t, carry):
            body((spot.z + t) % 4)
            return carry

        if unrolled:
            for t in FAR_FIRST:
                shifted(t, 0)
        else:
            lax.fori_loop(0, 4, shifted, 0)

    def project_in(j):
        inner = only(kind4[j], inner4[...])

        def body(n):
            cols = tile(n)
            value = dot(tok[...], columns(j, n)) + dot_nt(inner, rank_up[cols, :])
            if j == 0:
                value = (value + vec[0:1, cols]) * 0.125
            if j == 2:
                value = value + vec[1:2, cols]
            to_heads(j, n, value)

        turn(body)
        swaps.keep(j)

    def attention(t):
        if t == 0:
            for j in range(3):
                swaps.wait(j)
        block = (spot.z + t) % 4
        keys = heads_in[1].reshape(1024, 128)
        values = heads_in[2].reshape(1024, 128)
        rows = tile(block)
        query = heads_in[0, pl.ds(block * 4, 4)].reshape(256, 128)
        results, stats = [], []
        for slot in range(2):
            scores = dot_nt(half(query, slot), keys)
            scores = jnp.where(lanes(scores.shape) < lengths[slot], scores, NEG_FILL)
            top = jnp.max(scores, axis=-1, keepdims=True)
            shifted = jnp.exp(scores - top)
            total = jnp.sum(shifted, axis=-1, keepdims=True)
            low = (shifted * (1.0 / total)).astype(BF16)
            weights_low[slot, rows, :] = low
            results.append(dot(low, values))
            stats.append(jnp.broadcast_to(top + jnp.log(total), (256, 128)))
        result = pair(results[0], results[1])
        attended[rows, :] = result
        heads_out[3, pl.ds(block * 4, 4)] = result.astype(BF16).reshape(4, 64, 128)
        stat[rows, :] = pair(stats[0], stats[1])
        swaps.start(3, block)
        if t == 3:
            swaps.keep(3)

    def attention_turned(first):
        logsum = stat[...].T
        queries = heads_in[0].reshape(1024, 128)
        turned = [logsum[0:1], logsum[64:65]]

        def body(t, carry):
            rows = tile(t)
            keys = heads_in[1, pl.ds(t * 4, 4)].reshape(256, 128)
            for slot in range(2):
                scores = dot_nt(half(keys, slot), queries)
                weights = jnp.exp(scores - turned[slot])
                place = lax.broadcasted_iota(jnp.int32, weights.shape, 0) + t * 256
                weights = jnp.where(place < lengths[slot], weights, 0.0)
                weights_back[slot, rows, :] = weights.astype(BF16)
            return carry

        lax.fori_loop(first, first + 2, body, 0)

    def normalize(value):
        centered = value - jnp.mean(value, axis=-1, keepdims=True)
        spread = lax.rsqrt(jnp.mean(centered * centered, axis=-1, keepdims=True) + NORM_EPS)
        return centered * spread, spread

    def normalize_back(grad, scaled, spread):
        shift = jnp.mean(grad, axis=-1, keepdims=True)
        along = jnp.mean(grad * scaled, axis=-1, keepdims=True)
        return spread * (grad - shift - scaled * along)

    saved = {}

    def branch():
        swaps.wait(3)
        heads_to_rows(heads_in.at[3], mixed, 1.0)
        saved["o"] = only(kind4[3], dot(mixed[...], rank_in[...])).astype(BF16)

        def body(n, carry):
            cols = tile(n)
            value = dot(mixed[...], columns(3, n)) + dot_nt(saved["o"], rank_up[cols, :])
            sum_one[:, cols] = tok[:, cols].astype(F32) + value + vec[2:3, cols]
            return carry

        lax.fori_loop(0, 4, body, 0)
        scaled, saved["spread_one"] = normalize(sum_one[...])
        scaled_one[...] = scaled
        value = scaled * vec[4:5] + vec[5:6]
        normed[...] = value
        normed_low[...] = value.astype(BF16)
        saved["hidden"] = only(kind_ff[0], dot(normed_low[...], rank_x[...])).astype(BF16)

    def expand(k):
        def body(i, carry):
            n = k * 2 + i
            cols = tile(n)
            value = dot(normed_low[...], wide[8 + k, :, :, :, :, :, tile(i)].reshape(1024, 256))
            value = value + dot_nt(saved["hidden"], ff_rows(n * 2, 2)) + bias[0:1, cols]
            share = 0.5 * (1.0 + lax.erf(value * math.sqrt(0.5)))
            act[:, cols] = (value * share).astype(BF16)
            bell = jnp.exp(-0.5 * value * value) * (1.0 / math.sqrt(2.0 * math.pi))
            slope[:, cols] = share + value * bell
            return carry

        lax.fori_loop(0, 2, body, 0)

    def contract(q):
        if q == 0:
            saved["out"] = only(kind_ff[1], dot(act[...], ff_rows(0, 32))).astype(BF16)
        cols = slice(q * 256, q * 256 + 256)
        halves = []
        for k in (2 * q, 2 * q + 1):
            places = [(o // 16, (o // 4) % 4, (o // 2) % 2, o % 2) for o in range(32)]
            halves.append(jnp.concatenate([tall[(k,) + place] for place in places], axis=1))
        value = dot_nt(act[...], jnp.concatenate(halves, axis=0)) + dot_nt(saved["out"], rank_x[cols, :])
        tmp[:, cols] = normed[:, cols] + value + vec[3:4, cols]

    def outer():
        rows = lax.broadcasted_iota(jnp.int32, (128, 1), 0)
        place = spot.s * 64 + (rows & 63)
        limit = jnp.where(rows < 64, lengths[0], lengths[1])
        live = (place < limit).astype(F32)
        scaled, spread = normalize(tmp[...])
        layer_out[...] = (live * (scaled * vec[6:7] + vec[7:8])).astype(BF16)
        grad = normalize_back(live * cot[...].astype(F32) * vec[6:7], scaled, spread)
        grad_second[...] = grad
        out_low[...] = grad.astype(BF16)
        saved["g_out"] = only(kind_ff[1], dot(out_low[...], rank_x[...])).astype(BF16)

    def hidden_back():
        def body(t, carry):
            rows = tile(t)
            pieces = [tall[:, t // 8, (t // 2) % 4, t % 2, c].reshape(1024, 128) for c in range(2)]
            value = dot(out_low[...], jnp.concatenate(pieces, axis=1))
            value = value + dot_nt(saved["g_out"], ff_rows(t * 2, 2))
            grad_hidden[:, rows] = (value * slope[:, rows]).astype(BF16)
            return carry

        lax.fori_loop(0, 16, body, 0, unroll=True)
        saved["g_hidden"] = only(kind_ff[0], dot(grad_hidden[...], ff_rows(0, 32))).astype(BF16)

    def normed_back():
        def body(t, carry):
            rows = tile(t)
            value = dot_nt(saved["g_hidden"], rank_x[rows, :]) + grad_second[:, rows]
            for q in range(4):
                value = value + dot_nt(grad_hidden[:, q * 1024 : q * 1024 + 1024], square(4 + q, t))
            tmp[:, rows] = value
            return carry

        lax.fori_loop(0, 4, body, 0, unroll=True)
        grad = normalize_back(tmp[...] * vec[4:5], scaled_one[...], saved["spread_one"])
        grad_first[...] = grad
        branch_low[...] = grad.astype(BF16)
        saved["g_o"] = only(kind4[3], dot(branch_low[...], rank_up[...])).astype(BF16)

    def mixed_back():
        def body(n):
            value = dot_nt(branch_low[...], square(3, n)) + dot_nt(saved["g_o"], rank_in[tile(n), :])
            to_heads(4, n, value)

        turn(body, True)
        swaps.keep(4)

    def early_grads():
        own_grads = early.own
        value = dot_tn(normed_low[...], saved["g_hidden"]) + dot_tn(out_low[...], saved["out"])
        value = value.reshape(32, 2, 16, 128)
        value = value[:, 0] + swap(value[:, 1].reshape(512, 128)).reshape(32, 16, 128)
        own_grads[:, :, :, :, 0:16, :] = value.astype(BF16).reshape(2, 4, 2, 2, 16, 128)
        for y in range(2):
            for z in range(4):
                cols = slice((y * 4 + z) * 512, (y * 4 + z) * 512 + 512)
                value = dot_tn(grad_hidden[:, cols], saved["hidden"]) + dot_tn(act[:, cols], saved["g_out"])
                value = value.reshape(4, 128, 128)
                for o in range(4):
                    packed = value[o, 0:64] + swap(value[o, 64:128])
                    own_grads[y, z, o // 2, o % 2, 16:80, :] = packed.astype(BF16)

    def query_back(t):
        block = (spot.z + 4 - t) % 4
        swaps.wait_block(4, (4 - t) % 4)
        rows = tile(block)
        keys = heads_in[1].reshape(1024, 128)
        values = heads_in[2].reshape(1024, 128)
        grad_block = heads_in[4, pl.ds(block * 4, 4)].reshape(256, 128)
        product = grad_block.astype(F32) * attended[rows, :]
        parts_, deltas = [], []
        for slot in range(2):
            delta = jnp.sum(half(product, slot), axis=-1, keepdims=True)
            grad_probs = dot_nt(half(grad_block, slot), values)
            weights = weights_low[slot, rows, :].astype(F32)
            grad_scores = (weights * (grad_probs - delta)).astype(BF16)
            parts_.append(dot(grad_scores, keys))
            deltas.append(jnp.broadcast_to(delta, (256, 128)))
        heads_out[5, pl.ds(block * 4, 4)] = pair(*parts_).astype(BF16).reshape(4, 64, 128)
        stat[rows, :] = pair(*deltas)
        swaps.start(5, block)
        if t == FAR_FIRST[-1]:
            swaps.keep(5)

    def key_back():
        queries = heads_in[0].reshape(1024, 128)
        grads = heads_in[4].reshape(1024, 128)
        turned = stat[...].T
        turned = [turned[0:1], turned[64:65]]

        def body(block):
            rows = tile(block)
            value_block = heads_in[2, pl.ds(block * 4, 4)].reshape(256, 128)
            key_parts, value_parts = [], []
            for slot in range(2):
                weights = weights_back[slot, rows, :]
                grad_probs = dot_nt(half(value_block, slot), grads)
                grad_scores = (weights.astype(F32) * (grad_probs - turned[slot])).astype(BF16)
                key_parts.append(dot(grad_scores, queries))
                value_parts.append(dot(weights, grads))
            heads_out[6, pl.ds(block * 4, 4)] = pair(*key_parts).astype(BF16).reshape(4, 64, 128)
            heads_out[7, pl.ds(block * 4, 4)] = pair(*value_parts).astype(BF16).reshape(4, 64, 128)
            swaps.start(6, block)
            swaps.start(7, block)

        turn(body, True)
        swaps.keep(6)
        swaps.keep(7)

    def inputs_back():
        grads = (query_low, key_low, value_low)
        ups = dot_tn(branch_low[...], saved["o"])
        downs = dot_tn(mixed[...], saved["g_o"])
        for j, grad in enumerate(grads):
            swaps.wait(5 + j)
            heads_to_rows(heads_in.at[5 + j], grad, 0.125 if j == 0 else 1.0)
            ups = ups + dot_tn(grad[...], only(kind4[j], inner4[...]))
        late_up.own[...] = ups.astype(BF16).reshape(2, 4, 2, 2, 32, 128)
        late_up.first()
        inner = jnp.zeros((128, 128), F32)
        for j, grad in enumerate(grads):
            inner = jnp.where(kind4[j], dot(grad[...], rank_up[...]), inner)
        saved["g_in"] = inner.astype(BF16)
        downs = downs + dot_tn(tok[...], saved["g_in"])
        late_down.own[...] = downs.astype(BF16).reshape(2, 4, 2, 2, 32, 128)
        late_down.first()
        late_up.second()
        late_up.third()
        late_down.second()
        late_down.third()

    def tokens_back(t):
        rows = pl.ds(t * 256, 256)
        value = dot_nt(saved["g_in"], rank_in[rows, :]) + grad_first[:, rows]
        for j, grad in enumerate((query_low, key_low, value_low)):
            value = value + dot_nt(grad[...], square(j, t))
        input_grad[:, rows] = value.astype(BF16)

    for t in range(1, CHUNKS + 4):
        if t == 2:
            id_copy.wait_recv()
            pick_all()
        if t == 4:
            like = wide.at[(pl.ds(8, 8),) + here]
            pltpu.make_async_copy(like, like, own.at[0]).wait()
            placed[0].wait()
            for k in range(8):
                turned = query_low[:, k * 128 : k * 128 + 128].astype(F32).T
                tall[(k,) + here] = turned.astype(BF16)
        gather.step(t)
        if t == 7:
            tok_copy.wait()
            unpack_rank()
            unpack_ff()
            inner4[...] = dot(tok[...], rank_in[...]).astype(BF16)
        if t in (7, 9, 11):
            project_in((t - 7) // 2)
        if 14 <= t <= 17:
            attention(t - 14)
        if 18 <= t <= 19:
            attention_turned((t - 18) * 2)
        if t == 20:
            branch()
        if 21 <= t <= 24:
            expand(2 * t - 42)
            expand(2 * t - 41)
        if t == 27:
            contract(0)
        if t >= 27:
            contract(t - 26)
    cot_copy.wait()
    outer()
    hidden_back()
    normed_back()
    mixed_back()
    early_grads()
    early.first()
    for t in FAR_FIRST:
        query_back(t)
    early.second()
    key_back()
    early.third()
    inputs_back()
    for t in range(4):
        tokens_back(t)
    for first, scatter in ((0, early), (EARLY, late_down), (EARLY + LATE, late_up)):
        for dy, total in enumerate(scatter.fourth()):
            sums_out[dy, first : first + total.shape[0], :] = total
    for dy in range(2):
        ids_out[dy] = id_rows[(spot.y + dy) % 2]
    id_copy.wait_send()
    gather.finish()
    swaps.finish(8)


def hand_on_kernel(layer_in, grad_in, sums, ids, layer_out, grad_out, down_out, up_out, ff_out):
    layer_out[...] = layer_in[...]
    grad_out[...] = grad_in[...]
    turned, ff_turned = [], []
    for dy in range(2):
        packed = sums[dy, 16:80, :]
        ff_turned.append(jnp.concatenate([packed, swap(packed)], axis=0).T)
        cross = sums[dy, 0:16, :]
        rows = [sums[dy, EARLY : EARLY + 2 * LATE, :], cross, swap(cross), jnp.zeros((32, 128), F32)]
        turned.append(jnp.concatenate(rows, axis=0).T)
    for a in range(ADAPTERS):
        share = [(ids[dy, 0:2, :] == a).astype(F32) for dy in range(2)]

        def spread(source, first):
            total = None
            for dy in range(2):
                for slot in range(2):
                    row = first + slot * 16
                    term = share[dy][slot : slot + 1] * source[dy][row : row + 16, :]
                    total = term if total is None else total + term
            return total

        for j in range(4):
            value = spread(turned, j * 32)
            down_out[a, j] = value[:, 0:32]
            up_out[a, j] = value[:, 32:64]
        down_out[a, 4] = spread(turned, 0)[:, 64:96]
        up_out[a, 4] = spread(turned, 32)[:, 64:96]
        for kind in range(2):
            ff_out[a, kind] = spread(ff_turned, kind * 32)


def hand_on(arrays, shapes):
    near = pl.BlockSpec(memory_space=pltpu.VMEM)
    return pl.pallas_call(
        hand_on_kernel,
        out_shape=[jax.ShapeDtypeStruct(array.shape, array.dtype) for array in arrays[:2]]
        + [jax.ShapeDtypeStruct(shape, F32) for shape in shapes],
        in_specs=[near] * 4,
        out_specs=[near] * 5,
        name="hand_on",
    )(*arrays)


def layer(attn, fc1, fc2, tok, cot, down, up, ff, vec, bias, lengths, ids):
    lead = (2, 4, 2, 2)
    anywhere = pl.BlockSpec(memory_space=pl.ANY)
    near = pl.BlockSpec(memory_space=pltpu.VMEM)
    scalar = pl.BlockSpec(memory_space=pltpu.SMEM)

    def buffer(*shape, dtype=BF16):
        return pltpu.VMEM(shape, dtype)

    scratch = [
        buffer(16, *lead, 32, 512),
        buffer(8, *lead, 128, 128),
        buffer(*lead, 32, 384),
        buffer(*lead, 80, 128),
    ]
    scratch += [buffer(1024, 128)] * 3 + [buffer(8, 1024, dtype=F32), buffer(32, 2, 64, 128)]
    scratch += [buffer(8, 4096, dtype=F32)]
    scratch += [buffer(8, 16, 64, 128)] * 2
    scratch += [buffer(2, 1024, 1024)] * 2
    scratch += [buffer(1024, 128, dtype=F32)] * 2
    scratch += [buffer(128, 1024, dtype=F32)] * 6
    scratch += [buffer(128, 1024)] * 9
    scratch += [buffer(128, 4096, dtype=F32), buffer(128, 4096), buffer(128, 4096), buffer(128, 128)]
    scratch += [buffer(2, 8, 128, dtype=jnp.int32), buffer(896, 128, dtype=F32)]
    scratch += [buffer(32, 384), buffer(80, 128)]
    scratch += scatter_shapes(EARLY, False) + scatter_shapes(LATE, True) * 2
    scratch += [pltpu.SemaphoreType.DMA((4,))]
    scratch += [pltpu.SemaphoreType.DMA((DEPTH, 6))] * 2
    scratch += [pltpu.SemaphoreType.DMA((8, 4))] * 2
    scratch += [pltpu.SemaphoreType.DMA((2,))]
    return pl.pallas_call(
        layer_kernel,
        out_shape=[
            jax.ShapeDtypeStruct(tok.shape, BF16),
            jax.ShapeDtypeStruct(tok.shape, BF16),
            jax.ShapeDtypeStruct((2, EARLY + 2 * LATE, 128), F32),
            jax.ShapeDtypeStruct((2, 8, 128), jnp.int32),
        ],
        in_specs=[near] + [anywhere] * 4 + [near] * 5 + [scalar] * 2,
        out_specs=[near] * 4,
        scratch_shapes=scratch,
        compiler_params=pltpu.CompilerParams(
            collective_id=0, has_side_effects=True, vmem_limit_bytes=63 * 2**20
        ),
        name="layer",
    )(attn, fc1, fc2, tok, cot, down, up, ff, vec, bias, lengths, ids)


def fast_device(
    tokens,
    cotangent,
    lengths,
    adapter_ids,
    attn_weight,
    fc1_weight,
    fc2_weight,
    vectors,
    fc1_bias,
    adapter_down,
    adapter_up,
    ff_adapters,
):
    width = tokens.shape[2]
    tables = [table.transpose(1, 2, 3, 0) for table in (adapter_down, adapter_up, ff_adapters)]
    outs = layer(
        attn_weight,
        fc1_weight,
        fc2_weight,
        tokens.reshape(-1, width),
        cotangent.reshape(-1, width),
        *tables,
        vectors.T,
        fc1_bias[None],
        lengths,
        adapter_ids,
    )
    outs = hand_on(outs, [table.shape for table in tables])
    grads = [grad.transpose(3, 0, 1, 2) for grad in outs[2:]]
    return (outs[0].reshape(tokens.shape), outs[1].reshape(tokens.shape), *grads)


def solution(mesh):
    in_specs = (
        P("fsdp", "seq", None),
        P("fsdp", "seq", None),
        P("fsdp"),
        P("fsdp"),
        P(("fsdp", "seq"), None, None),
        P(("fsdp", "seq"), None),
        P(("fsdp", "seq"), None),
        P(("fsdp", "seq"), None),
        P(("fsdp", "seq")),
        P(("fsdp", "seq"), None, None, None),
        P(("fsdp", "seq"), None, None, None),
        P(("fsdp", "seq"), None, None, None),
    )
    out_specs = (
        P("fsdp", "seq", None),
        P("fsdp", "seq", None),
        P(("fsdp", "seq"), None, None, None),
        P(("fsdp", "seq"), None, None, None),
        P(("fsdp", "seq"), None, None, None),
    )
    fast = mesh.shape["fsdp"] == 2 and mesh.shape["seq"] == HEADS
    return jax.shard_map(
        fast_device if fast else on_device, mesh=mesh, in_specs=in_specs, out_specs=out_specs, check_vma=False
    )
```

```python
from functools import partial
import math

import jax
import jax.numpy as jnp
from jax import lax
from jax.experimental import pallas as pl
from jax.experimental.pallas import tpu as pltpu
from jax.sharding import PartitionSpec as P

HEADS = 16
HEAD = 64
ADAPTERS = 8


NEG_FILL = -1e30
NORM_EPS = 1e-05


def split_heads(values_in):
    return values_in.reshape(values_in.shape[:-1] + (HEADS, HEAD))


def norm_rows(value, gain, shift):
    centered = value - jnp.mean(value, axis=-1, keepdims=True)
    scaled = centered * lax.rsqrt(jnp.mean(centered * centered, axis=-1, keepdims=True) + NORM_EPS)
    return scaled * gain + shift


def gelu_exact(value):
    return jax.nn.gelu(value, approximate=False)


def choose(onehot, table):
    return jnp.einsum("si,dikr->sdkr", onehot, table, preferred_element_type=jnp.float32).astype(
        jnp.bfloat16
    )


def unpack(gathered, onehot):
    attn_all, fc1_all, fc2_all, vector_all, bias_ff, down_all, up_all, ff_all = gathered
    return (
        attn_all,
        fc1_all,
        fc2_all,
        vector_all.astype(jnp.float32),
        bias_ff.astype(jnp.float32),
        choose(onehot, down_all),
        choose(onehot, up_all),
        choose(onehot, ff_all),
    )


def project(inputs, weight, down_table, up_table):
    frozen_part = jnp.einsum("spd,de->spe", inputs, weight, preferred_element_type=jnp.float32)
    inner_low = jnp.einsum(
        "spd,sdr->spr", inputs, down_table, preferred_element_type=jnp.float32
    ).astype(jnp.bfloat16)
    return (
        frozen_part
        + jnp.einsum("spr,ser->spe", inner_low, up_table, preferred_element_type=jnp.float32),
        inner_low,
    )


def project_back(inputs, inner_low, grad_out, weight, down_table, up_table):
    grad_inner = jnp.einsum(
        "spe,ser->spr", grad_out, up_table, preferred_element_type=jnp.float32
    ).astype(jnp.bfloat16)
    grad_in = jnp.einsum("spe,de->spd", grad_out, weight, preferred_element_type=jnp.float32)
    grad_in = grad_in + jnp.einsum(
        "spr,sdr->spd", grad_inner, down_table, preferred_element_type=jnp.float32
    )
    grad_up = jnp.einsum("spe,spr->ser", grad_out, inner_low, preferred_element_type=jnp.float32)
    grad_down = jnp.einsum("spd,spr->sdr", inputs, grad_inner, preferred_element_type=jnp.float32)
    return (grad_in, grad_down, grad_up)


def block_scores(query_heads, key_block, key_start, lengths):
    block_rows = key_block.shape[1]
    scores = jnp.einsum(
        "sqhd,skhd->shqk", query_heads, split_heads(key_block), preferred_element_type=jnp.float32
    )
    valid_keys = (key_start + jnp.arange(block_rows))[None, :] < lengths[:, None]
    return jnp.where(valid_keys[:, None, None, :], scores, NEG_FILL)


def score_grads(scores, logsum, row_delta, grad_heads, value_heads):
    probs = jnp.exp(scores - logsum[..., None])
    grad_probs = jnp.einsum(
        "sqhd,skhd->shqk", grad_heads, value_heads, preferred_element_type=jnp.float32
    )
    grad_scores = (probs * (grad_probs - row_delta[..., None])).astype(jnp.bfloat16)
    return (grad_scores, probs.astype(jnp.bfloat16))


def attend(query, all_keys, all_values, lengths):
    seq_span = all_keys.shape[1]
    block_rows = math.gcd(seq_span, 512)
    blocks = seq_span // block_rows
    query_heads = split_heads(query)
    slot_count, query_rows = (query.shape[0], query.shape[1])
    stats_shape = (slot_count, HEADS, query_rows)

    def stats_step(running, step_index):
        row_top, row_total = running
        offset = step_index * block_rows
        scores = block_scores(
            query_heads, lax.dynamic_slice_in_dim(all_keys, offset, block_rows, 1), offset, lengths
        )
        new_top = jnp.maximum(row_top, jnp.max(scores, axis=-1))
        row_total = row_total * jnp.exp(row_top - new_top) + jnp.sum(
            jnp.exp(scores - new_top[..., None]), axis=-1
        )
        return ((new_top, row_total), None)

    start_top = jnp.full(stats_shape, NEG_FILL, jnp.float32)
    (row_top, row_total), _ = lax.scan(
        stats_step, (start_top, jnp.zeros(stats_shape, jnp.float32)), jnp.arange(blocks)
    )
    logsum = row_top + jnp.log(row_total)

    def mix_step(running, step_index):
        offset = step_index * block_rows
        scores = block_scores(
            query_heads, lax.dynamic_slice_in_dim(all_keys, offset, block_rows, 1), offset, lengths
        )
        weights_low = jnp.exp(scores - logsum[..., None]).astype(jnp.bfloat16)
        value_heads = split_heads(lax.dynamic_slice_in_dim(all_values, offset, block_rows, 1))
        return (
            running
            + jnp.einsum(
                "shqk,skhd->sqhd", weights_low, value_heads, preferred_element_type=jnp.float32
            ),
            None,
        )

    mixed_heads, _ = lax.scan(
        mix_step, jnp.zeros(query_heads.shape, jnp.float32), jnp.arange(blocks)
    )
    return (mixed_heads.reshape(query.shape), logsum)


def query_side(query, all_keys, all_values, grad_low, logsum, row_delta, lengths):
    seq_span = all_keys.shape[1]
    block_rows = math.gcd(seq_span, 512)
    blocks = seq_span // block_rows
    query_heads = split_heads(query)
    grad_heads = split_heads(grad_low)
    slot_count = query.shape[0]
    width = query.shape[2]

    def step(running, step_index):
        offset = step_index * block_rows
        key_block = lax.dynamic_slice_in_dim(all_keys, offset, block_rows, 1)
        value_block = lax.dynamic_slice_in_dim(all_values, offset, block_rows, 1)
        scores = block_scores(query_heads, key_block, offset, lengths)
        grad_scores, weights_low = score_grads(
            scores, logsum, row_delta, grad_heads, split_heads(value_block)
        )
        grad_acc = running[0] + jnp.einsum(
            "shqk,skhd->sqhd",
            grad_scores,
            split_heads(key_block),
            preferred_element_type=jnp.float32,
        )
        key_part = jnp.einsum(
            "shqk,sqhd->skhd", grad_scores, query_heads, preferred_element_type=jnp.float32
        ).reshape(slot_count, block_rows, width)
        value_part = jnp.einsum(
            "shqk,sqhd->skhd", weights_low, grad_heads, preferred_element_type=jnp.float32
        ).reshape(slot_count, block_rows, width)
        key_buffer = lax.dynamic_update_slice_in_dim(running[1], key_part, offset, 1)
        value_buffer = lax.dynamic_update_slice_in_dim(running[2], value_part, offset, 1)
        return ((grad_acc, key_buffer, value_buffer), None)

    start = (jnp.zeros(query_heads.shape, jnp.float32),)
    empty = jnp.zeros((slot_count, seq_span, width), jnp.float32)
    start = start + (empty, empty)
    result, _ = lax.scan(step, start, jnp.arange(blocks))
    return (result[0].reshape(query.shape), result[1:])


def sum_by_adapter(picks, terms):
    return jnp.einsum("si,sdkr->dikr", picks, terms, precision=lax.Precision.HIGHEST)


def on_device(
    tokens,
    cotangent,
    lengths,
    adapter_ids,
    attn_weight,
    fc1_weight,
    fc2_weight,
    vectors,
    fc1_bias,
    adapter_down,
    adapter_up,
    ff_adapters,
):
    slot_count, slot_rows, width = tokens.shape
    row_start = lax.axis_index("seq") * slot_rows
    positions = row_start + jnp.arange(slot_rows)
    live_rows = (positions[None, :] < lengths[:, None]).astype(jnp.float32)[..., None]
    matches = adapter_ids[:, None] == jnp.arange(ADAPTERS)[None, :]
    onehot_low = matches.astype(jnp.bfloat16)
    onehot_full = matches.astype(jnp.float32)
    gathered = (
        lax.all_gather(attn_weight, ("fsdp", "seq"), axis=0, tiled=True),
        lax.all_gather(fc1_weight, ("fsdp", "seq"), axis=0, tiled=True),
        lax.all_gather(fc2_weight, ("fsdp", "seq"), axis=0, tiled=True),
        lax.all_gather(vectors, ("fsdp", "seq"), axis=0, tiled=True),
        lax.all_gather(fc1_bias, ("fsdp", "seq"), axis=0, tiled=True),
        lax.all_gather(adapter_down, ("fsdp", "seq"), axis=0, tiled=True),
        lax.all_gather(adapter_up, ("fsdp", "seq"), axis=0, tiled=True),
        lax.all_gather(ff_adapters, ("fsdp", "seq"), axis=0, tiled=True),
    )
    attn_all, fc1_all, fc2_all, vector_cols, bias_ff, down_pick, up_pick, ff_pick = unpack(
        gathered, onehot_low
    )
    query_pre, inner_query = project(
        tokens, attn_all[:, 0, :], down_pick[:, :, 0], up_pick[:, :, 0]
    )
    query = ((query_pre + vector_cols[:, 0]) * 0.125).astype(jnp.bfloat16)
    key_pre, inner_key = project(tokens, attn_all[:, 1, :], down_pick[:, :, 1], up_pick[:, :, 1])
    keys = key_pre.astype(jnp.bfloat16)
    value_pre, inner_value = project(
        tokens, attn_all[:, 2, :], down_pick[:, :, 2], up_pick[:, :, 2]
    )
    values = (value_pre + vector_cols[:, 1]).astype(jnp.bfloat16)
    all_keys, all_values = (
        lax.all_gather(keys, "seq", axis=1, tiled=True),
        lax.all_gather(values, "seq", axis=1, tiled=True),
    )
    attended, logsum = attend(query, all_keys, all_values, lengths)
    mixed = attended.astype(jnp.bfloat16)
    branch_pre, inner_branch = project(
        mixed, attn_all[:, 3, :], down_pick[:, :, 3], up_pick[:, :, 3]
    )
    first_sum = tokens.astype(jnp.float32) + branch_pre + vector_cols[:, 2]
    normed, first_back = jax.vjp(
        partial(norm_rows, gain=vector_cols[:, 4], shift=vector_cols[:, 5]), first_sum
    )
    normed_low = normed.astype(jnp.bfloat16)
    hidden_pre, inner_hidden = project(normed_low, fc1_all, down_pick[:, :, 4], ff_pick[:, :, 0])
    activated, gelu_back = jax.vjp(gelu_exact, hidden_pre + bias_ff)
    activated_low = activated.astype(jnp.bfloat16)
    out_pre, inner_out = project(activated_low, fc2_all, ff_pick[:, :, 1], up_pick[:, :, 4])
    second = normed + out_pre + vector_cols[:, 3]
    final, second_back = jax.vjp(
        partial(norm_rows, gain=vector_cols[:, 6], shift=vector_cols[:, 7]), second
    )
    layer_out = (final * live_rows).astype(jnp.bfloat16)
    regathered = (
        lax.all_gather(attn_weight, ("fsdp", "seq"), axis=0, tiled=True),
        lax.all_gather(fc1_weight, ("fsdp", "seq"), axis=0, tiled=True),
        lax.all_gather(fc2_weight, ("fsdp", "seq"), axis=0, tiled=True),
        lax.all_gather(vectors, ("fsdp", "seq"), axis=0, tiled=True),
        lax.all_gather(fc1_bias, ("fsdp", "seq"), axis=0, tiled=True),
        lax.all_gather(adapter_down, ("fsdp", "seq"), axis=0, tiled=True),
        lax.all_gather(adapter_up, ("fsdp", "seq"), axis=0, tiled=True),
        lax.all_gather(ff_adapters, ("fsdp", "seq"), axis=0, tiled=True),
    )
    attn_all, fc1_all, fc2_all, vector_cols, bias_ff, down_pick, up_pick, ff_pick = unpack(
        regathered, onehot_low
    )
    grad_final = cotangent.astype(jnp.float32) * live_rows
    (grad_second,) = second_back(grad_final)
    grad_out_low = grad_second.astype(jnp.bfloat16)
    grad_activated, down_of_fc2, up_of_fc2 = project_back(
        activated_low, inner_out, grad_out_low, fc2_all, ff_pick[:, :, 1], up_pick[:, :, 4]
    )
    (grad_hidden,) = gelu_back(grad_activated)
    grad_hidden_low = grad_hidden.astype(jnp.bfloat16)
    grad_normed, down_of_fc1, up_of_fc1 = project_back(
        normed_low, inner_hidden, grad_hidden_low, fc1_all, down_pick[:, :, 4], ff_pick[:, :, 0]
    )
    (grad_first,) = first_back(grad_normed + grad_second)
    grad_branch_low = grad_first.astype(jnp.bfloat16)
    grad_mixed, down_of_out, up_of_out = project_back(
        mixed,
        inner_branch,
        grad_branch_low,
        attn_all[:, 3, :],
        down_pick[:, :, 3],
        up_pick[:, :, 3],
    )
    grad_mixed_low = grad_mixed.astype(jnp.bfloat16)
    row_delta = jnp.einsum(
        "sqhd,sqhd->shq", split_heads(grad_mixed_low.astype(jnp.float32)), split_heads(attended)
    )
    grad_query, parts = query_side(
        query, all_keys, all_values, grad_mixed_low, logsum, row_delta, lengths
    )
    grad_keys, grad_values = (
        lax.psum_scatter(
            parts[0].astype(jnp.bfloat16), "seq", scatter_dimension=1, tiled=True
        ).astype(jnp.float32),
        lax.psum_scatter(
            parts[1].astype(jnp.bfloat16), "seq", scatter_dimension=1, tiled=True
        ).astype(jnp.float32),
    )
    grad_query_low = grad_query.astype(jnp.bfloat16) * 0.125
    grad_keys_low = grad_keys.astype(jnp.bfloat16)
    grad_values_low = grad_values.astype(jnp.bfloat16)
    grad_from_query, down_of_query, up_of_query = project_back(
        tokens, inner_query, grad_query_low, attn_all[:, 0, :], down_pick[:, :, 0], up_pick[:, :, 0]
    )
    grad_from_key, down_of_key, up_of_key = project_back(
        tokens, inner_key, grad_keys_low, attn_all[:, 1, :], down_pick[:, :, 1], up_pick[:, :, 1]
    )
    grad_from_value, down_of_value, up_of_value = project_back(
        tokens,
        inner_value,
        grad_values_low,
        attn_all[:, 2, :],
        down_pick[:, :, 2],
        up_pick[:, :, 2],
    )
    input_grad = (grad_from_query + grad_from_key + grad_from_value + grad_first).astype(
        jnp.bfloat16
    )
    down_terms = jnp.stack(
        (down_of_query, down_of_key, down_of_value, down_of_out, down_of_fc1), axis=2
    )
    up_terms = jnp.stack((up_of_query, up_of_key, up_of_value, up_of_out, up_of_fc2), axis=2)
    ff_terms = jnp.stack((up_of_fc1, down_of_fc2), axis=2)
    down_table = sum_by_adapter(onehot_full, down_terms)
    up_table = sum_by_adapter(onehot_full, up_terms)
    ff_table = sum_by_adapter(onehot_full, ff_terms)
    down_grad, up_grad, ff_grad = (
        lax.psum_scatter(down_table, ("fsdp", "seq"), scatter_dimension=0, tiled=True),
        lax.psum_scatter(up_table, ("fsdp", "seq"), scatter_dimension=0, tiled=True),
        lax.psum_scatter(ff_table, ("fsdp", "seq"), scatter_dimension=0, tiled=True),
    )
    return (layer_out, input_grad, down_grad, up_grad, ff_grad)


MESH = pl.DeviceIdType.MESH
CHUNKS = 26
DEPTH = 8
BY_BLOCK = 4
ALL2, ALL4 = pl.ds(0, 2), pl.ds(0, 4)


class Spot:
    def __init__(self):
        self.y = lax.axis_index("fsdp")
        self.s = lax.axis_index("seq")
        self.z = self.s // 4
        self.x = (self.s // 2) % 2
        self.c = self.s % 2
        self.pair_z = self.z + 1 - 2 * (self.z % 2)
        self.inner = (self.z + 1) // 2 == 1

    def at(self, dy=0, dz=0, dx=0, dc=0):
        y = (self.y + dy) % 2
        z = (self.z + dz) % 4
        x = (self.x + dx) % 2
        c = (self.c + dc) % 2
        return (y, (z * 2 + x) * 2 + c)


def enter(spot):
    barrier = pltpu.get_barrier_semaphore()
    for step in range(1, 16):
        peer = (spot.y, (spot.s + step) % 16)
        pl.semaphore_signal(barrier, inc=1, device_id=peer, device_id_type=MESH)
    pl.semaphore_signal(barrier, inc=1, device_id=spot.at(dy=1), device_id_type=MESH)
    pl.semaphore_wait(barrier, 16)


class Gather:
    def __init__(self, spot, parts, ways, others, send, recv):
        self.spot, self.parts, self.ways, self.others = spot, parts, ways, others
        self.send, self.recv = send, recv

    def block(self, k, dy=0, dz=0, dx=0, dc=0):
        p = self.spot
        places = ((p.y, dy, 2), (p.z, dz, 4), (p.x, dx, 2), (p.c, dc, 2))
        return self.parts[k].at[tuple((place + d) % n if isinstance(d, int) else d for place, d, n in places)]

    def copy(self, source, target, k, out, into, peer):
        return pltpu.make_async_remote_copy(
            src_ref=source,
            dst_ref=target,
            send_sem=self.send.at[k % DEPTH, out],
            recv_sem=self.recv.at[k % DEPTH, into],
            device_id=peer,
            device_id_type=MESH,
        )

    def push(self, ref, k, out, into, source=None, **hop):
        self.copy(ref if source is None else source, ref, k, out, into, self.spot.at(**hop)).start()

    def arrive(self, like, k, into):
        self.copy(like, like, k, 0, into, self.spot.at(dc=1)).wait_recv()

    def retire(self, k):
        if self.ways[k] == "z":
            pieces = ((1, 3, 1), (2, 3, 2), (2, 3, 2), (1, 4, 1))
        elif self.ways[k] == "h":
            pieces = ((1, 1, 1), (2, 3, 2), (2, 3, 2), (1, 4, 1))

            @pl.when(self.spot.inner)
            def _():
                for out in (4, 5):
                    like = self.pair_of(k, 0)
                    self.copy(like, like, k, out, 0, self.spot.at(dc=1)).wait_send()

        else:
            pieces = ((1, 1, 1), (2, 3, 1), (2, 4, 2), (2, 4, 1))
        for out, (ys, zs, xs) in enumerate(pieces):
            like = self.parts[k].at[pl.ds(0, ys), pl.ds(0, zs), pl.ds(0, xs), 0]
            self.copy(like, like, k, out, 0, self.spot.at(dc=1)).wait_send()

    def pair_of(self, k, far):
        p = self.spot
        return self.parts[k].at[p.y, pl.ds(((p.z // 2 + far) % 2) * 2, 2), p.x, p.c]

    def hand(self, k):
        self.arrive(self.block(k), k, 0)

        @pl.when(self.spot.inner)
        def _():
            self.push_to(self.pair_of(k, 0), k, 4, 5, 3 - self.spot.z)

    def pass_on(self, k):
        @pl.when(self.spot.inner)
        def _():
            self.arrive(self.pair_of(k, 1), k, 5)
            self.push_to(self.pair_of(k, 1), k, 5, 5, self.spot.pair_z)

    def push_to(self, ref, k, out, into, z):
        p = self.spot
        self.copy(ref, ref, k, out, into, (p.y, (z * 2 + p.x) * 2 + p.c)).start()

    def first(self, k):
        if k >= DEPTH:
            self.retire(k - DEPTH)
        if self.ways[k] == "h":
            self.push_to(self.block(k), k, 0, 0, self.spot.pair_z)
        elif self.ways[k] == "z":
            for d in range(1, 4):
                self.push(self.block(k), k, 0, 0, dz=d)
        else:
            self.push(self.block(k), k, 0, 0, self.others.get(k), **{"d" + self.ways[k]: 1})

    def second(self, k):
        if self.ways[k] in "zh":
            if self.ways[k] == "z":
                self.arrive(self.block(k, dz=pl.ds(0, 3)), k, 0)
            else:

                @pl.when(jnp.logical_not(self.spot.inner))
                def _():
                    self.arrive(self.pair_of(k, 1), k, 5)

            line = self.block(k, dz=ALL4)
            self.push(line, k, 1, 1, dx=1)
            self.push(line, k, 1, 2, dy=1)
            self.push(line, k, 1, 4, dc=1)
        else:
            self.arrive(self.block(k), k, 0)
            for d in range(1, 4):
                self.push(self.block(k, **{"d" + self.ways[k]: ALL2}), k, 1, 1, dz=d)

    def third(self, k):
        if self.ways[k] in "zh":
            cut = 3 if k in SHIFTED else 2
            self.arrive(self.block(k, dz=ALL4), k, 1)
            self.push(self.block(k, dz=pl.ds(0, cut), dx=1), k, 2, 3, dy=1)
            self.arrive(self.block(k, dz=ALL4), k, 2)
            self.push(self.block(k, dz=pl.ds(cut, 4 - cut), dy=1), k, 2, 3, dx=1)
            self.push(self.block(k, dz=ALL4, dx=1), k, 2, 4, dc=1)
            self.push(self.block(k, dz=ALL4, dy=1), k, 2, 4, dc=1)
        else:
            near, far = "d" + self.ways[k], "dy" if self.ways[k] == "x" else "dx"
            self.arrive(self.block(k, **{near: ALL2, "dz": pl.ds(0, 3)}), k, 1)
            plane = self.block(k, **{near: ALL2, "dz": ALL4})
            self.push(plane, k, 2, 2, **{far: 1})
            self.push(plane, k, 2, 4, dc=1)

    def fourth(self, k):
        if self.ways[k] in "zh":
            self.arrive(self.block(k, dz=ALL4), k, 3)
            self.push(self.block(k, dz=ALL4, dx=1, dy=1), k, 3, 4, dc=1)
        else:
            near, far = "d" + self.ways[k], "dy" if self.ways[k] == "x" else "dx"
            self.arrive(self.block(k, **{near: ALL2, "dz": ALL4}), k, 2)
            self.push(self.block(k, **{near: ALL2, "dz": ALL4, far: 1}), k, 3, 4, dc=1)

    def ready(self, k):
        self.arrive(self.block(k, dy=ALL2, dz=ALL4, dx=ALL2), k, 4)

    def step(self, t):
        moves = ((0, self.first), (1, self.second), (2, self.third), (3, self.fourth), (4, self.ready))
        hops = ((-2, self.first), (-1, self.hand), (0, self.pass_on)) + moves[1:]
        order = [(late, k, move) for k, way in enumerate(self.ways) for late, move in (hops if way == "h" else moves)]
        for late, k, move in sorted(order, key=lambda entry: (entry[0], entry[1])):
            if k + late == t:
                move(k)

    def finish(self):
        for k in range(len(self.parts) - DEPTH, len(self.parts)):
            self.retire(k)


F32, BF16 = jnp.float32, jnp.bfloat16
ORDER = (0, 1, 24, 25) + tuple(range(2, 24))
WAYS = "zzyyzz" + "h" * 20
SHIFTED = (6, 7, 8, 9, 10, 12, 13, 16)
EARLY, LATE = 80, 32
FAR_FIRST = (2, 1, 3, 0)


def dot(left, right):
    return jnp.dot(left, right, preferred_element_type=F32)


def dot_nt(left, right):
    return lax.dot_general(left, right, (((1,), (1,)), ((), ())), preferred_element_type=F32)


def dot_tn(left, right):
    return lax.dot_general(left, right, (((0,), (0,)), ((), ())), preferred_element_type=F32)


def lanes(shape):
    return lax.broadcasted_iota(jnp.int32, shape, len(shape) - 1)


def half(value, slot):
    low_half = lanes(value.shape) < HEAD
    zero = jnp.zeros_like(value)
    return jnp.where(low_half, value, zero) if slot == 0 else jnp.where(low_half, zero, value)


def pair(first, second):
    return jnp.where(lanes(first.shape) < HEAD, first, second)


def swap(value):
    return pltpu.roll(value, HEAD, 1)


def heads_to_rows(heads, rows, factor):
    for p in range(HEADS // 2):
        even = heads[2 * p].astype(F32) * factor
        odd = heads[2 * p + 1].astype(F32) * factor
        rows[0:64, p * 128 : p * 128 + 128] = pair(even, swap(odd)).astype(BF16)
        rows[64:128, p * 128 : p * 128 + 128] = pair(swap(even), odd).astype(BF16)


class Exchange:
    def __init__(self, spot, out, into, send, recv):
        self.spot, self.out, self.into, self.send, self.recv = spot, out, into, send, recv

    def arrived(self, unit, z):
        return self.recv.at[unit if unit != BY_BLOCK else 8 + z]

    def copy(self, unit, source, target, peer):
        return pltpu.make_async_remote_copy(
            src_ref=source,
            dst_ref=target,
            send_sem=self.send.at[unit],
            recv_sem=self.arrived(unit, self.spot.z),
            device_id=(self.spot.y, peer),
            device_id_type=MESH,
        )

    def start(self, unit, block):
        me = self.spot.s

        def body(i, carry):
            peer = block * 4 + i

            @pl.when(peer != me)
            def _():
                self.copy(unit, self.out.at[unit, peer], self.into.at[unit, me], peer).start()

            return carry

        lax.fori_loop(0, 4, body, 0)

    def keep(self, unit):
        self.into[unit, self.spot.s] = self.out[unit, self.spot.s]

    def wait_block(self, far):
        like = self.into.at[BY_BLOCK, pl.ds(0, 4 if far else 3)]
        pltpu.make_async_copy(like, like, self.arrived(BY_BLOCK, (self.spot.z + far) % 4)).wait()

    def wait(self, unit):
        like = self.into.at[unit, pl.ds(0, 15)]
        pltpu.make_async_copy(like, like, self.recv.at[unit]).wait()

    def finish(self, units):
        for unit in range(units):
            like = self.out.at[unit, pl.ds(0, 15)]
            pltpu.make_async_copy(like, like, self.send.at[unit]).wait()


class Scatter:
    def __init__(self, spot, wide, own, core_in, core_sum, x_in, x_sum, into, send, recv):
        self.spot, self.wide = spot, wide
        self.own, self.core_in, self.core_sum = own, core_in, core_sum
        self.x_in, self.x_sum, self.into = x_in, x_sum, into
        self.send, self.recv = send, recv

    def copy(self, source, target, route, peer):
        return pltpu.make_async_remote_copy(
            src_ref=source,
            dst_ref=target,
            send_sem=self.send.at[route],
            recv_sem=self.recv.at[route],
            device_id=peer,
            device_id_type=MESH,
        )

    def first(self):
        p = self.spot
        self.hop = self.copy(self.own.at[:, :, :, 1 - p.c], self.core_in, 0, p.at(dc=1))
        self.hop.start()

    def second(self):
        p = self.spot
        self.hop.wait()
        self.core_sum[...] = (self.own[:, :, :, p.c].astype(F32) + self.core_in[...].astype(F32)).astype(BF16)
        if not self.wide:
            self.hop = self.copy(self.core_sum.at[:, :, 1 - p.x], self.x_in, 1, p.at(dx=1))
            self.hop.start()

    def distances(self):
        every = [(dy, dz, dx) for dy in range(2) for dz in range(4) for dx in range(2 if self.wide else 1)]
        return every[1:]

    def third(self):
        p = self.spot
        if not self.wide:
            self.hop.wait()
            self.x_sum[...] = (self.core_sum[:, :, p.x].astype(F32) + self.x_in[...].astype(F32)).astype(BF16)
        for n, (dy, dz, dx) in enumerate(self.distances()):
            y, z, x = (p.y + dy) % 2, (p.z + dz) % 4, (p.x + dx) % 2
            source = self.core_sum.at[y, z, x] if self.wide else self.x_sum.at[y, z]
            self.copy(source, self.into.at[n], 2, p.at(dy=dy, dz=dz, dx=dx)).start()

    def fourth(self):
        p = self.spot
        self.copy(self.into, self.into, 2, p.at(dc=1)).wait()
        total = [self.core_sum[p.y, p.z, p.x] if self.wide else self.x_sum[p.y, p.z], None]
        total[0] = total[0].astype(F32)
        for n, (dy, _, _) in enumerate(self.distances()):
            term = self.into[n].astype(F32)
            total[dy] = term if total[dy] is None else total[dy] + term
        return total


def scatter_shapes(rows, wide):
    return [
        pltpu.VMEM((2, 4, 2, 2, rows, 128), BF16),
        pltpu.VMEM((2, 4, 2, rows, 128), BF16),
        pltpu.VMEM((2, 4, 2, rows, 128), BF16),
        pltpu.VMEM((2, 4, rows, 128), BF16),
        pltpu.VMEM((2, 4, rows, 128), BF16),
        pltpu.VMEM((15 if wide else 7, rows, 128), BF16),
        pltpu.SemaphoreType.DMA((3,)),
        pltpu.SemaphoreType.DMA((3,)),
    ]


def layer_kernel(*refs):
    it = iter(refs)

    def take(count):
        return [next(it) for _ in range(count)]

    attn, fc1, fc2, tok_far, cot_far, down_table, up_table, ff_table, vec_in, bias_in, lengths, ids = take(12)
    layer_out, input_grad, sums_out, ids_out = take(4)
    wide, tall, rank_all, ff_all = take(4)
    rank_in, rank_up, rank_x, vec, ff_low, bias = take(6)
    heads_out, heads_in = take(2)
    weights_low, weights_back = take(2)
    attended, stat, tmp, sum_one, scaled_one, normed, grad_second, grad_first = take(8)
    tok, cot, mixed, normed_low, out_low, branch_low, query_low, key_low, value_low = take(9)
    slope, act, grad_hidden, inner4 = take(4)
    id_rows, table, rank_other, ff_other = take(4)
    early_refs, up_refs, down_refs = take(8), take(8), take(8)
    own, send, recv, hsend, hrecv, id_sem = take(6)

    spot = Spot()
    here = (spot.y, spot.z, spot.x, spot.c)
    parts = [wide.at[k] for k in range(16)] + [tall.at[k] for k in range(8)] + [rank_all, ff_all]
    placed = [pltpu.make_async_copy(fc2, query_low, own.at[1])]
    for k in range(8):
        placed.append(pltpu.make_async_copy(fc1.at[:, pl.ds(k * 512, 512)], parts[8 + k].at[here], own.at[0]))
    tok_copy = pltpu.make_async_copy(tok_far, tok, own.at[2])
    cot_copy = pltpu.make_async_copy(cot_far, cot, own.at[3])
    tok_copy.start()
    for k in (0, 1):
        wide[(k,) + here] = attn[:, 0, k * 512 : k * 512 + 512]
    for copy in placed:
        copy.start()
    cot_copy.start()
    others = {2: rank_other, 3: ff_other}
    gather = Gather(spot, [parts[k] for k in ORDER], WAYS, others, send, recv)
    swaps = Exchange(spot, heads_out, heads_in, hsend, hrecv)
    early = Scatter(spot, False, *early_refs)
    late_up = Scatter(spot, True, *up_refs)
    late_down = Scatter(spot, True, *down_refs)
    first_row = lax.broadcasted_iota(jnp.int32, (8, 128), 0) == 0
    id_rows[spot.y] = jnp.where(first_row, ids[0], ids[1])
    enter(spot)
    gather.step(0)
    id_copy = pltpu.make_async_remote_copy(
        src_ref=id_rows.at[spot.y],
        dst_ref=id_rows.at[spot.y],
        send_sem=id_sem.at[0],
        recv_sem=id_sem.at[1],
        device_id=spot.at(dy=1),
        device_id_type=MESH,
    )
    id_copy.start()
    for j in range(1, 4):
        for k in range(2):
            wide[(2 * j + k,) + here] = attn[:, j, k * 512 : k * 512 + 512]

    def chosen(source, kind, y, slot):
        who = id_rows[y, slot : slot + 1, 0 : source.shape[3]]
        total = None
        for a in range(ADAPTERS):
            term = jnp.where(who == a, source[a, kind].astype(F32), 0.0)
            total = term if total is None else total + term
        return total

    def pick_all():
        table[...] = jnp.zeros_like(table)
        for g in range(2):
            y = (spot.y + g) % 2
            for slot in range(2):
                for j in range(4):
                    row = g * 384 + j * 32 + slot * 16
                    table[row : row + 16, 0:32] = chosen(down_table, j, y, slot)
                    table[row + 128 : row + 144, 0:32] = chosen(up_table, j, y, slot)
                row = g * 384 + 256 + slot * 16
                table[row : row + 16, 0:32] = chosen(down_table, 4, y, slot)
                table[row + 32 : row + 48, 0:32] = chosen(up_table, 4, y, slot)
                for kind in range(2):
                    row = 768 + g * 64 + kind * 32 + slot * 16
                    table[row : row + 16, :] = chosen(ff_table, kind, y, slot)
        for n in range(3):
            cols = slice(n * 128, n * 128 + 128)
            rank_all[here + (slice(None), cols)] = table[cols, :].T[0:32].astype(BF16)
            rank_other[:, cols] = table[384 + n * 128 : 512 + n * 128, :].T[0:32].astype(BF16)
        turned = table[768:896, :].T
        ff_all[here + (slice(0, 64),)] = pair(turned[0:64], swap(turned[64:128])).astype(BF16)
        ff_other[0:64] = pair(swap(turned[0:64]), turned[64:128]).astype(BF16)
        table[0:8, 0:32] = vec_in[...].astype(F32)
        table[0:8, 32:128] = jnp.zeros((8, 96), F32)
        columns = pltpu.roll(table[0:8, :], (spot.s % 4) * 32, 1)
        rows = jnp.concatenate([jnp.broadcast_to(bias_in[...].astype(F32), (8, 128)), columns], axis=0)
        ff_all[here + (slice(64, 80),)] = rows.astype(BF16)
        ff_other[64:80] = rows.astype(BF16)

    lane = lanes((128, 128))
    row_slot = lax.broadcasted_iota(jnp.int32, (128, 128), 0) >= 64
    slot_lane = ((lane & 16) != 0) == row_slot
    kind4 = [slot_lane & ((lane >> 5) == j) for j in range(4)]
    kind_ff = [slot_lane & ((lane >> 5) == k) for k in range(2)]

    def only(mask, value):
        return jnp.where(mask, value, jnp.zeros_like(value))

    def square(k, t):
        halves = [wide[2 * k + i, t // 2, pl.ds((t % 2) * 2, 2)].reshape(256, 512) for i in range(2)]
        return jnp.concatenate(halves, axis=1)

    def columns(k, n):
        return wide[2 * k + n // 2, :, :, :, :, :, tile(n % 2)].reshape(1024, 256)

    def tile(n, size=256):
        return pl.ds(pl.multiple_of(n * size, size), size)

    def unpack_rank():
        rank_in[...] = rank_all[:, :, :, :, :, 0:128].reshape(1024, 128)
        rank_up[...] = rank_all[:, :, :, :, :, 128:256].reshape(1024, 128)
        rank_x[...] = rank_all[:, :, :, :, :, 256:384].reshape(1024, 128)

    def ff_rows(first, count):
        return ff_low[pl.ds(first, count)].reshape(count * 128, 128)

    def unpack_ff():
        columns_of = {}
        packed = ff_all[:, :, :, :, 0:64, :].reshape(32, 64, 128)
        ff_low[:, 0] = packed
        ff_low[:, 1] = swap(packed.astype(F32).reshape(2048, 128)).astype(BF16).reshape(32, 64, 128)
        for o in range(32):
            y, z, x, c = o // 16, (o // 4) % 4, (o // 2) % 2, o % 2
            rows = ff_all[y, z, x, c, 64:80, :].astype(F32)
            bias[:, o * 128 : o * 128 + 128] = rows[0:8]
            columns_of[o // 4] = rows[8:16] if o % 4 == 0 else columns_of[o // 4] + rows[8:16]
        for n in range(8):
            vec[:, n * 128 : n * 128 + 128] = columns_of[n]

    def to_heads(unit, block, value):
        for p in range(2):
            first = value[0:64, p * 128 : p * 128 + 128]
            second = value[64:128, p * 128 : p * 128 + 128]
            heads_out[unit, block * 4 + 2 * p] = pair(first, swap(second)).astype(BF16)
            heads_out[unit, block * 4 + 2 * p + 1] = pair(swap(first), second).astype(BF16)
        swaps.start(unit, block)

    def turn(body, unrolled=False):
        def shifted(t, carry):
            body((spot.z + t) % 4)
            return carry

        if unrolled:
            for t in FAR_FIRST:
                shifted(t, 0)
        else:
            lax.fori_loop(0, 4, shifted, 0)

    def project_in(j):
        inner = only(kind4[j], inner4[...])

        def body(n):
            cols = tile(n)
            value = dot(tok[...], columns(j, n)) + dot_nt(inner, rank_up[cols, :])
            if j == 0:
                value = (value + vec[0:1, cols]) * 0.125
            if j == 2:
                value = value + vec[1:2, cols]
            to_heads(j, n, value)

        turn(body)
        swaps.keep(j)

    def attention(t):
        if t == 0:
            for j in range(3):
                swaps.wait(j)
        block = (spot.z + t) % 4
        keys = heads_in[1].reshape(1024, 128)
        values = heads_in[2].reshape(1024, 128)
        rows = tile(block)
        query = heads_in[0, pl.ds(block * 4, 4)].reshape(256, 128)
        results, stats = [], []
        for slot in range(2):
            scores = dot_nt(half(query, slot), keys)
            scores = jnp.where(lanes(scores.shape) < lengths[slot], scores, NEG_FILL)
            top = jnp.max(scores, axis=-1, keepdims=True)
            shifted = jnp.exp(scores - top)
            total = jnp.sum(shifted, axis=-1, keepdims=True)
            low = (shifted * (1.0 / total)).astype(BF16)
            weights_low[slot, rows, :] = low
            results.append(dot(low, values))
            stats.append(jnp.broadcast_to(top + jnp.log(total), (256, 128)))
        result = pair(results[0], results[1])
        attended[rows, :] = result
        heads_out[3, pl.ds(block * 4, 4)] = result.astype(BF16).reshape(4, 64, 128)
        stat[rows, :] = pair(stats[0], stats[1])
        swaps.start(3, block)
        if t == 3:
            swaps.keep(3)

    def attention_turned(first):
        logsum = stat[...].T
        queries = heads_in[0].reshape(1024, 128)
        turned = [logsum[0:1], logsum[64:65]]

        def body(t, carry):
            rows = tile(t)
            keys = heads_in[1, pl.ds(t * 4, 4)].reshape(256, 128)
            for slot in range(2):
                scores = dot_nt(half(keys, slot), queries)
                weights = jnp.exp(scores - turned[slot])
                place = lax.broadcasted_iota(jnp.int32, weights.shape, 0) + t * 256
                weights = jnp.where(place < lengths[slot], weights, 0.0)
                weights_back[slot, rows, :] = weights.astype(BF16)
            return carry

        lax.fori_loop(first, first + 2, body, 0)

    def normalize(value):
        centered = value - jnp.mean(value, axis=-1, keepdims=True)
        spread = lax.rsqrt(jnp.mean(centered * centered, axis=-1, keepdims=True) + NORM_EPS)
        return centered * spread, spread

    def normalize_back(grad, scaled, spread):
        shift = jnp.mean(grad, axis=-1, keepdims=True)
        along = jnp.mean(grad * scaled, axis=-1, keepdims=True)
        return spread * (grad - shift - scaled * along)

    saved = {}

    def branch():
        swaps.wait(3)
        heads_to_rows(heads_in.at[3], mixed, 1.0)
        saved["o"] = only(kind4[3], dot(mixed[...], rank_in[...])).astype(BF16)

        def body(n, carry):
            cols = tile(n)
            value = dot(mixed[...], columns(3, n)) + dot_nt(saved["o"], rank_up[cols, :])
            sum_one[:, cols] = tok[:, cols].astype(F32) + value + vec[2:3, cols]
            return carry

        lax.fori_loop(0, 4, body, 0)
        scaled, saved["spread_one"] = normalize(sum_one[...])
        scaled_one[...] = scaled
        value = scaled * vec[4:5] + vec[5:6]
        normed[...] = value
        normed_low[...] = value.astype(BF16)
        saved["hidden"] = only(kind_ff[0], dot(normed_low[...], rank_x[...])).astype(BF16)

    def expand(k):
        def body(i, carry):
            n = k * 2 + i
            cols = tile(n)
            value = dot(normed_low[...], wide[8 + k, :, :, :, :, :, tile(i)].reshape(1024, 256))
            value = value + dot_nt(saved["hidden"], ff_rows(n * 2, 2)) + bias[0:1, cols]
            share = 0.5 * (1.0 + lax.erf(value * math.sqrt(0.5)))
            act[:, cols] = (value * share).astype(BF16)
            bell = jnp.exp(-0.5 * value * value) * (1.0 / math.sqrt(2.0 * math.pi))
            slope[:, cols] = share + value * bell
            return carry

        lax.fori_loop(0, 2, body, 0)

    def contract(q):
        if q == 0:
            saved["out"] = only(kind_ff[1], dot(act[...], ff_rows(0, 32))).astype(BF16)
        cols = slice(q * 256, q * 256 + 256)
        halves = []
        for k in (2 * q, 2 * q + 1):
            places = [(o // 16, (o // 4) % 4, (o // 2) % 2, o % 2) for o in range(32)]
            halves.append(jnp.concatenate([tall[(k,) + place] for place in places], axis=1))
        value = dot_nt(act[...], jnp.concatenate(halves, axis=0)) + dot_nt(saved["out"], rank_x[cols, :])
        tmp[:, cols] = normed[:, cols] + value + vec[3:4, cols]

    def outer():
        rows = lax.broadcasted_iota(jnp.int32, (128, 1), 0)
        place = spot.s * 64 + (rows & 63)
        limit = jnp.where(rows < 64, lengths[0], lengths[1])
        live = (place < limit).astype(F32)
        scaled, spread = normalize(tmp[...])
        layer_out[...] = (live * (scaled * vec[6:7] + vec[7:8])).astype(BF16)
        grad = normalize_back(live * cot[...].astype(F32) * vec[6:7], scaled, spread)
        grad_second[...] = grad
        out_low[...] = grad.astype(BF16)
        saved["g_out"] = only(kind_ff[1], dot(out_low[...], rank_x[...])).astype(BF16)

    def hidden_back():
        def body(t, carry):
            rows = tile(t)
            pieces = [tall[:, t // 8, (t // 2) % 4, t % 2, c].reshape(1024, 128) for c in range(2)]
            value = dot(out_low[...], jnp.concatenate(pieces, axis=1))
            value = value + dot_nt(saved["g_out"], ff_rows(t * 2, 2))
            grad_hidden[:, rows] = (value * slope[:, rows]).astype(BF16)
            return carry

        lax.fori_loop(0, 16, body, 0, unroll=True)
        saved["g_hidden"] = only(kind_ff[0], dot(grad_hidden[...], ff_rows(0, 32))).astype(BF16)

    def normed_back():
        def body(t, carry):
            rows = tile(t)
            value = dot_nt(saved["g_hidden"], rank_x[rows, :]) + grad_second[:, rows]
            for q in range(4):
                value = value + dot_nt(grad_hidden[:, q * 1024 : q * 1024 + 1024], square(4 + q, t))
            tmp[:, rows] = value
            return carry

        lax.fori_loop(0, 4, body, 0, unroll=True)
        grad = normalize_back(tmp[...] * vec[4:5], scaled_one[...], saved["spread_one"])
        grad_first[...] = grad
        branch_low[...] = grad.astype(BF16)
        saved["g_o"] = only(kind4[3], dot(branch_low[...], rank_up[...])).astype(BF16)

    def mixed_back():
        def body(n):
            value = dot_nt(branch_low[...], square(3, n)) + dot_nt(saved["g_o"], rank_in[tile(n), :])
            to_heads(4, n, value)

        turn(body, True)
        swaps.keep(4)

    def early_grads():
        own_grads = early.own
        value = dot_tn(normed_low[...], saved["g_hidden"]) + dot_tn(out_low[...], saved["out"])
        value = value.reshape(32, 2, 16, 128)
        value = value[:, 0] + swap(value[:, 1].reshape(512, 128)).reshape(32, 16, 128)
        own_grads[:, :, :, :, 0:16, :] = value.astype(BF16).reshape(2, 4, 2, 2, 16, 128)
        for y in range(2):
            for z in range(4):
                cols = slice((y * 4 + z) * 512, (y * 4 + z) * 512 + 512)
                value = dot_tn(grad_hidden[:, cols], saved["hidden"]) + dot_tn(act[:, cols], saved["g_out"])
                value = value.reshape(4, 128, 128)
                for o in range(4):
                    packed = value[o, 0:64] + swap(value[o, 64:128])
                    own_grads[y, z, o // 2, o % 2, 16:80, :] = packed.astype(BF16)

    def query_back(t):
        block = (spot.z + 4 - t) % 4
        swaps.wait_block((4 - t) % 4)
        rows = tile(block)
        keys = heads_in[1].reshape(1024, 128)
        values = heads_in[2].reshape(1024, 128)
        grad_block = heads_in[4, pl.ds(block * 4, 4)].reshape(256, 128)
        product = grad_block.astype(F32) * attended[rows, :]
        parts_, deltas = [], []
        for slot in range(2):
            delta = jnp.sum(half(product, slot), axis=-1, keepdims=True)
            grad_probs = dot_nt(half(grad_block, slot), values)
            weights = weights_low[slot, rows, :].astype(F32)
            grad_scores = (weights * (grad_probs - delta)).astype(BF16)
            parts_.append(dot(grad_scores, keys))
            deltas.append(jnp.broadcast_to(delta, (256, 128)))
        heads_out[5, pl.ds(block * 4, 4)] = pair(*parts_).astype(BF16).reshape(4, 64, 128)
        stat[rows, :] = pair(*deltas)
        swaps.start(5, block)
        if t == FAR_FIRST[-1]:
            swaps.keep(5)

    def key_back():
        queries = heads_in[0].reshape(1024, 128)
        grads = heads_in[4].reshape(1024, 128)
        turned = stat[...].T
        turned = [turned[0:1], turned[64:65]]

        def body(block):
            rows = tile(block)
            value_block = heads_in[2, pl.ds(block * 4, 4)].reshape(256, 128)
            key_parts, value_parts = [], []
            for slot in range(2):
                weights = weights_back[slot, rows, :]
                grad_probs = dot_nt(half(value_block, slot), grads)
                grad_scores = (weights.astype(F32) * (grad_probs - turned[slot])).astype(BF16)
                key_parts.append(dot(grad_scores, queries))
                value_parts.append(dot(weights, grads))
            heads_out[6, pl.ds(block * 4, 4)] = pair(*key_parts).astype(BF16).reshape(4, 64, 128)
            heads_out[7, pl.ds(block * 4, 4)] = pair(*value_parts).astype(BF16).reshape(4, 64, 128)
            swaps.start(6, block)
            swaps.start(7, block)

        turn(body, True)
        swaps.keep(6)
        swaps.keep(7)

    def inputs_back():
        grads = (query_low, key_low, value_low)
        ups = dot_tn(branch_low[...], saved["o"])
        downs = dot_tn(mixed[...], saved["g_o"])
        for j, grad in enumerate(grads):
            swaps.wait(5 + j)
            heads_to_rows(heads_in.at[5 + j], grad, 0.125 if j == 0 else 1.0)
            ups = ups + dot_tn(grad[...], only(kind4[j], inner4[...]))
        late_up.own[...] = ups.astype(BF16).reshape(2, 4, 2, 2, 32, 128)
        late_up.first()
        inner = jnp.zeros((128, 128), F32)
        for j, grad in enumerate(grads):
            inner = jnp.where(kind4[j], dot(grad[...], rank_up[...]), inner)
        saved["g_in"] = inner.astype(BF16)
        downs = downs + dot_tn(tok[...], saved["g_in"])
        late_down.own[...] = downs.astype(BF16).reshape(2, 4, 2, 2, 32, 128)
        late_down.first()
        late_up.second()
        late_up.third()
        late_down.second()
        late_down.third()

    def tokens_back(t):
        rows = pl.ds(t * 256, 256)
        value = dot_nt(saved["g_in"], rank_in[rows, :]) + grad_first[:, rows]
        for j, grad in enumerate((query_low, key_low, value_low)):
            value = value + dot_nt(grad[...], square(j, t))
        input_grad[:, rows] = value.astype(BF16)

    for t in range(1, CHUNKS + 4):
        if t == 2:
            id_copy.wait_recv()
            pick_all()
        if t == 4:
            like = wide.at[(pl.ds(8, 8),) + here]
            pltpu.make_async_copy(like, like, own.at[0]).wait()
            placed[0].wait()
            for k in range(8):
                turned = query_low[:, k * 128 : k * 128 + 128].astype(F32).T
                tall[(k,) + here] = turned.astype(BF16)
        gather.step(t)
        if t == 7:
            tok_copy.wait()
            unpack_rank()
            unpack_ff()
            inner4[...] = dot(tok[...], rank_in[...]).astype(BF16)
        if t in (7, 9, 11):
            project_in((t - 7) // 2)
        if 14 <= t <= 17:
            attention(t - 14)
        if 18 <= t <= 19:
            attention_turned((t - 18) * 2)
        if t == 20:
            branch()
        if 21 <= t <= 24:
            expand(2 * t - 42)
            expand(2 * t - 41)
        if t == 27:
            contract(0)
        if t >= 27:
            contract(t - 26)
    cot_copy.wait()
    outer()
    hidden_back()
    normed_back()
    mixed_back()
    early_grads()
    early.first()
    for t in FAR_FIRST:
        query_back(t)
    early.second()
    key_back()
    early.third()
    inputs_back()
    for t in range(4):
        tokens_back(t)
    for first, scatter in ((0, early), (EARLY, late_down), (EARLY + LATE, late_up)):
        for dy, total in enumerate(scatter.fourth()):
            sums_out[dy, first : first + total.shape[0], :] = total
    for dy in range(2):
        ids_out[dy] = id_rows[(spot.y + dy) % 2]
    id_copy.wait_send()
    gather.finish()
    swaps.finish(8)


def hand_on_kernel(layer_in, grad_in, sums, ids, layer_out, grad_out, down_out, up_out, ff_out):
    layer_out[...] = layer_in[...]
    grad_out[...] = grad_in[...]
    turned, ff_turned = [], []
    for dy in range(2):
        packed = sums[dy, 16:80, :]
        ff_turned.append(jnp.concatenate([packed, swap(packed)], axis=0).T)
        cross = sums[dy, 0:16, :]
        rows = [sums[dy, EARLY : EARLY + 2 * LATE, :], cross, swap(cross), jnp.zeros((32, 128), F32)]
        turned.append(jnp.concatenate(rows, axis=0).T)
    for a in range(ADAPTERS):
        share = [(ids[dy, 0:2, :] == a).astype(F32) for dy in range(2)]

        def spread(source, first):
            total = None
            for dy in range(2):
                for slot in range(2):
                    row = first + slot * 16
                    term = share[dy][slot : slot + 1] * source[dy][row : row + 16, :]
                    total = term if total is None else total + term
            return total

        for j in range(4):
            value = spread(turned, j * 32)
            down_out[a, j] = value[:, 0:32]
            up_out[a, j] = value[:, 32:64]
        down_out[a, 4] = spread(turned, 0)[:, 64:96]
        up_out[a, 4] = spread(turned, 32)[:, 64:96]
        for kind in range(2):
            ff_out[a, kind] = spread(ff_turned, kind * 32)


def hand_on(arrays, shapes):
    near = pl.BlockSpec(memory_space=pltpu.VMEM)
    return pl.pallas_call(
        hand_on_kernel,
        out_shape=[jax.ShapeDtypeStruct(array.shape, array.dtype) for array in arrays[:2]]
        + [jax.ShapeDtypeStruct(shape, F32) for shape in shapes],
        in_specs=[near] * 4,
        out_specs=[near] * 5,
        name="hand_on",
    )(*arrays)


def layer(attn, fc1, fc2, tok, cot, down, up, ff, vec, bias, lengths, ids):
    lead = (2, 4, 2, 2)
    anywhere = pl.BlockSpec(memory_space=pl.ANY)
    near = pl.BlockSpec(memory_space=pltpu.VMEM)
    scalar = pl.BlockSpec(memory_space=pltpu.SMEM)

    def buffer(*shape, dtype=BF16):
        return pltpu.VMEM(shape, dtype)

    scratch = [
        buffer(16, *lead, 32, 512),
        buffer(8, *lead, 128, 128),
        buffer(*lead, 32, 384),
        buffer(*lead, 80, 128),
    ]
    scratch += [buffer(1024, 128)] * 3 + [buffer(8, 1024, dtype=F32), buffer(32, 2, 64, 128)]
    scratch += [buffer(8, 4096, dtype=F32)]
    scratch += [buffer(8, 16, 64, 128)] * 2
    scratch += [buffer(2, 1024, 1024)] * 2
    scratch += [buffer(1024, 128, dtype=F32)] * 2
    scratch += [buffer(128, 1024, dtype=F32)] * 6
    scratch += [buffer(128, 1024)] * 9
    scratch += [buffer(128, 4096, dtype=F32), buffer(128, 4096), buffer(128, 4096), buffer(128, 128)]
    scratch += [buffer(2, 8, 128, dtype=jnp.int32), buffer(896, 128, dtype=F32)]
    scratch += [buffer(32, 384), buffer(80, 128)]
    scratch += scatter_shapes(EARLY, False) + scatter_shapes(LATE, True) * 2
    scratch += [pltpu.SemaphoreType.DMA((4,))]
    scratch += [pltpu.SemaphoreType.DMA((DEPTH, 6))] * 2
    scratch += [pltpu.SemaphoreType.DMA((8,)), pltpu.SemaphoreType.DMA((12,))]
    scratch += [pltpu.SemaphoreType.DMA((2,))]
    return pl.pallas_call(
        layer_kernel,
        out_shape=[
            jax.ShapeDtypeStruct(tok.shape, BF16),
            jax.ShapeDtypeStruct(tok.shape, BF16),
            jax.ShapeDtypeStruct((2, EARLY + 2 * LATE, 128), F32),
            jax.ShapeDtypeStruct((2, 8, 128), jnp.int32),
        ],
        in_specs=[near] + [anywhere] * 4 + [near] * 5 + [scalar] * 2,
        out_specs=[near] * 4,
        scratch_shapes=scratch,
        compiler_params=pltpu.CompilerParams(
            collective_id=0, has_side_effects=True, vmem_limit_bytes=63 * 2**20
        ),
        name="layer",
    )(attn, fc1, fc2, tok, cot, down, up, ff, vec, bias, lengths, ids)


def fast_device(
    tokens,
    cotangent,
    lengths,
    adapter_ids,
    attn_weight,
    fc1_weight,
    fc2_weight,
    vectors,
    fc1_bias,
    adapter_down,
    adapter_up,
    ff_adapters,
):
    width = tokens.shape[2]
    tables = [table.transpose(1, 2, 3, 0) for table in (adapter_down, adapter_up, ff_adapters)]
    outs = layer(
        attn_weight,
        fc1_weight,
        fc2_weight,
        tokens.reshape(-1, width),
        cotangent.reshape(-1, width),
        *tables,
        vectors.T,
        fc1_bias[None],
        lengths,
        adapter_ids,
    )
    outs = hand_on(outs, [table.shape for table in tables])
    grads = [grad.transpose(3, 0, 1, 2) for grad in outs[2:]]
    return (outs[0].reshape(tokens.shape), outs[1].reshape(tokens.shape), *grads)


def solution(mesh):
    in_specs = (
        P("fsdp", "seq", None),
        P("fsdp", "seq", None),
        P("fsdp"),
        P("fsdp"),
        P(("fsdp", "seq"), None, None),
        P(("fsdp", "seq"), None),
        P(("fsdp", "seq"), None),
        P(("fsdp", "seq"), None),
        P(("fsdp", "seq")),
        P(("fsdp", "seq"), None, None, None),
        P(("fsdp", "seq"), None, None, None),
        P(("fsdp", "seq"), None, None, None),
    )
    out_specs = (
        P("fsdp", "seq", None),
        P("fsdp", "seq", None),
        P(("fsdp", "seq"), None, None, None),
        P(("fsdp", "seq"), None, None, None),
        P(("fsdp", "seq"), None, None, None),
    )
    fast = mesh.shape["fsdp"] == 2 and mesh.shape["seq"] == HEADS
    return jax.shard_map(
        fast_device if fast else on_device, mesh=mesh, in_specs=in_specs, out_specs=out_specs, check_vma=False
    )
```
